32 devices in a mesh: groups: 2 (over x), rows: 16 (over z, y, core).
Axes of the slice: x: 2, y: 2, z: 4, core: 2. Of those that a mesh axis runs over, the one named last changes fastest.
Arguments:
- queries: bfloat16 [64, 4096], P(('groups', 'rows')), parts along dimension 0, may hold values from -128 to 128
- new_keys: bfloat16 [64, 4096], P(('groups', 'rows')), parts along dimension 0, may hold values from -4 to 4
- new_values: bfloat16 [64, 4096], P(('groups', 'rows')), parts along dimension 0, may hold values from -5 to 5
- cache_keys: bfloat16 [64, 64, 4096], P(('groups', 'rows')), parts along dimension 0, may hold values from -4 to 4
- cache_values: bfloat16 [64, 64, 4096], P(('groups', 'rows')), parts along dimension 0, may hold values from -5 to 5
- cache_lengths: int32 [64], P(('groups', 'rows')), parts along dimension 0, may hold values from 1 to 64, as said below
- out_weight: bfloat16 [4096, 4096], P('rows'), may hold values from -0.09375 to 0.09375
- codes: int32 [64, 768], P(('groups', 'rows')), parts along dimension 0, may hold values from 0 to 1073741823
- tile_slot: int32 [64], P(('groups', 'rows')), parts along dimension 0, may hold values from -1 to 3, as said below
- code_weight: float32 [5, 512], replicated, may hold values from -2.5 to 2.5
- conv_one: bfloat16 [3, 3, 512, 512], replicated, may hold values from -0.09375 to 0.09375
- conv_two: bfloat16 [3, 3, 512, 512], replicated, may hold values from -0.09375 to 0.09375
Outputs:
- mixed: bfloat16 [64, 4096], P(('groups', 'rows')), parts along dimension 0
- decoded: bfloat16 [256, 48, 512], P(('groups', 'rows')), parts along dimension 0
The draws below stay inside these ranges and needn't reach their ends.
There are 2 independent parts, one for each index of `groups`. The reference program is written for one: setup_inputs(seed, part) draws one part's arguments, and reference() takes and returns one part's arrays. A program takes and returns all parts, laid end to end along the dimension named above; an argument that names none is the same for every part. Nothing has to cross between parts.
Inputs may be any that keep to these rules, and one draw needn't show every extreme that they name: `cache_lengths`: some row's length is exactly 64. `tile_slot`: each slot 0 to 3 belongs to exactly one row; all other rows hold -1.
All inputs are finite; a program needn't handle non-finite values.
Results may differ from the reference program's by a relative error of at most 0.0075.
Values may be sent and summed in bfloat16 or wider, within the bound.
No kernel may reach another device: no remote copies, remote signals or barrier semaphores. Data moves between devices by JAX's collectives and lax.ppermute only.
A program may use at most 64 MiB of HBM per device.

```python
import math
import jax
import jax.numpy as jnp
from jax import lax

HEADS = 32
HEAD_DIM = 128
D = 4096
CACHE = 64
NROWS = 32
CHAN = 512
FSQ_DIMS = 5
IMG_W = 48
IMG_H = 32
WORDS = 768
SLOTS = 4


def attention_fields(key):
    base = jax.random.fold_in(key, 11)
    first_key, second_key, third_key = jax.random.split(base, 3)
    stored = jnp.clip(jax.random.normal(first_key, (NROWS, CACHE, D), jnp.float32), -4.0, 4.0)
    asking = jnp.clip(jax.random.normal(second_key, (NROWS, D), jnp.float32), -4.0, 4.0)
    fresh = jnp.clip(jax.random.normal(third_key, (NROWS, D), jnp.float32), -4.0, 4.0)
    return (stored, asking, fresh)


def draw_queries(key, part):
    return attention_fields(key)[1].astype(jnp.bfloat16)


def draw_new_keys(key, part):
    return attention_fields(key)[2].astype(jnp.bfloat16)


def draw_cache_keys(key, part):
    return attention_fields(key)[0].astype(jnp.bfloat16)


def draw_cache_lengths(key, part):
    first_key, second_key = jax.random.split(jax.random.fold_in(key, 23))
    lengths = jax.random.randint(first_key, (NROWS,), 1, CACHE + 1, jnp.int32)
    longest = jax.random.randint(second_key, (), 0, NROWS, jnp.int32)
    return lengths.at[longest].set(CACHE)


def draw_tile_slot(key, part):
    order = jax.random.permutation(jax.random.fold_in(key, 37), NROWS)
    chosen = order[:SLOTS]
    empty = jnp.full((NROWS,), -1, jnp.int32)
    return empty.at[chosen].set(jnp.arange(SLOTS, dtype=jnp.int32))


def set_ends(drawn, key, least, largest):
    dims = drawn.shape
    index_at = [jax.random.randint(jax.random.fold_in(key, axis), (), 0, dims[axis]) for axis in range(len(dims))]
    drawn = drawn.at[tuple(index_at)].set(least)
    longest = dims.index(max(dims))
    index_at[longest] = (index_at[longest] + 1) % dims[longest]
    return drawn.at[tuple(index_at)].set(largest)


def block_scale(stream_key, dims, cuts, low, top_value):
    gain, own = 1.0, jax.random.fold_in(stream_key, 6)
    for dim, parts in cuts:
        steps = jnp.exp(jax.random.uniform(jax.random.fold_in(own, dim), (parts,), jnp.float32, low / len(cuts), top_value / len(cuts)))
        gain = gain * jnp.repeat(steps, dims[dim] // parts).reshape([-1 if axis == dim else 1 for axis in range(len(dims))])
    return gain


def gaussian(stream_key, dims, deviation, limit, pieces=(), kind=jnp.bfloat16):
    values = jax.random.normal(stream_key, dims, jnp.float32) * deviation
    if len(pieces) > 0:
        values = block_scale(stream_key, dims, pieces, -0.22, 0.18) * values
    return jnp.clip(values, min=-limit, max=limit).astype(kind)


def setup_inputs(seed: int = 0, part: int = 0) -> dict:
    splits = jax.random.split(jax.random.key(seed), 13)
    own_keys = jax.random.split(jax.random.fold_in(splits[12], part), 13)
    return {
        "queries": draw_queries(jax.random.fold_in(jax.random.fold_in(splits[12], part), 71), part),
        "new_keys": draw_new_keys(jax.random.fold_in(jax.random.fold_in(splits[12], part), 71), part),
        "new_values": gaussian(own_keys[2], (NROWS, D), 1.0, 5.0, ((0, 16),)),
        "cache_keys": draw_cache_keys(jax.random.fold_in(jax.random.fold_in(splits[12], part), 71), part),
        "cache_values": gaussian(own_keys[4], (NROWS, CACHE, D), 1.0, 5.0, ((0, 16),)),
        "cache_lengths": draw_cache_lengths(jax.random.fold_in(jax.random.fold_in(splits[12], part), 71), part),
        "out_weight": gaussian(splits[6], (D, D), D ** -0.5, 0.09375, ((0, 16),)),
        "codes": set_ends(jax.random.randint(own_keys[7], (NROWS, WORDS), 0, 1073741824), jax.random.fold_in(own_keys[7], 1), 0, 1073741823).astype(jnp.int32),
        "tile_slot": draw_tile_slot(jax.random.fold_in(jax.random.fold_in(splits[12], part), 71), part),
        "code_weight": gaussian(splits[9], (FSQ_DIMS, CHAN), FSQ_DIMS ** -0.5, 2.5, (), jnp.float32),
        "conv_one": gaussian(splits[10], (3, 3, CHAN, CHAN), (9 * CHAN) ** -0.5, 0.09375),
        "conv_two": gaussian(splits[11], (3, 3, CHAN, CHAN), (9 * CHAN) ** -0.5, 0.09375),
    }


def convolve(padded, weights):
    out_h = padded.shape[0] - 2
    out_w = padded.shape[1] - 2
    channels = padded.shape[2]
    summed = jnp.zeros((out_h * out_w, weights.shape[3]), jnp.float32)
    for row_step in range(3):
        for col_step in range(3):
            window = padded[row_step:row_step + out_h, col_step:col_step + out_w].reshape(out_h * out_w, channels)
            summed = summed + jnp.dot(window, weights[row_step, col_step], preferred_element_type=jnp.float32)
    return summed.reshape(out_h, out_w, weights.shape[3])

def unpack(words, code_weight):
    lower = words % 32768
    upper = words // 32768
    position_codes = jnp.stack([lower, upper], 1).reshape(-1)
    levels = jnp.stack([position_codes // 8 ** level % 8 for level in range(FSQ_DIMS)], 1)
    values = (2 * levels - 7).astype(jnp.float32) * 0.125
    return jnp.dot(values, code_weight, precision=lax.Precision.HIGHEST, preferred_element_type=jnp.float32)

def attend(queries, new_keys, new_values, cache_keys, cache_values, cache_lengths):
    count = queries.shape[0]
    factor = 1.0 / math.sqrt(HEAD_DIM)
    query_heads = queries.astype(jnp.float32).reshape(count, HEADS, HEAD_DIM)
    key_heads = cache_keys.astype(jnp.float32).reshape(count, -1, HEADS, HEAD_DIM)
    value_heads = cache_values.astype(jnp.float32).reshape(count, -1, HEADS, HEAD_DIM)
    scores = jnp.einsum('rhd,rlhd->rhl', query_heads, key_heads) * factor
    own_score = lax.optimization_barrier(jnp.sum(query_heads * new_keys.astype(jnp.float32).reshape(count, HEADS, HEAD_DIM), -1)) * factor
    live = jnp.arange(key_heads.shape[1], dtype=jnp.int32)[None, None, :] < cache_lengths[:, None, None]
    scores = jnp.where(live, scores, jnp.float32(-1e+30))
    highest = jnp.maximum(lax.optimization_barrier(jnp.max(scores, -1)), own_score)
    cache_exp = jnp.where(live, jnp.exp(scores - highest[..., None]), jnp.float32(0.0))
    own_exp = jnp.exp(own_score - highest)
    denom = lax.optimization_barrier(jnp.sum(cache_exp, -1)) + own_exp
    cache_weight = (cache_exp / denom[..., None]).astype(jnp.bfloat16)
    own_weight = (own_exp / denom).astype(jnp.bfloat16)
    attended = jnp.einsum('rhl,rlhd->rhd', cache_weight.astype(jnp.float32), value_heads)
    attended = attended + own_weight.astype(jnp.float32)[..., None] * new_values.astype(jnp.float32).reshape(count, HEADS, HEAD_DIM)
    return attended.reshape(count, HEADS * HEAD_DIM).astype(jnp.bfloat16)

def reference(queries, new_keys, new_values, cache_keys, cache_values, cache_lengths, out_weight, codes, tile_slot, code_weight, conv_one, conv_two):
    attended = attend(queries, new_keys, new_values, cache_keys, cache_values, cache_lengths)
    mixed = jnp.dot(attended, out_weight, preferred_element_type=jnp.float32).astype(jnp.bfloat16)

    def decode_one(slot):
        chosen = lax.optimization_barrier(jnp.sum(jnp.where((tile_slot == slot)[:, None], codes, 0), 0)).astype(jnp.int32)
        latent = unpack(chosen, code_weight).reshape(IMG_H, IMG_W, -1).astype(jnp.bfloat16)
        padded = jnp.pad(latent, ((1, 1), (1, 1), (0, 0)))
        hidden = convolve(padded, conv_one)
        activated = jax.nn.silu(hidden).astype(jnp.bfloat16)
        padded_two = jnp.pad(activated, ((1, 1), (1, 1), (0, 0)))
        return convolve(padded_two, conv_two).astype(jnp.bfloat16)
    images = lax.map(decode_one, jnp.arange(SLOTS, dtype=jnp.int32))
    stacked = images.reshape(SLOTS * IMG_H, IMG_W, images.shape[3])
    decoded = jnp.roll(stacked, -(IMG_H // 2), axis=0)
    return (mixed, decoded)
```

```python
import math

import jax
import jax.numpy as jnp
from jax import lax
from jax.sharding import PartitionSpec as P

HEADS = 32
HEAD_DIM = 128
FSQ_DIMS = 5
IMG_SPLIT = 4
TILE_H = 8
IMG_W = 48


def convolve(padded, weights):
    out_h = padded.shape[0] - 2
    out_w = padded.shape[1] - 2
    channels = padded.shape[2]
    summed = jnp.zeros((out_h * out_w, weights.shape[3]), jnp.float32)
    for row_step in range(3):
        for col_step in range(3):
            window = padded[row_step : row_step + out_h, col_step : col_step + out_w].reshape(
                out_h * out_w, channels
            )
            summed = summed + jnp.dot(
                window, weights[row_step, col_step], preferred_element_type=jnp.float32
            )
    return summed.reshape(out_h, out_w, weights.shape[3])


def unpack(words, code_weight):
    lower = words % 32768
    upper = words // 32768
    position_codes = jnp.stack([lower, upper], 1).reshape(-1)
    levels = jnp.stack([position_codes // 8**level % 8 for level in range(FSQ_DIMS)], 1)
    values = (2 * levels - 7).astype(jnp.float32) * 0.125
    return jnp.dot(
        values, code_weight, precision=lax.Precision.HIGHEST, preferred_element_type=jnp.float32
    )


def attend(queries, new_keys, new_values, cache_keys, cache_values, cache_lengths):
    count = queries.shape[0]
    factor = 1.0 / math.sqrt(HEAD_DIM)
    query_heads = queries.reshape(count, HEADS, HEAD_DIM)
    key_heads = cache_keys.reshape(count, -1, HEADS, HEAD_DIM)
    value_heads = cache_values.reshape(count, -1, HEADS, HEAD_DIM)
    scores = (
        jnp.einsum("rhd,rlhd->rhl", query_heads, key_heads, preferred_element_type=jnp.float32)
        * factor
    )
    own_score = (
        jnp.sum(
            query_heads.astype(jnp.float32)
            * new_keys.astype(jnp.float32).reshape(count, HEADS, HEAD_DIM),
            -1,
        )
        * factor
    )
    live = (
        jnp.arange(key_heads.shape[1], dtype=jnp.int32)[None, None, :]
        < cache_lengths[:, None, None]
    )
    scores = jnp.where(live, scores, jnp.float32(-1e30))
    highest = jnp.maximum(jnp.max(scores, -1), own_score)
    cache_exp = jnp.where(live, jnp.exp(scores - highest[..., None]), jnp.float32(0.0))
    own_exp = jnp.exp(own_score - highest)
    denom = jnp.sum(cache_exp, -1) + own_exp
    cache_weight = (cache_exp / denom[..., None]).astype(jnp.bfloat16)
    own_weight = (own_exp / denom).astype(jnp.bfloat16)
    attended = jnp.einsum(
        "rhl,rlhd->rhd", cache_weight, value_heads, preferred_element_type=jnp.float32
    )
    attended = attended + own_weight.astype(jnp.float32)[..., None] * new_values.astype(
        jnp.float32
    ).reshape(count, HEADS, HEAD_DIM)
    return attended.reshape(count, HEADS * HEAD_DIM).astype(jnp.bfloat16)


def clear_edges(field, depth, section):
    height = field.shape[0]
    line = jnp.arange(height, dtype=jnp.int32)[:, None, None]
    cleared = (line < depth) & (section == 0) | (line >= height - depth) & (
        section == IMG_SPLIT - 1
    )
    return jnp.where(cleared, jnp.zeros((), field.dtype), field)


def widen_columns(field):
    return jnp.pad(field, ((0, 0), (1, 1), (0, 0)))


def on_device(
    queries,
    new_keys,
    new_values,
    cache_keys,
    cache_values,
    cache_lengths,
    out_weight,
    codes,
    tile_slot,
    code_weight,
    conv_one,
    conv_two,
):
    attended = attend(queries, new_keys, new_values, cache_keys, cache_values, cache_lengths)
    feature_rows = lax.all_to_all(attended, "rows", split_axis=1, concat_axis=0, tiled=True)
    own_count = attended.shape[0]
    partial_value = jnp.dot(feature_rows, out_weight, preferred_element_type=jnp.float32)
    tiles = lax.axis_size("rows")
    place = lax.axis_index("rows")
    shares = partial_value.astype(jnp.bfloat16).reshape(tiles, own_count, -1)
    tile_number = (place + IMG_SPLIT // 2) % tiles
    section = tile_number % IMG_SPLIT
    row_words = IMG_W // 2
    images = codes.reshape(own_count, IMG_SPLIT * TILE_H, row_words)
    images = jnp.pad(images, ((0, 0), (2, 2), (0, 0)))
    sections = jnp.stack(
        [images[:, TILE_H * s : TILE_H * s + TILE_H + 4] for s in range(IMG_SPLIT)], 1
    ).reshape(own_count, IMG_SPLIT, -1)
    slots = jnp.arange(tiles // IMG_SPLIT, dtype=jnp.int32)
    matches = tile_slot[:, None] == slots[None, :]
    outgoing = jnp.sum(
        jnp.where(matches[:, :, None, None], sections[:, None], 0), 0
    ).reshape(tiles, -1)
    outgoing = jnp.roll(outgoing, -(IMG_SPLIT // 2), 0)
    incoming = lax.all_to_all(outgoing, "rows", split_axis=0, concat_axis=0, tiled=True)
    gathered = lax.all_to_all(shares, "rows", split_axis=0, concat_axis=0, tiled=True)
    mixed = jnp.sum(gathered.astype(jnp.float32), 0).astype(jnp.bfloat16)
    chosen = jnp.sum(incoming, 0)
    latent = unpack(chosen, code_weight).reshape(TILE_H + 4, IMG_W, -1).astype(jnp.bfloat16)
    hidden = convolve(widen_columns(clear_edges(latent, 2, section)), conv_one)
    activated = jax.nn.silu(hidden).astype(jnp.bfloat16)
    decoded = convolve(widen_columns(clear_edges(activated, 1, section)), conv_two).astype(jnp.bfloat16)
    return (mixed, decoded)


def solution(mesh):
    in_specs = (
        P(("groups", "rows"), None),
        P(("groups", "rows"), None),
        P(("groups", "rows"), None),
        P(("groups", "rows"), None, None),
        P(("groups", "rows"), None, None),
        P(("groups", "rows")),
        P("rows", None),
        P(("groups", "rows"), None),
        P(("groups", "rows")),
        P(),
        P(),
        P(),
    )
    out_specs = (P(("groups", "rows"), None), P(("groups", "rows"), None, None))
    return jax.shard_map(
        on_device, mesh=mesh, in_specs=in_specs, out_specs=out_specs, check_vma=False
    )
```

```python
import functools
import math

import jax
import jax.numpy as jnp
from jax import lax
from jax.experimental import pallas as pl
from jax.experimental.pallas import tpu as pltpu
from jax.sharding import PartitionSpec as P

HEAD_DIM = 128
FSQ_DIMS = 5
IMG_SPLIT = 4
TILE_H = 8
IMG_W = 48
LANES = 128
HALO = 2
ROW_WORDS = IMG_W // 2
TILE_ROWS = TILE_H + 2 * HALO
WINDOW = 3
PIECES = 4
CODE_ROWS = WINDOW * PIECES
VMEM_LIMIT = 56 * 1024 * 1024


def window_start(section):
    return (TILE_H * ROW_WORDS * section - HALO * ROW_WORDS) // LANES


def message_rows(features):
    return -(-(features + CODE_ROWS) // 16) * 16


def attend_kernel(
    lengths,
    slots,
    q_ref,
    nk_ref,
    nv_ref,
    k_ref,
    v_ref,
    codes_ref,
    out_ref,
    att_ref,
    msg,
    *,
    tiles,
    per,
    feature_rows,
):
    row = pl.program_id(0)
    rows, width = q_ref.shape
    heads = width // HEAD_DIM
    factor = 1.0 / math.sqrt(HEAD_DIM)

    def own_row(ref):
        whole = ref[...].astype(jnp.float32)
        at = lax.broadcasted_iota(jnp.int32, whole.shape, 0)
        return jnp.sum(jnp.where(at == row, whole, 0.0), 0, keepdims=True)

    query, new_key, new_value = own_row(q_ref), own_row(nk_ref), own_row(nv_ref)
    same = (
        lax.broadcasted_iota(jnp.int32, (heads, width), 1) // HEAD_DIM
        == lax.broadcasted_iota(jnp.int32, (heads, width), 0)
    )
    spread = jnp.where(same, query, 0.0).astype(jnp.bfloat16)
    scores = (
        lax.dot_general(
            spread, k_ref[0], (((1,), (1,)), ((), ())), preferred_element_type=jnp.float32
        )
        * factor
    )
    own_score = jnp.sum(jnp.where(same, query * new_key, 0.0), 1, keepdims=True) * factor
    live = lax.broadcasted_iota(jnp.int32, scores.shape, 1) < lengths[row]
    scores = jnp.where(live, scores, jnp.float32(-1e30))
    highest = jnp.maximum(jnp.max(scores, 1, keepdims=True), own_score)
    cache_exp = jnp.where(live, jnp.exp(scores - highest), 0.0)
    own_exp = jnp.exp(own_score - highest)
    denom = jnp.sum(cache_exp, 1, keepdims=True) + own_exp
    cache_weight = (cache_exp / denom).astype(jnp.bfloat16)
    own_weight = (own_exp / denom).astype(jnp.bfloat16).astype(jnp.float32)
    mixed_in = jnp.dot(cache_weight, v_ref[0], preferred_element_type=jnp.float32)
    attended = jnp.sum(
        jnp.where(same, mixed_in + own_weight * new_value, 0.0), 0, keepdims=True
    )

    @pl.when(row == 0)
    def _():
        msg[...] = jnp.zeros_like(msg)
        pieces = []
        words = codes_ref[...]
        for shift, mask in ((0, 255), (8, 127), (15, 255), (23, 127)):
            pieces.append(((words >> shift) & mask).astype(jnp.float32))
        blocks = words.shape[1] // LANES
        for tile in range(tiles):
            number = (tile + IMG_SPLIT // 2) % tiles
            start = window_start(number % IMG_SPLIT)
            gains = [
                jnp.where(slots[r] == number // IMG_SPLIT, 1.0, 0.0).astype(jnp.float32)
                for r in range(rows)
            ]
            for at, piece in enumerate(pieces):
                for step in range(WINDOW):
                    block = start + step
                    if block < 0 or block >= blocks:
                        continue
                    part = piece[:, block * LANES : (block + 1) * LANES]
                    total = part[0:1] * gains[0]
                    for r in range(1, rows):
                        total = total + part[r : r + 1] * gains[r]
                    place = feature_rows + at * WINDOW + step
                    msg[tile, place : place + 1, :] = total

    if per:
        for tile in range(tiles):
            for step in range(per):
                begin = (tile * per + step) * LANES
                msg[tile, pl.ds(row * per + step, 1), :] = attended[:, begin : begin + LANES]
    at = lax.broadcasted_iota(jnp.int32, att_ref.shape, 0)
    att_ref[...] = jnp.where(at == row, attended, att_ref[...])

    @pl.when(row == rows - 1)
    def _():
        out_ref[...] = msg[...].astype(jnp.bfloat16)


def project_kernel(in_ref, w_ref, out_ref, held, total, *, rows, per):
    tiles, depth = in_ref.shape[:2]
    held[...] = in_ref[...].astype(jnp.float32).reshape(held.shape)
    groups, _, _ = total.shape
    lines = out_ref.shape[2] // rows
    lhs = []
    for row in range(rows):
        parts = [held[pl.ds(row * per + j, tiles, stride=depth), :] for j in range(per)]
        lhs.append(jnp.concatenate(parts, 1))
    product = jnp.dot(
        jnp.concatenate(lhs, 0).astype(jnp.bfloat16), w_ref[...], preferred_element_type=jnp.float32
    )
    for row in range(rows):
        for group in range(groups):
            for line in range(lines):
                begin = (group * lines + line) * LANES
                total[group, pl.ds(row * lines + line, tiles, stride=rows * lines), :] = product[
                    row * tiles : (row + 1) * tiles, begin : begin + LANES
                ]
    for group in range(groups):
        out_ref[:, group] = (
            total[group].astype(jnp.bfloat16).reshape(tiles, rows * lines, LANES)
        )


def total_kernel(in_ref, out_ref, held, *, rows):
    tiles, groups, depth, _ = in_ref.shape
    lines = depth // rows
    held[...] = jnp.sum(in_ref[...].astype(jnp.float32), 0)
    for group in range(groups):
        for line in range(lines):
            begin = (group * lines + line) * LANES
            out_ref[:, begin : begin + LANES] = held[
                group, pl.ds(line, rows, stride=lines), :
            ].astype(jnp.bfloat16)


def convolve(field, w_ref, sems, copies):
    count = field.shape[0] - 2 * IMG_W
    stacked = jnp.concatenate(
        [field[step * IMG_W : step * IMG_W + count] for step in range(3)], 1
    )
    column = lax.broadcasted_iota(jnp.int32, (count, 1), 0) % IMG_W
    summed = None
    for step in (1, 0, 2):
        for copy in copies[step]:
            copy.wait()
        part = jnp.dot(stacked, w_ref[step], preferred_element_type=jnp.float32)
        if step == 0:
            part = jnp.where(column == 0, 0.0, pltpu.roll(part, 1, 0))
        if step == 2:
            part = jnp.where(column == IMG_W - 1, 0.0, pltpu.roll(part, count - 1, 0))
        summed = part if summed is None else summed + part
    return summed


def decode_kernel(
    section_ref, in_ref, cw_ref, one_ref, two_ref, out_ref, w_one, w_two, levels_w, sems, *, feature_rows
):
    channels = cw_ref.shape[1]
    copies = []
    for which, (source, target) in enumerate(((one_ref, w_one), (two_ref, w_two))):
        mine = {}
        for dc in (1, 0, 2):
            mine[dc] = [
                pltpu.make_async_copy(
                    source.at[dr, dc],
                    target.at[dc, pl.ds(dr * channels, channels)],
                    sems.at[which, dc, dr],
                )
                for dr in range(3)
            ]
            for copy in mine[dc]:
                copy.start()
        copies.append(mine)

    section = section_ref[0]
    levels_w[...] = jnp.zeros_like(levels_w)
    levels_w[0:FSQ_DIMS, :] = cw_ref[...]
    whole = levels_w[...]
    high = whole.astype(jnp.bfloat16).astype(jnp.float32)
    middle = (whole - high).astype(jnp.bfloat16).astype(jnp.float32)
    low = whole - high - middle
    weights = jnp.concatenate(
        [high, middle, low, jnp.zeros((LANES - 24, channels), jnp.float32)], 0
    ).astype(jnp.bfloat16)

    got = jnp.sum(in_ref[...].astype(jnp.float32), 0)
    pieces = []
    for at in range(PIECES):
        lines = [
            got[feature_rows + at * WINDOW + step : feature_rows + at * WINDOW + step + 1]
            for step in range(WINDOW)
        ]
        pieces.append(jnp.concatenate(lines, 1).astype(jnp.int32))
    codes = jnp.concatenate([pieces[0] + 256 * pieces[1], pieces[2] + 256 * pieces[3]], 1)
    span = codes.shape[1]
    level = lax.broadcasted_iota(jnp.int32, (LANES, span), 0)
    taken = ((level & 7) < FSQ_DIMS) & (level < 24)
    shift = jnp.where(taken, (level & 7) * 3, 0)
    value = (2 * ((jnp.broadcast_to(codes, (LANES, span)) >> shift) & 7) - 7).astype(
        jnp.float32
    ) * 0.125
    value = jnp.where(taken, value, 0.0).astype(jnp.bfloat16)

    count = TILE_ROWS * IMG_W
    begin = TILE_H * ROW_WORDS * section - HALO * ROW_WORDS
    offset = begin & (LANES - 1)
    spot = lax.broadcasted_iota(jnp.int32, (count, 1), 0)
    line = spot // IMG_W + TILE_H * section - HALO
    inside = (line >= 0) & (line < IMG_SPLIT * TILE_H)
    target = jnp.where(inside, (spot >> 1) + offset + (span // 2) * (spot & 1), -1)
    chooser = jnp.where(
        lax.broadcasted_iota(jnp.int32, (count, span), 1) == target, 1.0, 0.0
    ).astype(jnp.bfloat16)
    placed = lax.dot_general(
        chooser, value, (((1,), (1,)), ((), ())), preferred_element_type=jnp.float32
    ).astype(jnp.bfloat16)
    latent = jnp.dot(placed, weights, preferred_element_type=jnp.float32).astype(jnp.bfloat16)

    hidden = convolve(latent, w_one, sems, copies[0])
    count = hidden.shape[0]
    line = lax.broadcasted_iota(jnp.int32, (count, 1), 0) // IMG_W + TILE_H * section - 1
    inside = (line >= 0) & (line < IMG_SPLIT * TILE_H)
    activated = jnp.where(inside, hidden * jax.nn.sigmoid(hidden), 0.0).astype(jnp.bfloat16)
    out_ref[...] = convolve(activated, w_two, sems, copies[1]).astype(jnp.bfloat16)


def on_device(
    queries,
    new_keys,
    new_values,
    cache_keys,
    cache_values,
    cache_lengths,
    out_weight,
    codes,
    tile_slot,
    code_weight,
    conv_one,
    conv_two,
):
    tiles = lax.axis_size("rows")
    place = lax.axis_index("rows")
    rows, width = queries.shape
    cache = cache_keys.shape[1]
    channels = code_weight.shape[1]
    share = width // tiles
    per = share // LANES if share % LANES == 0 else 0
    feature_rows = rows * share // LANES
    depth = message_rows(feature_rows)
    params = pltpu.CompilerParams(vmem_limit_bytes=VMEM_LIMIT)
    smem = pl.BlockSpec(memory_space=pltpu.SMEM)

    def full(*shape):
        return pl.BlockSpec(shape, lambda *_: (0,) * len(shape))

    outgoing, attended = pl.pallas_call(
        functools.partial(attend_kernel, tiles=tiles, per=per, feature_rows=feature_rows),
        grid=(rows,),
        in_specs=[
            smem,
            smem,
            full(rows, width),
            full(rows, width),
            full(rows, width),
            pl.BlockSpec((1, cache, width), lambda r: (r, 0, 0)),
            pl.BlockSpec((1, cache, width), lambda r: (r, 0, 0)),
            full(*codes.shape),
        ],
        out_specs=[full(tiles, depth, LANES), full(rows, width)],
        out_shape=[
            jax.ShapeDtypeStruct((tiles, depth, LANES), jnp.bfloat16),
            jax.ShapeDtypeStruct((rows, width), jnp.float32),
        ],
        scratch_shapes=[pltpu.VMEM((tiles, depth, LANES), jnp.float32)],
        compiler_params=params,
    )(cache_lengths, tile_slot, queries, new_keys, new_values, cache_keys, cache_values, codes)
    if not per:
        feats = attended.astype(jnp.bfloat16).reshape(rows, tiles, share)
        feats = feats.transpose(1, 0, 2).reshape(tiles, feature_rows, LANES)
        outgoing = lax.dynamic_update_slice(outgoing, feats, (0, 0, 0))
    incoming = lax.all_to_all(outgoing, "rows", split_axis=0, concat_axis=0, tiled=True)

    lines = 8
    groups = width // (lines * LANES)
    if per:
        partials = pl.pallas_call(
            functools.partial(project_kernel, rows=rows, per=per),
            out_shape=jax.ShapeDtypeStruct((tiles, groups, rows * lines, LANES), jnp.bfloat16),
            scratch_shapes=[
                pltpu.VMEM((tiles * depth, LANES), jnp.float32),
                pltpu.VMEM((groups, tiles * rows * lines, LANES), jnp.float32),
            ],
            compiler_params=params,
        )(incoming, out_weight)
    else:
        feats = incoming[:, :feature_rows].reshape(tiles * rows, share)
        partials = jnp.dot(feats, out_weight, preferred_element_type=jnp.float32)
        partials = partials.astype(jnp.bfloat16).reshape(tiles, rows, groups, lines, LANES)
        partials = partials.transpose(0, 2, 1, 3, 4).reshape(tiles, groups, rows * lines, LANES)
    gathered = lax.all_to_all(partials, "rows", split_axis=0, concat_axis=0, tiled=True)

    section = (place + IMG_SPLIT // 2) % tiles % IMG_SPLIT
    vmem = pl.BlockSpec(memory_space=pltpu.VMEM)
    anywhere = pl.BlockSpec(memory_space=pl.ANY)
    decoded = pl.pallas_call(
        functools.partial(decode_kernel, feature_rows=feature_rows),
        in_specs=[smem, vmem, vmem, anywhere, anywhere],
        out_specs=vmem,
        out_shape=jax.ShapeDtypeStruct((TILE_H * IMG_W, channels), jnp.bfloat16),
        scratch_shapes=[
            pltpu.VMEM((3, 3 * channels, channels), jnp.bfloat16),
            pltpu.VMEM((3, 3 * channels, channels), jnp.bfloat16),
            pltpu.VMEM((8, channels), jnp.float32),
            pltpu.SemaphoreType.DMA((2, 3, 3)),
        ],
        compiler_params=params,
    )(section.reshape(1).astype(jnp.int32), incoming, code_weight, conv_one, conv_two)

    mixed = pl.pallas_call(
        functools.partial(total_kernel, rows=rows),
        out_shape=jax.ShapeDtypeStruct((rows, width), jnp.bfloat16),
        scratch_shapes=[pltpu.VMEM((groups, rows * lines, LANES), jnp.float32)],
        compiler_params=params,
    )(gathered)
    return (mixed, decoded.reshape(TILE_H, IMG_W, channels))


def solution(mesh):
    in_specs = (
        P(("groups", "rows"), None),
        P(("groups", "rows"), None),
        P(("groups", "rows"), None),
        P(("groups", "rows"), None, None),
        P(("groups", "rows"), None, None),
        P(("groups", "rows")),
        P("rows", None),
        P(("groups", "rows"), None),
        P(("groups", "rows")),
        P(),
        P(),
        P(),
    )
    out_specs = (P(("groups", "rows"), None), P(("groups", "rows"), None, None))
    return jax.shard_map(
        on_device, mesh=mesh, in_specs=in_specs, out_specs=out_specs, check_vma=False
    )
```

```python
import functools
import math

import jax
import jax.numpy as jnp
from jax import lax
from jax.experimental import pallas as pl
from jax.experimental.pallas import tpu as pltpu
from jax.sharding import PartitionSpec as P

HEAD_DIM = 128
FSQ_DIMS = 5
IMG_SPLIT = 4
TILE_H = 8
IMG_W = 48
LANES = 128
HALO = 2
ROW_WORDS = IMG_W // 2
TILE_ROWS = TILE_H + 2 * HALO
WINDOW = 3
PIECES = 4
CODE_ROWS = WINDOW * PIECES
TAP_ROWS = 24
FOLD_ROWS = 256
VMEM_LIMIT = 24 * 1024 * 1024


def window_start(section):
    return (TILE_H * ROW_WORDS * section - HALO * ROW_WORDS) // LANES


def message_rows(features):
    return -(-(features + CODE_ROWS) // 16) * 16


def attend_kernel(
    lengths,
    slots,
    q_ref,
    nk_ref,
    nv_ref,
    k_ref,
    v_ref,
    codes_ref,
    out_ref,
    att_ref,
    msg,
    *,
    tiles,
    per,
    feature_rows,
):
    row = pl.program_id(0)
    rows, width = q_ref.shape
    heads = width // HEAD_DIM
    factor = 1.0 / math.sqrt(HEAD_DIM)

    def own_row(ref):
        whole = ref[...].astype(jnp.float32)
        at = lax.broadcasted_iota(jnp.int32, whole.shape, 0)
        return jnp.sum(jnp.where(at == row, whole, 0.0), 0, keepdims=True)

    query, new_key, new_value = own_row(q_ref), own_row(nk_ref), own_row(nv_ref)
    same = (
        lax.broadcasted_iota(jnp.int32, (heads, width), 1) // HEAD_DIM
        == lax.broadcasted_iota(jnp.int32, (heads, width), 0)
    )
    spread = jnp.where(same, query, 0.0).astype(jnp.bfloat16)
    scores = (
        lax.dot_general(
            spread, k_ref[0], (((1,), (1,)), ((), ())), preferred_element_type=jnp.float32
        )
        * factor
    )
    own_score = jnp.sum(jnp.where(same, query * new_key, 0.0), 1, keepdims=True) * factor
    live = lax.broadcasted_iota(jnp.int32, scores.shape, 1) < lengths[row]
    scores = jnp.where(live, scores, jnp.float32(-1e30))
    highest = jnp.maximum(jnp.max(scores, 1, keepdims=True), own_score)
    cache_exp = jnp.where(live, jnp.exp(scores - highest), 0.0)
    own_exp = jnp.exp(own_score - highest)
    denom = jnp.sum(cache_exp, 1, keepdims=True) + own_exp
    cache_weight = (cache_exp / denom).astype(jnp.bfloat16)
    own_weight = (own_exp / denom).astype(jnp.bfloat16).astype(jnp.float32)
    mixed_in = jnp.dot(cache_weight, v_ref[0], preferred_element_type=jnp.float32)
    attended = jnp.sum(
        jnp.where(same, mixed_in + own_weight * new_value, 0.0), 0, keepdims=True
    )

    @pl.when(row == 0)
    def _():
        msg[...] = jnp.zeros_like(msg)
        pieces = []
        words = codes_ref[...]
        for shift, mask in ((0, 255), (8, 127), (15, 255), (23, 127)):
            pieces.append(((words >> shift) & mask).astype(jnp.float32))
        blocks = words.shape[1] // LANES
        for tile in range(tiles):
            number = (tile + IMG_SPLIT // 2) % tiles
            start = window_start(number % IMG_SPLIT)
            gains = [
                jnp.where(slots[r] == number // IMG_SPLIT, 1.0, 0.0).astype(jnp.float32)
                for r in range(rows)
            ]
            for at, piece in enumerate(pieces):
                for step in range(WINDOW):
                    block = start + step
                    if block < 0 or block >= blocks:
                        continue
                    part = piece[:, block * LANES : (block + 1) * LANES]
                    total = part[0:1] * gains[0]
                    for r in range(1, rows):
                        total = total + part[r : r + 1] * gains[r]
                    place = feature_rows + at * WINDOW + step
                    msg[tile, place : place + 1, :] = total

    if per:
        for tile in range(tiles):
            for step in range(per):
                begin = (tile * per + step) * LANES
                msg[tile, pl.ds(row * per + step, 1), :] = attended[:, begin : begin + LANES]
    at = lax.broadcasted_iota(jnp.int32, att_ref.shape, 0)
    att_ref[...] = jnp.where(at == row, attended, att_ref[...])

    @pl.when(row == rows - 1)
    def _():
        out_ref[...] = msg[...].astype(jnp.bfloat16)


def project_kernel(in_ref, w_ref, out_ref, held, total, *, rows, per):
    tiles, depth = in_ref.shape[:2]
    held[...] = in_ref[...].astype(jnp.float32).reshape(held.shape)
    groups, _, _ = total.shape
    lines = out_ref.shape[2] // rows
    lhs = []
    for row in range(rows):
        parts = [held[pl.ds(row * per + j, tiles, stride=depth), :] for j in range(per)]
        lhs.append(jnp.concatenate(parts, 1))
    product = jnp.dot(
        jnp.concatenate(lhs, 0).astype(jnp.bfloat16), w_ref[...], preferred_element_type=jnp.float32
    )
    for row in range(rows):
        for group in range(groups):
            for line in range(lines):
                begin = (group * lines + line) * LANES
                total[group, pl.ds(row * lines + line, tiles, stride=rows * lines), :] = product[
                    row * tiles : (row + 1) * tiles, begin : begin + LANES
                ]
    for group in range(groups):
        out_ref[:, group] = (
            total[group].astype(jnp.bfloat16).reshape(tiles, rows * lines, LANES)
        )


def total_kernel(in_ref, out_ref, held, *, rows):
    tiles, groups, depth, _ = in_ref.shape
    lines = depth // rows
    held[...] = jnp.sum(in_ref[...].astype(jnp.float32), 0)
    for group in range(groups):
        for line in range(lines):
            begin = (group * lines + line) * LANES
            out_ref[:, begin : begin + LANES] = held[
                group, pl.ds(line, rows, stride=lines), :
            ].astype(jnp.bfloat16)


def split_three(whole):
    high = whole.astype(jnp.bfloat16).astype(jnp.float32)
    middle = (whole - high).astype(jnp.bfloat16).astype(jnp.float32)
    return jnp.concatenate([high, middle, whole - high - middle], 0)


def fold_kernel(cw_ref, conv_ref, out_ref, levels_w, folded):
    step = pl.program_id(0)
    taps = conv_ref.shape[1]
    levels_w[...] = jnp.zeros_like(levels_w)
    levels_w[0:FSQ_DIMS, :] = cw_ref[...]
    left = split_three(levels_w[...]).astype(jnp.bfloat16)

    @pl.when(step == 0)
    def _():
        folded[...] = jnp.zeros_like(folded)

    for tap in range(taps):
        parts = jnp.dot(left, conv_ref[0, tap], preferred_element_type=jnp.float32)
        total = parts[0:8] + parts[8:16] + parts[16:24]
        at = pl.multiple_of((step * taps + tap) * TAP_ROWS, 8)
        folded[pl.ds(at, TAP_ROWS), :] = split_three(total)

    @pl.when(step == pl.num_programs(0) - 1)
    def _():
        out_ref[...] = folded[...].astype(jnp.bfloat16)


def decode_kernel(section_ref, in_ref, fold_ref, two_ref, out_ref, *, feature_rows):
    section = section_ref[0]
    got = jnp.sum(in_ref[...].astype(jnp.float32), 0)
    pieces = []
    for at in range(PIECES):
        lines = [
            got[feature_rows + at * WINDOW + step : feature_rows + at * WINDOW + step + 1]
            for step in range(WINDOW)
        ]
        pieces.append(jnp.concatenate(lines, 1).astype(jnp.int32))
    codes = jnp.concatenate([pieces[0] + 256 * pieces[1], pieces[2] + 256 * pieces[3]], 1)
    span = codes.shape[1]
    depth = fold_ref.shape[0]
    level = lax.broadcasted_iota(jnp.int32, (8, span), 0)
    taken = level < FSQ_DIMS
    shift = jnp.where(taken, level * 3, 0)
    value = (2 * ((jnp.broadcast_to(codes, (8, span)) >> shift) & 7) - 7).astype(
        jnp.float32
    ) * 0.125
    value = jnp.where(taken, value, 0.0)
    value = jnp.concatenate([value] * (depth // 8), 0).astype(jnp.bfloat16)

    count = TILE_ROWS * IMG_W
    begin = TILE_H * ROW_WORDS * section - HALO * ROW_WORDS
    offset = begin & (LANES - 1)
    spot = lax.broadcasted_iota(jnp.int32, (count, 1), 0)
    line = spot // IMG_W + TILE_H * section - HALO
    inside = (line >= 0) & (line < IMG_SPLIT * TILE_H)
    target = jnp.where(inside, (spot >> 1) + offset + (span // 2) * (spot & 1), -1)
    chooser = jnp.where(
        lax.broadcasted_iota(jnp.int32, (count, span), 1) == target, 1.0, 0.0
    ).astype(jnp.bfloat16)
    placed = lax.dot_general(
        chooser, value, (((1,), (1,)), ((), ())), preferred_element_type=jnp.float32
    )
    column = spot % IMG_W
    moved = [
        jnp.where(column == 0, 0.0, pltpu.roll(placed, 1, 0)),
        placed,
        jnp.where(column == IMG_W - 1, 0.0, pltpu.roll(placed, count - 1, 0)),
    ]
    count = count - 2 * IMG_W
    tap_of = lax.broadcasted_iota(jnp.int32, (1, depth), 1) // TAP_ROWS
    taps = jnp.zeros((count, depth), jnp.float32)
    for dr in range(3):
        for dc in range(3):
            taps = jnp.where(
                tap_of == 3 * dr + dc, moved[dc][dr * IMG_W : dr * IMG_W + count], taps
            )
    hidden = jnp.dot(taps.astype(jnp.bfloat16), fold_ref[...], preferred_element_type=jnp.float32)

    line = lax.broadcasted_iota(jnp.int32, (count, 1), 0) // IMG_W + TILE_H * section - 1
    inside = (line >= 0) & (line < IMG_SPLIT * TILE_H)
    activated = jnp.where(inside, hidden * jax.nn.sigmoid(hidden), 0.0).astype(jnp.bfloat16)

    count = count - 2 * IMG_W
    column = lax.broadcasted_iota(jnp.int32, (count, 1), 0) % IMG_W
    summed = None
    for dc in (1, 0, 2):
        part = None
        for dr in range(3):
            term = jnp.dot(
                activated[dr * IMG_W : dr * IMG_W + count],
                two_ref[dr, dc],
                preferred_element_type=jnp.float32,
            )
            part = term if part is None else part + term
        if dc == 0:
            part = jnp.where(column == 0, 0.0, pltpu.roll(part, 1, 0))
        if dc == 2:
            part = jnp.where(column == IMG_W - 1, 0.0, pltpu.roll(part, count - 1, 0))
        summed = part if summed is None else summed + part
    out_ref[...] = summed.astype(jnp.bfloat16)


def near(array):
    return pltpu.with_memory_space_constraint(array, pltpu.VMEM)


def far(array):
    return pltpu.with_memory_space_constraint(array, pltpu.HBM)


def on_device(
    queries,
    new_keys,
    new_values,
    cache_keys,
    cache_values,
    cache_lengths,
    out_weight,
    codes,
    tile_slot,
    code_weight,
    conv_one,
    conv_two,
):
    tiles = lax.axis_size("rows")
    place = lax.axis_index("rows")
    rows, width = queries.shape
    cache = cache_keys.shape[1]
    channels = code_weight.shape[1]
    share = width // tiles
    per = share // LANES if share % LANES == 0 else 0
    feature_rows = rows * share // LANES
    depth = message_rows(feature_rows)
    params = pltpu.CompilerParams(vmem_limit_bytes=VMEM_LIMIT)
    smem = pl.BlockSpec(memory_space=pltpu.SMEM)
    vmem = pl.BlockSpec(memory_space=pltpu.VMEM)

    def full(*shape):
        return pl.BlockSpec(shape, lambda *_: (0,) * len(shape))

    outgoing, attended = pl.pallas_call(
        functools.partial(attend_kernel, tiles=tiles, per=per, feature_rows=feature_rows),
        grid=(rows,),
        in_specs=[
            smem,
            smem,
            full(rows, width),
            full(rows, width),
            full(rows, width),
            pl.BlockSpec((1, cache, width), lambda r: (r, 0, 0)),
            pl.BlockSpec((1, cache, width), lambda r: (r, 0, 0)),
            full(*codes.shape),
        ],
        out_specs=[full(tiles, depth, LANES), full(rows, width)],
        out_shape=[
            jax.ShapeDtypeStruct((tiles, depth, LANES), jnp.bfloat16),
            jax.ShapeDtypeStruct((rows, width), jnp.float32),
        ],
        scratch_shapes=[pltpu.VMEM((tiles, depth, LANES), jnp.float32)],
        compiler_params=params,
    )(
        cache_lengths,
        tile_slot,
        far(queries),
        far(new_keys),
        far(new_values),
        far(cache_keys),
        far(cache_values),
        far(codes),
    )
    if not per:
        feats = attended.astype(jnp.bfloat16).reshape(rows, tiles, share)
        feats = feats.transpose(1, 0, 2).reshape(tiles, feature_rows, LANES)
        outgoing = lax.dynamic_update_slice(outgoing, feats, (0, 0, 0))
    incoming = lax.all_to_all(outgoing, "rows", split_axis=0, concat_axis=0, tiled=True)

    folded = pl.pallas_call(
        fold_kernel,
        grid=(conv_one.shape[0],),
        in_specs=[
            full(*code_weight.shape),
            pl.BlockSpec((1,) + conv_one.shape[1:], lambda t: (t, 0, 0, 0)),
        ],
        out_specs=full(FOLD_ROWS, channels),
        out_shape=jax.ShapeDtypeStruct((FOLD_ROWS, channels), jnp.bfloat16),
        scratch_shapes=[
            pltpu.VMEM((8, channels), jnp.float32),
            pltpu.VMEM((FOLD_ROWS, channels), jnp.float32),
        ],
        compiler_params=params,
    )(far(code_weight), far(conv_one))

    lines = 8
    groups = width // (lines * LANES)
    if per:
        partials = pl.pallas_call(
            functools.partial(project_kernel, rows=rows, per=per),
            in_specs=[vmem, vmem],
            out_shape=jax.ShapeDtypeStruct((tiles, groups, rows * lines, LANES), jnp.bfloat16),
            scratch_shapes=[
                pltpu.VMEM((tiles * depth, LANES), jnp.float32),
                pltpu.VMEM((groups, tiles * rows * lines, LANES), jnp.float32),
            ],
            compiler_params=params,
        )(incoming, near(out_weight))
    else:
        feats = incoming[:, :feature_rows].reshape(tiles * rows, share)
        partials = jnp.dot(feats, out_weight, preferred_element_type=jnp.float32)
        partials = partials.astype(jnp.bfloat16).reshape(tiles, rows, groups, lines, LANES)
        partials = partials.transpose(0, 2, 1, 3, 4).reshape(tiles, groups, rows * lines, LANES)
    gathered = lax.all_to_all(partials, "rows", split_axis=0, concat_axis=0, tiled=True)

    section = (place + IMG_SPLIT // 2) % tiles % IMG_SPLIT
    decoded = pl.pallas_call(
        functools.partial(decode_kernel, feature_rows=feature_rows),
        in_specs=[smem, vmem, vmem, vmem],
        out_specs=vmem,
        out_shape=jax.ShapeDtypeStruct((TILE_H * IMG_W, channels), jnp.bfloat16),
        compiler_params=params,
    )(section.reshape(1).astype(jnp.int32), incoming, folded, near(conv_two))

    mixed = pl.pallas_call(
        functools.partial(total_kernel, rows=rows),
        in_specs=[vmem],
        out_shape=jax.ShapeDtypeStruct((rows, width), jnp.bfloat16),
        scratch_shapes=[pltpu.VMEM((groups, rows * lines, LANES), jnp.float32)],
        compiler_params=params,
    )(near(gathered))
    return (mixed, decoded.reshape(TILE_H, IMG_W, channels))


def solution(mesh):
    in_specs = (
        P(("groups", "rows"), None),
        P(("groups", "rows"), None),
        P(("groups", "rows"), None),
        P(("groups", "rows"), None, None),
        P(("groups", "rows"), None, None),
        P(("groups", "rows")),
        P("rows", None),
        P(("groups", "rows"), None),
        P(("groups", "rows")),
        P(),
        P(),
        P(),
    )
    out_specs = (P(("groups", "rows"), None), P(("groups", "rows"), None, None))
    return jax.shard_map(
        on_device, mesh=mesh, in_specs=in_specs, out_specs=out_specs, check_vma=False
    )
```

```python
import functools
import math

import jax
import jax.numpy as jnp
from jax import lax
from jax.experimental import pallas as pl
from jax.experimental.pallas import tpu as pltpu
from jax.sharding import PartitionSpec as P

HEAD_DIM = 128
FSQ_DIMS = 5
IMG_SPLIT = 4
TILE_H = 8
IMG_W = 48
LANES = 128
HALO = 2
ROW_WORDS = IMG_W // 2
TILE_ROWS = TILE_H + 2 * HALO
WINDOW = 3
PIECES = 4
CODE_ROWS = WINDOW * PIECES
TAP_ROWS = 24
FOLD_ROWS = 256
VMEM_LIMIT = 24 * 1024 * 1024


def window_start(section):
    return (TILE_H * ROW_WORDS * section - HALO * ROW_WORDS) // LANES


def message_rows(features):
    return -(-(features + CODE_ROWS) // 16) * 16


def attend_kernel(
    lengths,
    slots,
    q_ref,
    nk_ref,
    nv_ref,
    k_ref,
    v_ref,
    codes_ref,
    out_ref,
    att_ref,
    msg,
    *,
    tiles,
    per,
    feature_rows,
):
    row = pl.program_id(0)
    rows, width = q_ref.shape
    heads = width // HEAD_DIM
    factor = 1.0 / math.sqrt(HEAD_DIM)

    def own_row(ref):
        whole = ref[...].astype(jnp.float32)
        at = lax.broadcasted_iota(jnp.int32, whole.shape, 0)
        return jnp.sum(jnp.where(at == row, whole, 0.0), 0, keepdims=True)

    query, new_key, new_value = own_row(q_ref), own_row(nk_ref), own_row(nv_ref)
    same = (
        lax.broadcasted_iota(jnp.int32, (heads, width), 1) // HEAD_DIM
        == lax.broadcasted_iota(jnp.int32, (heads, width), 0)
    )
    spread = jnp.where(same, query, 0.0).astype(jnp.bfloat16)
    scores = (
        lax.dot_general(
            spread, k_ref[0], (((1,), (1,)), ((), ())), preferred_element_type=jnp.float32
        )
        * factor
    )
    own_score = jnp.sum(jnp.where(same, query * new_key, 0.0), 1, keepdims=True) * factor
    live = lax.broadcasted_iota(jnp.int32, scores.shape, 1) < lengths[row]
    scores = jnp.where(live, scores, jnp.float32(-1e30))
    highest = jnp.maximum(jnp.max(scores, 1, keepdims=True), own_score)
    cache_exp = jnp.where(live, jnp.exp(scores - highest), 0.0)
    own_exp = jnp.exp(own_score - highest)
    denom = jnp.sum(cache_exp, 1, keepdims=True) + own_exp
    cache_weight = (cache_exp / denom).astype(jnp.bfloat16)
    own_weight = (own_exp / denom).astype(jnp.bfloat16).astype(jnp.float32)
    mixed_in = jnp.dot(cache_weight, v_ref[0], preferred_element_type=jnp.float32)
    attended = jnp.sum(
        jnp.where(same, mixed_in + own_weight * new_value, 0.0), 0, keepdims=True
    )

    @pl.when(row == 0)
    def _():
        msg[...] = jnp.zeros_like(msg)
        pieces = []
        words = codes_ref[...]
        for shift, mask in ((0, 255), (8, 127), (15, 255), (23, 127)):
            pieces.append(((words >> shift) & mask).astype(jnp.float32))
        blocks = words.shape[1] // LANES
        for tile in range(tiles):
            number = (tile + IMG_SPLIT // 2) % tiles
            start = window_start(number % IMG_SPLIT)
            gains = [
                jnp.where(slots[r] == number // IMG_SPLIT, 1.0, 0.0).astype(jnp.float32)
                for r in range(rows)
            ]
            for at, piece in enumerate(pieces):
                for step in range(WINDOW):
                    block = start + step
                    if block < 0 or block >= blocks:
                        continue
                    part = piece[:, block * LANES : (block + 1) * LANES]
                    total = part[0:1] * gains[0]
                    for r in range(1, rows):
                        total = total + part[r : r + 1] * gains[r]
                    place = feature_rows + at * WINDOW + step
                    msg[tile, place : place + 1, :] = total

    if per:
        for tile in range(tiles):
            for step in range(per):
                begin = (tile * per + step) * LANES
                msg[tile, pl.ds(row * per + step, 1), :] = attended[:, begin : begin + LANES]
    at = lax.broadcasted_iota(jnp.int32, att_ref.shape, 0)
    att_ref[...] = jnp.where(at == row, attended, att_ref[...])

    @pl.when(row == rows - 1)
    def _():
        out_ref[...] = msg[...].astype(jnp.bfloat16)


def project_kernel(parity_ref, in_ref, w_ref, keep_ref, send_ref, held, total, *, rows, per):
    tiles, depth = in_ref.shape[:2]
    held[...] = in_ref[...].astype(jnp.float32).reshape(held.shape)
    groups, _, _ = total.shape
    lines = keep_ref.shape[2] // rows
    lhs = []
    for row in range(rows):
        parts = [held[pl.ds(row * per + j, tiles, stride=depth), :] for j in range(per)]
        lhs.append(jnp.concatenate(parts, 1))
    product = jnp.dot(
        jnp.concatenate(lhs, 0).astype(jnp.bfloat16), w_ref[...], preferred_element_type=jnp.float32
    )
    for row in range(rows):
        for group in range(groups):
            for line in range(lines):
                begin = (group * lines + line) * LANES
                total[group, pl.ds(row * lines + line, tiles, stride=rows * lines), :] = product[
                    row * tiles : (row + 1) * tiles, begin : begin + LANES
                ]
    even = parity_ref[0] == 0
    for group in range(groups):
        pairs = total[group].reshape(tiles // 2, 2, rows * lines, LANES)
        first, second = pairs[:, 0], pairs[:, 1]
        keep_ref[:, group] = jnp.where(even, first, second)
        send_ref[:, group] = jnp.where(even, second, first).astype(jnp.bfloat16)


def add_kernel(keep_ref, got_ref, out_ref):
    out_ref[...] = (keep_ref[...] + got_ref[...].astype(jnp.float32)).astype(jnp.bfloat16)


def total_kernel(in_ref, out_ref, held, *, rows):
    tiles, groups, depth, _ = in_ref.shape
    lines = depth // rows
    held[...] = jnp.sum(in_ref[...].astype(jnp.float32), 0)
    for group in range(groups):
        for line in range(lines):
            begin = (group * lines + line) * LANES
            out_ref[:, begin : begin + LANES] = held[
                group, pl.ds(line, rows, stride=lines), :
            ].astype(jnp.bfloat16)


def split_three(whole):
    high = whole.astype(jnp.bfloat16).astype(jnp.float32)
    middle = (whole - high).astype(jnp.bfloat16).astype(jnp.float32)
    return jnp.concatenate([high, middle, whole - high - middle], 0)


def fold_kernel(
    cw_ref, conv_ref, weight_ref, after_ref, out_ref, near_ref, levels_w, folded, held, sems, near_sem
):
    del after_ref
    taps = [(dr, dc) for dr in range(3) for dc in range(3)]
    copies = [
        pltpu.make_async_copy(conv_ref.at[dr, dc], held.at[at], sems.at[at])
        for at, (dr, dc) in enumerate(taps)
    ]
    for copy in copies:
        copy.start()
    bring = pltpu.make_async_copy(weight_ref, near_ref, near_sem)
    bring.start()
    levels_w[...] = jnp.zeros_like(levels_w)
    levels_w[0:FSQ_DIMS, :] = cw_ref[...]
    left = split_three(levels_w[...]).astype(jnp.bfloat16)
    folded[...] = jnp.zeros_like(folded)
    for at, copy in enumerate(copies):
        copy.wait()
        parts = jnp.dot(left, held[at], preferred_element_type=jnp.float32)
        total = parts[0:8] + parts[8:16] + parts[16:24]
        folded[at * TAP_ROWS : (at + 1) * TAP_ROWS, :] = split_three(total)
    out_ref[...] = folded[...].astype(jnp.bfloat16)
    bring.wait()


def decode_kernel(section_ref, in_ref, fold_ref, two_ref, after_ref, out_ref, *, feature_rows):
    del after_ref
    section = section_ref[0]
    got = jnp.sum(in_ref[...].astype(jnp.float32), 0)
    pieces = []
    for at in range(PIECES):
        lines = [
            got[feature_rows + at * WINDOW + step : feature_rows + at * WINDOW + step + 1]
            for step in range(WINDOW)
        ]
        pieces.append(jnp.concatenate(lines, 1).astype(jnp.int32))
    codes = jnp.concatenate([pieces[0] + 256 * pieces[1], pieces[2] + 256 * pieces[3]], 1)
    span = codes.shape[1]
    depth = fold_ref.shape[0]
    level = lax.broadcasted_iota(jnp.int32, (8, span), 0)
    taken = level < FSQ_DIMS
    shift = jnp.where(taken, level * 3, 0)
    value = (2 * ((jnp.broadcast_to(codes, (8, span)) >> shift) & 7) - 7).astype(
        jnp.float32
    ) * 0.125
    value = jnp.where(taken, value, 0.0)
    value = jnp.concatenate([value] * (depth // 8), 0).astype(jnp.bfloat16)

    count = TILE_ROWS * IMG_W
    begin = TILE_H * ROW_WORDS * section - HALO * ROW_WORDS
    offset = begin & (LANES - 1)
    spot = lax.broadcasted_iota(jnp.int32, (count, 1), 0)
    line = spot // IMG_W + TILE_H * section - HALO
    inside = (line >= 0) & (line < IMG_SPLIT * TILE_H)
    target = jnp.where(inside, (spot >> 1) + offset + (span // 2) * (spot & 1), -1)
    chooser = jnp.where(
        lax.broadcasted_iota(jnp.int32, (count, span), 1) == target, 1.0, 0.0
    ).astype(jnp.bfloat16)
    placed = lax.dot_general(
        chooser, value, (((1,), (1,)), ((), ())), preferred_element_type=jnp.float32
    )
    column = spot % IMG_W
    moved = [
        jnp.where(column == 0, 0.0, pltpu.roll(placed, 1, 0)),
        placed,
        jnp.where(column == IMG_W - 1, 0.0, pltpu.roll(placed, count - 1, 0)),
    ]
    count = count - 2 * IMG_W
    tap_of = lax.broadcasted_iota(jnp.int32, (1, depth), 1) // TAP_ROWS
    taps = jnp.zeros((count, depth), jnp.float32)
    for dr in range(3):
        for dc in range(3):
            taps = jnp.where(
                tap_of == 3 * dr + dc, moved[dc][dr * IMG_W : dr * IMG_W + count], taps
            )
    hidden = jnp.dot(taps.astype(jnp.bfloat16), fold_ref[...], preferred_element_type=jnp.float32)

    line = lax.broadcasted_iota(jnp.int32, (count, 1), 0) // IMG_W + TILE_H * section - 1
    inside = (line >= 0) & (line < IMG_SPLIT * TILE_H)
    activated = jnp.where(inside, hidden * jax.nn.sigmoid(hidden), 0.0).astype(jnp.bfloat16)

    count = count - 2 * IMG_W
    column = lax.broadcasted_iota(jnp.int32, (count, 1), 0) % IMG_W
    summed = None
    for dc in (1, 0, 2):
        part = None
        for dr in range(3):
            term = jnp.dot(
                activated[dr * IMG_W : dr * IMG_W + count],
                two_ref[dr, dc],
                preferred_element_type=jnp.float32,
            )
            part = term if part is None else part + term
        if dc == 0:
            part = jnp.where(column == 0, 0.0, pltpu.roll(part, 1, 0))
        if dc == 2:
            part = jnp.where(column == IMG_W - 1, 0.0, pltpu.roll(part, count - 1, 0))
        summed = part if summed is None else summed + part
    out_ref[...] = summed.astype(jnp.bfloat16)


def near(array):
    return pltpu.with_memory_space_constraint(array, pltpu.VMEM)


def far(array):
    return pltpu.with_memory_space_constraint(array, pltpu.HBM)


def on_device(
    queries,
    new_keys,
    new_values,
    cache_keys,
    cache_values,
    cache_lengths,
    out_weight,
    codes,
    tile_slot,
    code_weight,
    conv_one,
    conv_two,
):
    tiles = lax.axis_size("rows")
    place = lax.axis_index("rows")
    rows, width = queries.shape
    cache = cache_keys.shape[1]
    channels = code_weight.shape[1]
    share = width // tiles
    per = share // LANES if share % LANES == 0 else 0
    feature_rows = rows * share // LANES
    depth = message_rows(feature_rows)
    params = pltpu.CompilerParams(vmem_limit_bytes=VMEM_LIMIT)
    smem = pl.BlockSpec(memory_space=pltpu.SMEM)
    vmem = pl.BlockSpec(memory_space=pltpu.VMEM)
    anywhere = pl.BlockSpec(memory_space=pl.ANY)

    def full(*shape):
        return pl.BlockSpec(shape, lambda *_: (0,) * len(shape))

    outgoing, attended = pl.pallas_call(
        functools.partial(attend_kernel, tiles=tiles, per=per, feature_rows=feature_rows),
        grid=(rows,),
        in_specs=[
            smem,
            smem,
            full(rows, width),
            full(rows, width),
            full(rows, width),
            pl.BlockSpec((1, cache, width), lambda r: (r, 0, 0)),
            pl.BlockSpec((1, cache, width), lambda r: (r, 0, 0)),
            full(*codes.shape),
        ],
        out_specs=[full(tiles, depth, LANES), full(rows, width)],
        out_shape=[
            jax.ShapeDtypeStruct((tiles, depth, LANES), jnp.bfloat16),
            jax.ShapeDtypeStruct((rows, width), jnp.float32),
        ],
        scratch_shapes=[pltpu.VMEM((tiles, depth, LANES), jnp.float32)],
        compiler_params=pltpu.CompilerParams(vmem_limit_bytes=56 * 1024 * 1024),
    )(
        cache_lengths,
        tile_slot,
        far(queries),
        far(new_keys),
        far(new_values),
        far(cache_keys),
        far(cache_values),
        far(codes),
    )
    if not per:
        feats = attended.astype(jnp.bfloat16).reshape(rows, tiles, share)
        feats = feats.transpose(1, 0, 2).reshape(tiles, feature_rows, LANES)
        outgoing = lax.dynamic_update_slice(outgoing, feats, (0, 0, 0))
    incoming = lax.all_to_all(outgoing, "rows", split_axis=0, concat_axis=0, tiled=True)

    folded, weight = pl.pallas_call(
        fold_kernel,
        in_specs=[vmem, anywhere, anywhere, anywhere],
        out_specs=[vmem, vmem],
        out_shape=[
            jax.ShapeDtypeStruct((FOLD_ROWS, channels), jnp.bfloat16),
            pltpu.VMEM(out_weight.shape, out_weight.dtype),
        ],
        scratch_shapes=[
            pltpu.VMEM((8, channels), jnp.float32),
            pltpu.VMEM((FOLD_ROWS, channels), jnp.float32),
            pltpu.VMEM((9,) + conv_one.shape[2:], conv_one.dtype),
            pltpu.SemaphoreType.DMA((9,)),
            pltpu.SemaphoreType.DMA,
        ],
        compiler_params=params,
    )(far(code_weight), far(conv_one), far(out_weight), far(outgoing))

    lines = 8
    groups = width // (lines * LANES)
    half = tiles // 2
    chunk = (groups, rows * lines, LANES)
    parity = place % 2
    if per:
        keep, send = pl.pallas_call(
            functools.partial(project_kernel, rows=rows, per=per),
            in_specs=[smem, vmem, vmem],
            out_shape=[
                jax.ShapeDtypeStruct((half,) + chunk, jnp.float32),
                jax.ShapeDtypeStruct((half,) + chunk, jnp.bfloat16),
            ],
            scratch_shapes=[
                pltpu.VMEM((tiles * depth, LANES), jnp.float32),
                pltpu.VMEM((groups, tiles * rows * lines, LANES), jnp.float32),
            ],
            compiler_params=params,
        )(parity.reshape(1).astype(jnp.int32), near(incoming), near(weight))
    else:
        feats = incoming[:, :feature_rows].reshape(tiles * rows, share)
        partials = jnp.dot(feats, weight, preferred_element_type=jnp.float32)
        partials = partials.reshape(half, 2, rows, groups, lines, LANES)
        partials = partials.transpose(1, 0, 3, 2, 4, 5).reshape((2, half) + chunk)
        keep = jnp.where(parity == 0, partials[0], partials[1])
        send = jnp.where(parity == 0, partials[1], partials[0]).astype(jnp.bfloat16)
    got = lax.ppermute(send, "rows", [(i, i ^ 1) for i in range(tiles)])
    paired = pl.pallas_call(
        add_kernel,
        in_specs=[vmem, vmem],
        out_shape=jax.ShapeDtypeStruct((half,) + chunk, jnp.bfloat16),
        compiler_params=params,
    )(near(keep), near(got))
    gathered = lax.all_to_all(
        paired,
        "rows",
        split_axis=0,
        concat_axis=0,
        axis_index_groups=[list(range(c, tiles, 2)) for c in range(2)],
        tiled=True,
    )

    section = (place + IMG_SPLIT // 2) % tiles % IMG_SPLIT
    decoded = pl.pallas_call(
        functools.partial(decode_kernel, feature_rows=feature_rows),
        in_specs=[smem, vmem, vmem, vmem, anywhere],
        out_specs=vmem,
        out_shape=jax.ShapeDtypeStruct((TILE_H * IMG_W, channels), jnp.bfloat16),
        compiler_params=params,
    )(section.reshape(1).astype(jnp.int32), near(incoming), near(folded), near(conv_two), near(paired))

    mixed = pl.pallas_call(
        functools.partial(total_kernel, rows=rows),
        in_specs=[vmem],
        out_shape=jax.ShapeDtypeStruct((rows, width), jnp.bfloat16),
        scratch_shapes=[pltpu.VMEM((groups, rows * lines, LANES), jnp.float32)],
        compiler_params=params,
    )(near(gathered))
    return (mixed, decoded.reshape(TILE_H, IMG_W, channels))


def solution(mesh):
    in_specs = (
        P(("groups", "rows"), None),
        P(("groups", "rows"), None),
        P(("groups", "rows"), None),
        P(("groups", "rows"), None, None),
        P(("groups", "rows"), None, None),
        P(("groups", "rows")),
        P("rows", None),
        P(("groups", "rows"), None),
        P(("groups", "rows")),
        P(),
        P(),
        P(),
    )
    out_specs = (P(("groups", "rows"), None), P(("groups", "rows"), None, None))
    return jax.shard_map(
        on_device, mesh=mesh, in_specs=in_specs, out_specs=out_specs, check_vma=False
    )
```

```python
import functools
import math

import jax
import jax.numpy as jnp
from jax import lax
from jax.experimental import pallas as pl
from jax.experimental.pallas import tpu as pltpu
from jax.sharding import PartitionSpec as P

HEAD_DIM = 128
FSQ_DIMS = 5
IMG_SPLIT = 4
TILE_H = 8
IMG_W = 48
LANES = 128
HALO = 2
ROW_WORDS = IMG_W // 2
TILE_ROWS = TILE_H + 2 * HALO
WINDOW = 3
PIECES = 2
CODE_ROWS = WINDOW * PIECES
TAP_ROWS = 24
FOLD_ROWS = 256
VMEM_LIMIT = 24 * 1024 * 1024


def window_start(section):
    return (TILE_H * ROW_WORDS * section - HALO * ROW_WORDS) // LANES


def message_rows(features):
    return -(-(features + CODE_ROWS) // 16) * 16


def encode(code):
    fraction = (code & 127).astype(jnp.float32) * (1.0 / 128.0) + 1.0
    for bit in range(7):
        up = ((code >> (7 + bit)) & 1) == 1
        fraction = jnp.where(up, fraction * 2.0 ** (1 << bit), fraction)
        if bit == 5:
            fraction = fraction * 2.0**-64
    return jnp.where(((code >> 14) & 1) == 1, -fraction, fraction)


def decode_number(value):
    size = jnp.abs(value)
    code = jnp.where(value < 0.0, 1 << 14, 0)
    for bit in range(6, -1, -1):
        step = 1 << bit
        up = size >= 2.0 ** (step - 64)
        code = code + jnp.where(up, step << 7, 0)
        size = jnp.where(up, size * 2.0**-step, size)
    return code + ((size * 2.0**64 - 1.0) * 128.0).astype(jnp.int32)


def attend_kernel(
    lengths,
    slots,
    parity_ref,
    q_any,
    nk_any,
    nv_any,
    k_any,
    v_any,
    codes_any,
    weight_any,
    out_ref,
    give_ref,
    q_ref,
    nk_ref,
    nv_ref,
    k_ref,
    v_ref,
    codes_ref,
    msg,
    sems,
    *,
    tiles,
    per,
    feature_rows,
):
    rows, width = q_ref.shape
    give_columns = give_ref.shape[1]
    small = [
        pltpu.make_async_copy(source, target, sems.at[at])
        for at, (source, target) in enumerate(
            ((q_any, q_ref), (nk_any, nk_ref), (nv_any, nv_ref), (codes_any, codes_ref))
        )
    ]
    keys = [pltpu.make_async_copy(k_any.at[r], k_ref.at[r], sems.at[4 + r]) for r in range(rows)]
    values = [
        pltpu.make_async_copy(v_any.at[r], v_ref.at[r], sems.at[4 + rows + r]) for r in range(rows)
    ]
    begin = pl.multiple_of((1 - parity_ref[0]) * give_columns, LANES)
    give = pltpu.make_async_copy(
        weight_any.at[:, pl.ds(begin, give_columns)], give_ref, sems.at[4 + 2 * rows]
    )
    for copy in small:
        copy.start()
    for r in range(rows):
        keys[r].start()
        values[r].start()
    give.start()

    heads = width // HEAD_DIM
    factor = 1.0 / math.sqrt(HEAD_DIM)
    same = (
        lax.broadcasted_iota(jnp.int32, (heads, width), 1) // HEAD_DIM
        == lax.broadcasted_iota(jnp.int32, (heads, width), 0)
    )
    msg[...] = jnp.zeros_like(msg)
    for copy in small:
        copy.wait()

    words = codes_ref[...]
    blocks = words.shape[1] // LANES
    pieces = [encode(words & 32767), encode(words >> 15)]
    for tile in range(tiles):
        number = (tile + IMG_SPLIT // 2) % tiles
        start = window_start(number % IMG_SPLIT)
        gains = [
            jnp.where(slots[r] == number // IMG_SPLIT, 1.0, 0.0).astype(jnp.float32)
            for r in range(rows)
        ]
        for at, piece in enumerate(pieces):
            for step in range(WINDOW):
                block = start + step
                if block < 0 or block >= blocks:
                    continue
                part = piece[:, block * LANES : (block + 1) * LANES]
                total = part[0:1] * gains[0]
                for r in range(1, rows):
                    total = total + part[r : r + 1] * gains[r]
                place = feature_rows + at * WINDOW + step
                msg[tile, place : place + 1, :] = total

    queries = q_ref[...].astype(jnp.float32)
    new_keys = nk_ref[...].astype(jnp.float32)
    new_values = nv_ref[...].astype(jnp.float32)
    for r in range(rows):
        query, new_key, new_value = (x[r : r + 1] for x in (queries, new_keys, new_values))
        spread = jnp.where(same, query, 0.0).astype(jnp.bfloat16)
        own_score = jnp.sum(jnp.where(same, query * new_key, 0.0), 1, keepdims=True) * factor
        keys[r].wait()
        scores = (
            lax.dot_general(
                spread, k_ref[r], (((1,), (1,)), ((), ())), preferred_element_type=jnp.float32
            )
            * factor
        )
        live = lax.broadcasted_iota(jnp.int32, scores.shape, 1) < lengths[r]
        scores = jnp.where(live, scores, jnp.float32(-1e30))
        highest = jnp.maximum(jnp.max(scores, 1, keepdims=True), own_score)
        cache_exp = jnp.where(live, jnp.exp(scores - highest), 0.0)
        own_exp = jnp.exp(own_score - highest)
        denom = jnp.sum(cache_exp, 1, keepdims=True) + own_exp
        cache_weight = (cache_exp / denom).astype(jnp.bfloat16)
        own_weight = (own_exp / denom).astype(jnp.bfloat16).astype(jnp.float32)
        values[r].wait()
        mixed_in = jnp.dot(cache_weight, v_ref[r], preferred_element_type=jnp.float32)
        attended = jnp.sum(
            jnp.where(same, mixed_in + own_weight * new_value, 0.0), 0, keepdims=True
        )
        for tile in range(tiles):
            for step in range(per):
                begin = (tile // 2 * per + step) * LANES
                place = r * per + step
                msg[tile, place : place + 1, :] = attended[:, begin : begin + LANES]
    out_ref[...] = msg[...].astype(jnp.bfloat16)
    give.wait()


def project_kernel(parity_ref, in_ref, own_ref, other_ref, out_ref, held, total, *, rows, per):
    tiles, depth = in_ref.shape[:2]
    held[...] = in_ref[...].astype(jnp.float32).reshape(held.shape)
    groups = total.shape[0]
    lines = out_ref.shape[2] // rows
    share = own_ref.shape[0]
    lhs = []
    for row in range(rows):
        parts = [held[pl.ds(row * per + j, tiles, stride=depth), :] for j in range(per)]
        lhs.append(jnp.concatenate(parts, 1))
    lhs = jnp.concatenate(lhs, 0)
    even = parity_ref[0] == 0
    first, second = lhs[:, :share], lhs[:, share:]
    own = jnp.where(even, first, second).astype(jnp.bfloat16)
    other = jnp.where(even, second, first).astype(jnp.bfloat16)
    product = jnp.dot(own, own_ref[...], preferred_element_type=jnp.float32) + jnp.dot(
        other, other_ref[...], preferred_element_type=jnp.float32
    )
    for row in range(rows):
        for group in range(groups):
            for line in range(lines):
                begin = (group * lines + line) * LANES
                total[group, pl.ds(row * lines + line, tiles, stride=rows * lines), :] = product[
                    row * tiles : (row + 1) * tiles, begin : begin + LANES
                ]
    for group in range(groups):
        out_ref[:, group] = (
            total[group].astype(jnp.bfloat16).reshape(tiles, rows * lines, LANES)
        )


def total_kernel(in_ref, out_ref, held, *, rows):
    tiles, groups, depth, _ = in_ref.shape
    lines = depth // rows
    parts = in_ref[...].astype(jnp.float32).reshape(tiles // 2, 2 * groups, depth, LANES)
    held[...] = jnp.sum(parts, 0)
    for group in range(2 * groups):
        for line in range(lines):
            begin = (group * lines + line) * LANES
            out_ref[:, begin : begin + LANES] = held[
                group, pl.ds(line, rows, stride=lines), :
            ].astype(jnp.bfloat16)


def split_three(whole):
    high = whole.astype(jnp.bfloat16).astype(jnp.float32)
    middle = (whole - high).astype(jnp.bfloat16).astype(jnp.float32)
    return jnp.concatenate([high, middle, whole - high - middle], 0)


def fold_kernel(
    parity_ref, cw_ref, conv_ref, weight_ref, after_ref, out_ref, near_ref, levels_w, folded, held, sems, near_sem
):
    del after_ref
    taps = [(dr, dc) for dr in range(3) for dc in range(3)]
    copies = [
        pltpu.make_async_copy(conv_ref.at[dr, dc], held.at[at], sems.at[at])
        for at, (dr, dc) in enumerate(taps)
    ]
    for copy in copies:
        copy.start()
    begin = pl.multiple_of(parity_ref[0] * near_ref.shape[1], LANES)
    bring = pltpu.make_async_copy(
        weight_ref.at[:, pl.ds(begin, near_ref.shape[1])], near_ref, near_sem
    )
    bring.start()
    levels_w[...] = jnp.zeros_like(levels_w)
    levels_w[0:FSQ_DIMS, :] = cw_ref[...]
    left = split_three(levels_w[...]).astype(jnp.bfloat16)
    folded[...] = jnp.zeros_like(folded)
    for at, copy in enumerate(copies):
        copy.wait()
        parts = jnp.dot(left, held[at], preferred_element_type=jnp.float32)
        total = parts[0:8] + parts[8:16] + parts[16:24]
        folded[at * TAP_ROWS : (at + 1) * TAP_ROWS, :] = split_three(total)
    out_ref[...] = folded[...].astype(jnp.bfloat16)
    bring.wait()


def decode_kernel(section_ref, in_ref, fold_ref, two_ref, after_ref, out_ref, *, feature_rows):
    del after_ref
    section = section_ref[0]
    got = jnp.sum(in_ref[...].astype(jnp.float32), 0)
    pieces = []
    for at in range(PIECES):
        lines = [
            got[feature_rows + at * WINDOW + step : feature_rows + at * WINDOW + step + 1]
            for step in range(WINDOW)
        ]
        pieces.append(jnp.concatenate(lines, 1))
    codes = decode_number(jnp.concatenate(pieces, 1))
    span = codes.shape[1]
    depth = fold_ref.shape[0]
    level = lax.broadcasted_iota(jnp.int32, (8, span), 0)
    taken = level < FSQ_DIMS
    shift = jnp.where(taken, level * 3, 0)
    value = (2 * ((jnp.broadcast_to(codes, (8, span)) >> shift) & 7) - 7).astype(
        jnp.float32
    ) * 0.125
    value = jnp.where(taken, value, 0.0)
    value = jnp.concatenate([value] * (depth // 8), 0).astype(jnp.bfloat16)

    count = TILE_ROWS * IMG_W
    begin = TILE_H * ROW_WORDS * section - HALO * ROW_WORDS
    offset = begin & (LANES - 1)
    spot = lax.broadcasted_iota(jnp.int32, (count, 1), 0)
    line = spot // IMG_W + TILE_H * section - HALO
    inside = (line >= 0) & (line < IMG_SPLIT * TILE_H)
    target = jnp.where(inside, (spot >> 1) + offset + (span // 2) * (spot & 1), -1)
    chooser = jnp.where(
        lax.broadcasted_iota(jnp.int32, (count, span), 1) == target, 1.0, 0.0
    ).astype(jnp.bfloat16)
    placed = lax.dot_general(
        chooser, value, (((1,), (1,)), ((), ())), preferred_element_type=jnp.float32
    )
    column = spot % IMG_W
    moved = [
        jnp.where(column == 0, 0.0, pltpu.roll(placed, 1, 0)),
        placed,
        jnp.where(column == IMG_W - 1, 0.0, pltpu.roll(placed, count - 1, 0)),
    ]
    count = count - 2 * IMG_W
    tap_of = lax.broadcasted_iota(jnp.int32, (1, depth), 1) // TAP_ROWS
    taps = jnp.zeros((count, depth), jnp.float32)
    for dr in range(3):
        for dc in range(3):
            taps = jnp.where(
                tap_of == 3 * dr + dc, moved[dc][dr * IMG_W : dr * IMG_W + count], taps
            )
    hidden = jnp.dot(taps.astype(jnp.bfloat16), fold_ref[...], preferred_element_type=jnp.float32)

    line = lax.broadcasted_iota(jnp.int32, (count, 1), 0) // IMG_W + TILE_H * section - 1
    inside = (line >= 0) & (line < IMG_SPLIT * TILE_H)
    activated = jnp.where(inside, hidden * jax.nn.sigmoid(hidden), 0.0).astype(jnp.bfloat16)

    count = count - 2 * IMG_W
    column = lax.broadcasted_iota(jnp.int32, (count, 1), 0) % IMG_W
    summed = None
    for dc in (1, 0, 2):
        part = None
        for dr in range(3):
            term = jnp.dot(
                activated[dr * IMG_W : dr * IMG_W + count],
                two_ref[dr, dc],
                preferred_element_type=jnp.float32,
            )
            part = term if part is None else part + term
        if dc == 0:
            part = jnp.where(column == 0, 0.0, pltpu.roll(part, 1, 0))
        if dc == 2:
            part = jnp.where(column == IMG_W - 1, 0.0, pltpu.roll(part, count - 1, 0))
        summed = part if summed is None else summed + part
    out_ref[...] = summed.astype(jnp.bfloat16)


def near(array):
    return pltpu.with_memory_space_constraint(array, pltpu.VMEM)


def far(array):
    return pltpu.with_memory_space_constraint(array, pltpu.HBM)


def on_device(
    queries,
    new_keys,
    new_values,
    cache_keys,
    cache_values,
    cache_lengths,
    out_weight,
    codes,
    tile_slot,
    code_weight,
    conv_one,
    conv_two,
):
    tiles = lax.axis_size("rows")
    place = lax.axis_index("rows")
    rows, width = queries.shape
    channels = code_weight.shape[1]
    share = width // tiles
    per = 2 * share // LANES
    feature_rows = rows * per
    depth = message_rows(feature_rows)
    half = width // 2
    lines = 8
    groups = half // (lines * LANES)
    params = pltpu.CompilerParams(vmem_limit_bytes=VMEM_LIMIT)
    smem = pl.BlockSpec(memory_space=pltpu.SMEM)
    vmem = pl.BlockSpec(memory_space=pltpu.VMEM)
    anywhere = pl.BlockSpec(memory_space=pl.ANY)
    parity = (place % 2).reshape(1).astype(jnp.int32)

    outgoing, give = pl.pallas_call(
        functools.partial(attend_kernel, tiles=tiles, per=per, feature_rows=feature_rows),
        in_specs=[smem] * 3 + [anywhere] * 7,
        out_specs=[vmem, vmem],
        out_shape=[
            pltpu.VMEM((tiles, depth, LANES), jnp.bfloat16),
            pltpu.VMEM((share, half), out_weight.dtype),
        ],
        scratch_shapes=[
            pltpu.VMEM(queries.shape, queries.dtype),
            pltpu.VMEM(new_keys.shape, new_keys.dtype),
            pltpu.VMEM(new_values.shape, new_values.dtype),
            pltpu.VMEM(cache_keys.shape, cache_keys.dtype),
            pltpu.VMEM(cache_values.shape, cache_values.dtype),
            pltpu.VMEM(codes.shape, codes.dtype),
            pltpu.VMEM((tiles, depth, LANES), jnp.float32),
            pltpu.SemaphoreType.DMA((5 + 2 * rows,)),
        ],
        compiler_params=pltpu.CompilerParams(vmem_limit_bytes=56 * 1024 * 1024),
    )(
        cache_lengths,
        tile_slot,
        parity,
        far(queries),
        far(new_keys),
        far(new_values),
        far(cache_keys),
        far(cache_values),
        far(codes),
        far(out_weight),
    )
    incoming = lax.all_to_all(outgoing, "rows", split_axis=0, concat_axis=0, tiled=True)
    other = lax.ppermute(give, "rows", [(i, i ^ 1) for i in range(tiles)])

    folded, own = pl.pallas_call(
        fold_kernel,
        in_specs=[smem, vmem, anywhere, anywhere, anywhere],
        out_specs=[vmem, vmem],
        out_shape=[
            jax.ShapeDtypeStruct((FOLD_ROWS, channels), jnp.bfloat16),
            pltpu.VMEM((share, half), out_weight.dtype),
        ],
        scratch_shapes=[
            pltpu.VMEM((8, channels), jnp.float32),
            pltpu.VMEM((FOLD_ROWS, channels), jnp.float32),
            pltpu.VMEM((9,) + conv_one.shape[2:], conv_one.dtype),
            pltpu.SemaphoreType.DMA((9,)),
            pltpu.SemaphoreType.DMA,
        ],
        compiler_params=params,
    )(parity, far(code_weight), far(conv_one), far(out_weight), near(outgoing))

    partials = pl.pallas_call(
        functools.partial(project_kernel, rows=rows, per=per),
        in_specs=[smem, vmem, vmem, vmem],
        out_shape=pltpu.VMEM((tiles, groups, rows * lines, LANES), jnp.bfloat16),
        scratch_shapes=[
            pltpu.VMEM((tiles * depth, LANES), jnp.float32),
            pltpu.VMEM((groups, tiles * rows * lines, LANES), jnp.float32),
        ],
        compiler_params=params,
    )(parity, near(incoming), near(own), near(other))
    gathered = lax.all_to_all(partials, "rows", split_axis=0, concat_axis=0, tiled=True)

    section = (place + IMG_SPLIT // 2) % tiles % IMG_SPLIT
    decoded = pl.pallas_call(
        functools.partial(decode_kernel, feature_rows=feature_rows),
        in_specs=[smem, vmem, vmem, vmem, anywhere],
        out_specs=vmem,
        out_shape=jax.ShapeDtypeStruct((TILE_H * IMG_W, channels), jnp.bfloat16),
        compiler_params=params,
    )(section.reshape(1).astype(jnp.int32), near(incoming), near(folded), near(conv_two), near(partials))

    mixed = pl.pallas_call(
        functools.partial(total_kernel, rows=rows),
        in_specs=[vmem],
        out_shape=jax.ShapeDtypeStruct((rows, width), jnp.bfloat16),
        scratch_shapes=[pltpu.VMEM((2 * groups, rows * lines, LANES), jnp.float32)],
        compiler_params=params,
    )(near(gathered))
    return (mixed, decoded.reshape(TILE_H, IMG_W, channels))


def solution(mesh):
    in_specs = (
        P(("groups", "rows"), None),
        P(("groups", "rows"), None),
        P(("groups", "rows"), None),
        P(("groups", "rows"), None, None),
        P(("groups", "rows"), None, None),
        P(("groups", "rows")),
        P("rows", None),
        P(("groups", "rows"), None),
        P(("groups", "rows")),
        P(),
        P(),
        P(),
    )
    out_specs = (P(("groups", "rows"), None), P(("groups", "rows"), None, None))
    return jax.shard_map(
        on_device, mesh=mesh, in_specs=in_specs, out_specs=out_specs, check_vma=False
    )
```

```python
import functools
import math

import jax
import jax.numpy as jnp
from jax import lax
from jax.experimental import pallas as pl
from jax.experimental.pallas import tpu as pltpu
from jax.sharding import PartitionSpec as P

HEAD_DIM = 128
FSQ_DIMS = 5
IMG_SPLIT = 4
TILE_H = 8
IMG_W = 48
LANES = 128
HALO = 2
ROW_WORDS = IMG_W // 2
TILE_ROWS = TILE_H + 2 * HALO
WINDOW = 3
PIECES = 2
CODE_ROWS = WINDOW * PIECES
TAP_ROWS = 24
FOLD_ROWS = 256
VMEM_LIMIT = 24 * 1024 * 1024


def window_start(section):
    return (TILE_H * ROW_WORDS * section - HALO * ROW_WORDS) // LANES


def member(at, tiles):
    return (at + tiles // 4 * 2) % tiles


def message_rows(features):
    return -(-(features + CODE_ROWS) // 16) * 16


def encode(code):
    fraction = (code & 127).astype(jnp.float32) * (1.0 / 128.0) + 1.0
    for bit in range(7):
        up = ((code >> (7 + bit)) & 1) == 1
        fraction = jnp.where(up, fraction * 2.0 ** (1 << bit), fraction)
        if bit == 5:
            fraction = fraction * 2.0**-64
    return jnp.where(((code >> 14) & 1) == 1, -fraction, fraction)


def decode_number(value):
    size = jnp.abs(value)
    code = jnp.where(value < 0.0, 1 << 14, 0)
    for bit in range(6, -1, -1):
        step = 1 << bit
        up = size >= 2.0 ** (step - 64)
        code = code + jnp.where(up, step << 7, 0)
        size = jnp.where(up, size * 2.0**-step, size)
    return code + ((size * 2.0**64 - 1.0) * 128.0).astype(jnp.int32)


def attend_kernel(
    lengths,
    slots,
    parity_ref,
    q_any,
    nk_any,
    nv_any,
    k_any,
    v_any,
    codes_any,
    weight_any,
    out_ref,
    give_ref,
    q_ref,
    nk_ref,
    nv_ref,
    k_ref,
    v_ref,
    codes_ref,
    msg,
    sems,
    *,
    tiles,
    per,
    feature_rows,
):
    rows, width = q_ref.shape
    give_columns = give_ref.shape[1]
    small = [
        pltpu.make_async_copy(source, target, sems.at[at])
        for at, (source, target) in enumerate(
            ((q_any, q_ref), (nk_any, nk_ref), (nv_any, nv_ref), (codes_any, codes_ref))
        )
    ]
    keys = [pltpu.make_async_copy(k_any.at[r], k_ref.at[r], sems.at[4 + r]) for r in range(rows)]
    values = [
        pltpu.make_async_copy(v_any.at[r], v_ref.at[r], sems.at[4 + rows + r]) for r in range(rows)
    ]
    begin = pl.multiple_of((1 - parity_ref[0]) * give_columns, LANES)
    give = pltpu.make_async_copy(
        weight_any.at[:, pl.ds(begin, give_columns)], give_ref, sems.at[4 + 2 * rows]
    )
    for copy in small:
        copy.start()
    for r in range(rows):
        keys[r].start()
        values[r].start()
    give.start()

    heads = width // HEAD_DIM
    factor = 1.0 / math.sqrt(HEAD_DIM)
    same = (
        lax.broadcasted_iota(jnp.int32, (heads, width), 1) // HEAD_DIM
        == lax.broadcasted_iota(jnp.int32, (heads, width), 0)
    )
    msg[...] = jnp.zeros_like(msg)
    for copy in small:
        copy.wait()

    words = codes_ref[...]
    blocks = words.shape[1] // LANES
    pieces = [encode(words & 32767), encode(words >> 15)]
    for tile in range(tiles):
        number = (member(tile, tiles) + IMG_SPLIT // 2) % tiles
        start = window_start(number % IMG_SPLIT)
        gains = [
            jnp.where(slots[r] == number // IMG_SPLIT, 1.0, 0.0).astype(jnp.float32)
            for r in range(rows)
        ]
        for at, piece in enumerate(pieces):
            for step in range(WINDOW):
                block = start + step
                if block < 0 or block >= blocks:
                    continue
                part = piece[:, block * LANES : (block + 1) * LANES]
                total = part[0:1] * gains[0]
                for r in range(1, rows):
                    total = total + part[r : r + 1] * gains[r]
                place = feature_rows + at * WINDOW + step
                msg[tile, place : place + 1, :] = total

    queries = q_ref[...].astype(jnp.float32)
    new_keys = nk_ref[...].astype(jnp.float32)
    new_values = nv_ref[...].astype(jnp.float32)
    for r in range(rows):
        query, new_key, new_value = (x[r : r + 1] for x in (queries, new_keys, new_values))
        spread = jnp.where(same, query, 0.0).astype(jnp.bfloat16)
        own_score = jnp.sum(jnp.where(same, query * new_key, 0.0), 1, keepdims=True) * factor
        keys[r].wait()
        scores = (
            lax.dot_general(
                spread, k_ref[r], (((1,), (1,)), ((), ())), preferred_element_type=jnp.float32
            )
            * factor
        )
        live = lax.broadcasted_iota(jnp.int32, scores.shape, 1) < lengths[r]
        scores = jnp.where(live, scores, jnp.float32(-1e30))
        highest = jnp.maximum(jnp.max(scores, 1, keepdims=True), own_score)
        cache_exp = jnp.where(live, jnp.exp(scores - highest), 0.0)
        own_exp = jnp.exp(own_score - highest)
        denom = jnp.sum(cache_exp, 1, keepdims=True) + own_exp
        cache_weight = (cache_exp / denom).astype(jnp.bfloat16)
        own_weight = (own_exp / denom).astype(jnp.bfloat16).astype(jnp.float32)
        values[r].wait()
        mixed_in = jnp.dot(cache_weight, v_ref[r], preferred_element_type=jnp.float32)
        attended = jnp.sum(
            jnp.where(same, mixed_in + own_weight * new_value, 0.0), 0, keepdims=True
        )
        for tile in range(tiles):
            for step in range(per):
                begin = (member(tile, tiles) // 2 * per + step) * LANES
                place = r * per + step
                msg[tile, place : place + 1, :] = attended[:, begin : begin + LANES]
    out_ref[...] = msg[...].astype(jnp.bfloat16)
    give.wait()


def project_kernel(parity_ref, in_ref, own_ref, other_ref, out_ref, held, total, *, rows, per):
    tiles, depth = in_ref.shape[:2]
    held[...] = in_ref[...].astype(jnp.float32).reshape(held.shape)
    groups = total.shape[0]
    lines = out_ref.shape[2] // rows
    share = own_ref.shape[0]
    lhs = []
    for row in range(rows):
        parts = [held[pl.ds(row * per + j, tiles, stride=depth), :] for j in range(per)]
        lhs.append(jnp.concatenate(parts, 1))
    lhs = jnp.concatenate(lhs, 0)
    even = parity_ref[0] == 0
    first, second = lhs[:, :share], lhs[:, share:]
    own = jnp.where(even, first, second).astype(jnp.bfloat16)
    other = jnp.where(even, second, first).astype(jnp.bfloat16)
    product = jnp.dot(own, own_ref[...], preferred_element_type=jnp.float32) + jnp.dot(
        other, other_ref[...], preferred_element_type=jnp.float32
    )
    for row in range(rows):
        for group in range(groups):
            for line in range(lines):
                begin = (group * lines + line) * LANES
                total[group, pl.ds(row * lines + line, tiles, stride=rows * lines), :] = product[
                    row * tiles : (row + 1) * tiles, begin : begin + LANES
                ]
    for group in range(groups):
        out_ref[:, group] = (
            total[group].astype(jnp.bfloat16).reshape(tiles, rows * lines, LANES)
        )


def total_kernel(in_ref, out_ref, held, *, rows):
    tiles, groups, depth, _ = in_ref.shape
    lines = depth // rows
    parts = in_ref[...].astype(jnp.float32).reshape(tiles // 2, 2 * groups, depth, LANES)
    held[...] = jnp.sum(parts, 0)
    for group in range(2 * groups):
        for line in range(lines):
            begin = (group * lines + line) * LANES
            out_ref[:, begin : begin + LANES] = held[
                group, pl.ds(line, rows, stride=lines), :
            ].astype(jnp.bfloat16)


def split_three(whole):
    high = whole.astype(jnp.bfloat16).astype(jnp.float32)
    middle = (whole - high).astype(jnp.bfloat16).astype(jnp.float32)
    return jnp.concatenate([high, middle, whole - high - middle], 0)


def fold_kernel(
    parity_ref, cw_ref, conv_ref, weight_ref, after_ref, out_ref, near_ref, levels_w, folded, held, sems, near_sem
):
    del after_ref
    taps = [(dr, dc) for dr in range(3) for dc in range(3)]
    copies = [
        pltpu.make_async_copy(conv_ref.at[dr, dc], held.at[at], sems.at[at])
        for at, (dr, dc) in enumerate(taps)
    ]
    for copy in copies:
        copy.start()
    begin = pl.multiple_of(parity_ref[0] * near_ref.shape[1], LANES)
    bring = pltpu.make_async_copy(
        weight_ref.at[:, pl.ds(begin, near_ref.shape[1])], near_ref, near_sem
    )
    bring.start()
    levels_w[...] = jnp.zeros_like(levels_w)
    levels_w[0:FSQ_DIMS, :] = cw_ref[...]
    left = split_three(levels_w[...]).astype(jnp.bfloat16)
    folded[...] = jnp.zeros_like(folded)
    for at, copy in enumerate(copies):
        copy.wait()
        parts = jnp.dot(left, held[at], preferred_element_type=jnp.float32)
        total = parts[0:8] + parts[8:16] + parts[16:24]
        folded[at * TAP_ROWS : (at + 1) * TAP_ROWS, :] = split_three(total)
    out_ref[...] = folded[...].astype(jnp.bfloat16)
    bring.wait()


def decode_kernel(section_ref, in_ref, fold_ref, two_ref, after_ref, out_ref, *, feature_rows):
    del after_ref
    section = section_ref[0]
    got = jnp.sum(in_ref[...].astype(jnp.float32), 0)
    pieces = []
    for at in range(PIECES):
        lines = [
            got[feature_rows + at * WINDOW + step : feature_rows + at * WINDOW + step + 1]
            for step in range(WINDOW)
        ]
        pieces.append(jnp.concatenate(lines, 1))
    codes = decode_number(jnp.concatenate(pieces, 1))
    span = codes.shape[1]
    depth = fold_ref.shape[0]
    level = lax.broadcasted_iota(jnp.int32, (8, span), 0)
    taken = level < FSQ_DIMS
    shift = jnp.where(taken, level * 3, 0)
    value = (2 * ((jnp.broadcast_to(codes, (8, span)) >> shift) & 7) - 7).astype(
        jnp.float32
    ) * 0.125
    value = jnp.where(taken, value, 0.0)
    value = jnp.concatenate([value] * (depth // 8), 0).astype(jnp.bfloat16)

    count = TILE_ROWS * IMG_W
    begin = TILE_H * ROW_WORDS * section - HALO * ROW_WORDS
    offset = begin & (LANES - 1)
    spot = lax.broadcasted_iota(jnp.int32, (count, 1), 0)
    line = spot // IMG_W + TILE_H * section - HALO
    inside = (line >= 0) & (line < IMG_SPLIT * TILE_H)
    target = jnp.where(inside, (spot >> 1) + offset + (span // 2) * (spot & 1), -1)
    chooser = jnp.where(
        lax.broadcasted_iota(jnp.int32, (count, span), 1) == target, 1.0, 0.0
    ).astype(jnp.bfloat16)
    placed = lax.dot_general(
        chooser, value, (((1,), (1,)), ((), ())), preferred_element_type=jnp.float32
    )
    column = spot % IMG_W
    moved = [
        jnp.where(column == 0, 0.0, pltpu.roll(placed, 1, 0)),
        placed,
        jnp.where(column == IMG_W - 1, 0.0, pltpu.roll(placed, count - 1, 0)),
    ]
    count = count - 2 * IMG_W
    tap_of = lax.broadcasted_iota(jnp.int32, (1, depth), 1) // TAP_ROWS
    taps = jnp.zeros((count, depth), jnp.float32)
    for dr in range(3):
        for dc in range(3):
            taps = jnp.where(
                tap_of == 3 * dr + dc, moved[dc][dr * IMG_W : dr * IMG_W + count], taps
            )
    hidden = jnp.dot(taps.astype(jnp.bfloat16), fold_ref[...], preferred_element_type=jnp.float32)

    line = lax.broadcasted_iota(jnp.int32, (count, 1), 0) // IMG_W + TILE_H * section - 1
    inside = (line >= 0) & (line < IMG_SPLIT * TILE_H)
    activated = jnp.where(inside, hidden * jax.nn.sigmoid(hidden), 0.0).astype(jnp.bfloat16)

    count = count - 2 * IMG_W
    column = lax.broadcasted_iota(jnp.int32, (count, 1), 0) % IMG_W
    summed = None
    for dc in (1, 0, 2):
        part = None
        for dr in range(3):
            term = jnp.dot(
                activated[dr * IMG_W : dr * IMG_W + count],
                two_ref[dr, dc],
                preferred_element_type=jnp.float32,
            )
            part = term if part is None else part + term
        if dc == 0:
            part = jnp.where(column == 0, 0.0, pltpu.roll(part, 1, 0))
        if dc == 2:
            part = jnp.where(column == IMG_W - 1, 0.0, pltpu.roll(part, count - 1, 0))
        summed = part if summed is None else summed + part
    out_ref[...] = summed.astype(jnp.bfloat16)


def near(array):
    return pltpu.with_memory_space_constraint(array, pltpu.VMEM)


def far(array):
    return pltpu.with_memory_space_constraint(array, pltpu.HBM)


def on_device(
    queries,
    new_keys,
    new_values,
    cache_keys,
    cache_values,
    cache_lengths,
    out_weight,
    codes,
    tile_slot,
    code_weight,
    conv_one,
    conv_two,
):
    tiles = lax.axis_size("rows")
    place = lax.axis_index("rows")
    rows, width = queries.shape
    channels = code_weight.shape[1]
    share = width // tiles
    per = 2 * share // LANES
    feature_rows = rows * per
    depth = message_rows(feature_rows)
    half = width // 2
    lines = 8
    groups = half // (lines * LANES)
    params = pltpu.CompilerParams(vmem_limit_bytes=VMEM_LIMIT)
    smem = pl.BlockSpec(memory_space=pltpu.SMEM)
    vmem = pl.BlockSpec(memory_space=pltpu.VMEM)
    anywhere = pl.BlockSpec(memory_space=pl.ANY)
    parity = (place % 2).reshape(1).astype(jnp.int32)

    outgoing, give = pl.pallas_call(
        functools.partial(attend_kernel, tiles=tiles, per=per, feature_rows=feature_rows),
        in_specs=[smem] * 3 + [anywhere] * 7,
        out_specs=[vmem, vmem],
        out_shape=[
            pltpu.VMEM((tiles, depth, LANES), jnp.bfloat16),
            pltpu.VMEM((share, half), out_weight.dtype),
        ],
        scratch_shapes=[
            pltpu.VMEM(queries.shape, queries.dtype),
            pltpu.VMEM(new_keys.shape, new_keys.dtype),
            pltpu.VMEM(new_values.shape, new_values.dtype),
            pltpu.VMEM(cache_keys.shape, cache_keys.dtype),
            pltpu.VMEM(cache_values.shape, cache_values.dtype),
            pltpu.VMEM(codes.shape, codes.dtype),
            pltpu.VMEM((tiles, depth, LANES), jnp.float32),
            pltpu.SemaphoreType.DMA((5 + 2 * rows,)),
        ],
        compiler_params=pltpu.CompilerParams(vmem_limit_bytes=56 * 1024 * 1024),
    )(
        cache_lengths,
        tile_slot,
        parity,
        far(queries),
        far(new_keys),
        far(new_values),
        far(cache_keys),
        far(cache_values),
        far(codes),
        far(out_weight),
    )
    order = [[member(at, tiles) for at in range(tiles)]]
    incoming = lax.all_to_all(
        outgoing, "rows", split_axis=0, concat_axis=0, axis_index_groups=order, tiled=True
    )
    other = lax.ppermute(give, "rows", [(i, i ^ 1) for i in range(tiles)])

    folded, own = pl.pallas_call(
        fold_kernel,
        in_specs=[smem, vmem, anywhere, anywhere, anywhere],
        out_specs=[vmem, vmem],
        out_shape=[
            jax.ShapeDtypeStruct((FOLD_ROWS, channels), jnp.bfloat16),
            pltpu.VMEM((share, half), out_weight.dtype),
        ],
        scratch_shapes=[
            pltpu.VMEM((8, channels), jnp.float32),
            pltpu.VMEM((FOLD_ROWS, channels), jnp.float32),
            pltpu.VMEM((9,) + conv_one.shape[2:], conv_one.dtype),
            pltpu.SemaphoreType.DMA((9,)),
            pltpu.SemaphoreType.DMA,
        ],
        compiler_params=params,
    )(parity, far(code_weight), far(conv_one), far(out_weight), near(outgoing))

    partials = pl.pallas_call(
        functools.partial(project_kernel, rows=rows, per=per),
        in_specs=[smem, vmem, vmem, vmem],
        out_shape=pltpu.VMEM((tiles, groups, rows * lines, LANES), jnp.bfloat16),
        scratch_shapes=[
            pltpu.VMEM((tiles * depth, LANES), jnp.float32),
            pltpu.VMEM((groups, tiles * rows * lines, LANES), jnp.float32),
        ],
        compiler_params=params,
    )(parity, near(incoming), near(own), near(other))
    gathered = lax.all_to_all(
        partials, "rows", split_axis=0, concat_axis=0, axis_index_groups=order, tiled=True
    )

    section = (place + IMG_SPLIT // 2) % tiles % IMG_SPLIT
    decoded = pl.pallas_call(
        functools.partial(decode_kernel, feature_rows=feature_rows),
        in_specs=[smem, vmem, vmem, vmem, anywhere],
        out_specs=vmem,
        out_shape=jax.ShapeDtypeStruct((TILE_H * IMG_W, channels), jnp.bfloat16),
        compiler_params=params,
    )(section.reshape(1).astype(jnp.int32), near(incoming), near(folded), near(conv_two), near(partials))

    mixed = pl.pallas_call(
        functools.partial(total_kernel, rows=rows),
        in_specs=[vmem],
        out_shape=jax.ShapeDtypeStruct((rows, width), jnp.bfloat16),
        scratch_shapes=[pltpu.VMEM((2 * groups, rows * lines, LANES), jnp.float32)],
        compiler_params=params,
    )(near(gathered))
    return (mixed, decoded.reshape(TILE_H, IMG_W, channels))


def solution(mesh):
    in_specs = (
        P(("groups", "rows"), None),
        P(("groups", "rows"), None),
        P(("groups", "rows"), None),
        P(("groups", "rows"), None, None),
        P(("groups", "rows"), None, None),
        P(("groups", "rows")),
        P("rows", None),
        P(("groups", "rows"), None),
        P(("groups", "rows")),
        P(),
        P(),
        P(),
    )
    out_specs = (P(("groups", "rows"), None), P(("groups", "rows"), None, None))
    return jax.shard_map(
        on_device, mesh=mesh, in_specs=in_specs, out_specs=out_specs, check_vma=False
    )
```

```python
import functools
import math

import jax
import jax.numpy as jnp
from jax import lax
from jax.experimental import pallas as pl
from jax.experimental.pallas import tpu as pltpu
from jax.sharding import PartitionSpec as P

HEAD_DIM = 128
FSQ_DIMS = 5
IMG_SPLIT = 4
TILE_H = 8
IMG_W = 48
LANES = 128
HALO = 2
ROW_WORDS = IMG_W // 2
TILE_ROWS = TILE_H + 2 * HALO
WINDOW = 3
PIECES = 2
CODE_ROWS = WINDOW * PIECES
TAP_ROWS = 24
FOLD_ROWS = 256
VMEM_LIMIT = 24 * 1024 * 1024


def window_start(section):
    return (TILE_H * ROW_WORDS * section - HALO * ROW_WORDS) // LANES


def member(at, tiles):
    return (at + tiles // 4 * 2) % tiles


def message_rows(features):
    return -(-(features + CODE_ROWS) // 16) * 16


def encode(code):
    fraction = (code & 127).astype(jnp.float32) * (1.0 / 128.0) + 1.0
    for bit in range(7):
        up = ((code >> (7 + bit)) & 1) == 1
        fraction = jnp.where(up, fraction * 2.0 ** (1 << bit), fraction)
        if bit == 5:
            fraction = fraction * 2.0**-64
    return jnp.where(((code >> 14) & 1) == 1, -fraction, fraction)


def decode_number(value):
    size = jnp.abs(value)
    code = jnp.where(value < 0.0, 1 << 14, 0)
    for bit in range(6, -1, -1):
        step = 1 << bit
        up = size >= 2.0 ** (step - 64)
        code = code + jnp.where(up, step << 7, 0)
        size = jnp.where(up, size * 2.0**-step, size)
    return code + ((size * 2.0**64 - 1.0) * 128.0).astype(jnp.int32)


def attend_kernel(
    lengths,
    slots,
    parity_ref,
    q_any,
    nk_any,
    nv_any,
    k_any,
    v_any,
    codes_any,
    weight_any,
    out_ref,
    give_ref,
    q_ref,
    nk_ref,
    nv_ref,
    k_ref,
    v_ref,
    codes_ref,
    msg,
    sems,
    *,
    tiles,
    per,
    feature_rows,
):
    rows, width = q_ref.shape
    give_columns = give_ref.shape[1]
    small = [
        pltpu.make_async_copy(source, target, sems.at[at])
        for at, (source, target) in enumerate(
            ((q_any, q_ref), (nk_any, nk_ref), (nv_any, nv_ref), (codes_any, codes_ref))
        )
    ]
    cached = k_any.shape[1]
    keys, values = (
        [
            pltpu.make_async_copy(
                source.at[r], target.at[pl.ds(r * cached, cached)], sems.at[base + r]
            )
            for r in range(rows)
        ]
        for source, target, base in ((k_any, k_ref, 4), (v_any, v_ref, 4 + rows))
    )
    begin = pl.multiple_of((1 - parity_ref[0]) * give_columns, LANES)
    give = pltpu.make_async_copy(
        weight_any.at[:, pl.ds(begin, give_columns)], give_ref, sems.at[4 + 2 * rows]
    )
    for copy in small:
        copy.start()
    for copy in keys + values:
        copy.start()

    heads = width // HEAD_DIM
    factor = 1.0 / math.sqrt(HEAD_DIM)
    same = (
        lax.broadcasted_iota(jnp.int32, (heads, width), 1) // HEAD_DIM
        == lax.broadcasted_iota(jnp.int32, (heads, width), 0)
    )
    msg[...] = jnp.zeros_like(msg)
    for copy in small:
        copy.wait()

    words = codes_ref[...]
    blocks = words.shape[1] // LANES
    pieces = [encode(words & 32767), encode(words >> 15)]
    for tile in range(tiles):
        number = (member(tile, tiles) + IMG_SPLIT // 2) % tiles
        start = window_start(number % IMG_SPLIT)
        gains = [
            jnp.where(slots[r] == number // IMG_SPLIT, 1.0, 0.0).astype(jnp.float32)
            for r in range(rows)
        ]
        for at, piece in enumerate(pieces):
            for step in range(WINDOW):
                block = start + step
                if block < 0 or block >= blocks:
                    continue
                part = piece[:, block * LANES : (block + 1) * LANES]
                total = part[0:1] * gains[0]
                for r in range(1, rows):
                    total = total + part[r : r + 1] * gains[r]
                place = feature_rows + at * WINDOW + step
                msg[tile, place : place + 1, :] = total

    padding = jnp.zeros((16 - rows, width), jnp.float32)
    new_keys = jnp.concatenate([nk_ref[...].astype(jnp.float32), padding], 0).astype(jnp.bfloat16)
    new_values = jnp.concatenate([nv_ref[...].astype(jnp.float32), padding], 0).astype(jnp.bfloat16)
    queries = q_ref[...].astype(jnp.float32)
    spread = jnp.concatenate(
        [jnp.where(same, queries[r : r + 1], 0.0) for r in range(rows)], 0
    ).astype(jnp.bfloat16)

    def products(cached):
        return (
            lax.dot_general(
                spread, cached, (((1,), (1,)), ((), ())), preferred_element_type=jnp.float32
            )
            * factor
        )

    def owner(shape):
        return lax.broadcasted_iota(jnp.int32, shape, 0) // heads

    own_scores = products(new_keys)
    own_at = owner(own_scores.shape) == lax.broadcasted_iota(jnp.int32, own_scores.shape, 1)
    own_score = jnp.sum(jnp.where(own_at, own_scores, 0.0), 1, keepdims=True)
    for copy in keys:
        copy.wait()
    scores = products(k_ref[...])
    cache = scores.shape[1] // rows
    row = owner(scores.shape)
    position = lax.broadcasted_iota(jnp.int32, scores.shape, 1) - row * cache
    limit = jnp.zeros(scores.shape, jnp.int32)
    for r in range(rows):
        limit = jnp.where(row == r, lengths[r], limit)
    live = (position >= 0) & (position < limit)
    scores = jnp.where(live, scores, jnp.float32(-1e30))
    highest = jnp.maximum(jnp.max(scores, 1, keepdims=True), own_score)
    cache_exp = jnp.where(live, jnp.exp(scores - highest), 0.0)
    own_exp = jnp.exp(own_score - highest)
    denom = jnp.sum(cache_exp, 1, keepdims=True) + own_exp
    cache_weight = (cache_exp / denom).astype(jnp.bfloat16)
    own_weight = jnp.where(own_at, own_exp / denom, 0.0).astype(jnp.bfloat16)
    for copy in values:
        copy.wait()
    give.start()
    attended = jnp.dot(cache_weight, v_ref[...], preferred_element_type=jnp.float32) + jnp.dot(
        own_weight, new_values, preferred_element_type=jnp.float32
    )
    for tile in range(tiles):
        for r in range(rows):
            for step in range(per):
                head = member(tile, tiles) // 2 * per + step
                place = r * per + step
                msg[tile, place : place + 1, :] = attended[
                    r * heads + head : r * heads + head + 1, head * LANES : (head + 1) * LANES
                ]
    out_ref[...] = msg[...].astype(jnp.bfloat16)
    give.wait()


def project_kernel(parity_ref, in_ref, own_ref, other_ref, out_ref, held, total, *, rows, per):
    tiles, depth = in_ref.shape[:2]
    held[...] = in_ref[...].astype(jnp.float32).reshape(held.shape)
    groups = total.shape[0]
    lines = out_ref.shape[2] // rows
    share = own_ref.shape[0]
    lhs = []
    for row in range(rows):
        parts = [held[pl.ds(row * per + j, tiles, stride=depth), :] for j in range(per)]
        lhs.append(jnp.concatenate(parts, 1))
    lhs = jnp.concatenate(lhs, 0)
    even = parity_ref[0] == 0
    first, second = lhs[:, :share], lhs[:, share:]
    own = jnp.where(even, first, second).astype(jnp.bfloat16)
    other = jnp.where(even, second, first).astype(jnp.bfloat16)
    product = jnp.dot(own, own_ref[...], preferred_element_type=jnp.float32) + jnp.dot(
        other, other_ref[...], preferred_element_type=jnp.float32
    )
    for row in range(rows):
        for group in range(groups):
            for line in range(lines):
                begin = (group * lines + line) * LANES
                total[group, pl.ds(row * lines + line, tiles, stride=rows * lines), :] = product[
                    row * tiles : (row + 1) * tiles, begin : begin + LANES
                ]
    for group in range(groups):
        out_ref[:, group] = (
            total[group].astype(jnp.bfloat16).reshape(tiles, rows * lines, LANES)
        )


def total_kernel(in_ref, out_ref, held, *, rows):
    tiles, groups, depth, _ = in_ref.shape
    lines = depth // rows
    parts = in_ref[...].astype(jnp.float32).reshape(tiles // 2, 2 * groups, depth, LANES)
    held[...] = jnp.sum(parts, 0)
    for group in range(2 * groups):
        for line in range(lines):
            begin = (group * lines + line) * LANES
            out_ref[:, begin : begin + LANES] = held[
                group, pl.ds(line, rows, stride=lines), :
            ].astype(jnp.bfloat16)


def split_three(whole):
    high = whole.astype(jnp.bfloat16).astype(jnp.float32)
    middle = (whole - high).astype(jnp.bfloat16).astype(jnp.float32)
    return jnp.concatenate([high, middle, whole - high - middle], 0)


def fold_kernel(
    parity_ref, cw_ref, conv_ref, weight_ref, after_ref, out_ref, near_ref, levels_w, folded, held, sems, near_sem
):
    del after_ref
    taps = [(dr, dc) for dr in range(3) for dc in range(3)]
    copies = [
        pltpu.make_async_copy(conv_ref.at[dr, dc], held.at[at], sems.at[at])
        for at, (dr, dc) in enumerate(taps)
    ]
    for copy in copies:
        copy.start()
    begin = pl.multiple_of(parity_ref[0] * near_ref.shape[1], LANES)
    bring = pltpu.make_async_copy(
        weight_ref.at[:, pl.ds(begin, near_ref.shape[1])], near_ref, near_sem
    )
    bring.start()
    levels_w[...] = jnp.zeros_like(levels_w)
    levels_w[0:FSQ_DIMS, :] = cw_ref[...]
    left = split_three(levels_w[...]).astype(jnp.bfloat16)
    folded[...] = jnp.zeros_like(folded)
    for at, copy in enumerate(copies):
        copy.wait()
        parts = jnp.dot(left, held[at], preferred_element_type=jnp.float32)
        total = parts[0:8] + parts[8:16] + parts[16:24]
        folded[at * TAP_ROWS : (at + 1) * TAP_ROWS, :] = split_three(total)
    out_ref[...] = folded[...].astype(jnp.bfloat16)
    bring.wait()


def decode_kernel(section_ref, in_ref, fold_ref, two_ref, after_ref, out_ref, *, feature_rows):
    del after_ref
    section = section_ref[0]
    got = jnp.sum(in_ref[...].astype(jnp.float32), 0)
    pieces = []
    for at in range(PIECES):
        lines = [
            got[feature_rows + at * WINDOW + step : feature_rows + at * WINDOW + step + 1]
            for step in range(WINDOW)
        ]
        pieces.append(jnp.concatenate(lines, 1))
    codes = decode_number(jnp.concatenate(pieces, 1))
    span = codes.shape[1]
    depth = fold_ref.shape[0]
    level = lax.broadcasted_iota(jnp.int32, (8, span), 0)
    taken = level < FSQ_DIMS
    shift = jnp.where(taken, level * 3, 0)
    value = (2 * ((jnp.broadcast_to(codes, (8, span)) >> shift) & 7) - 7).astype(
        jnp.float32
    ) * 0.125
    value = jnp.where(taken, value, 0.0)
    value = jnp.concatenate([value] * (depth // 8), 0).astype(jnp.bfloat16)

    count = TILE_ROWS * IMG_W
    begin = TILE_H * ROW_WORDS * section - HALO * ROW_WORDS
    offset = begin & (LANES - 1)
    spot = lax.broadcasted_iota(jnp.int32, (count, 1), 0)
    line = spot // IMG_W + TILE_H * section - HALO
    inside = (line >= 0) & (line < IMG_SPLIT * TILE_H)
    target = jnp.where(inside, (spot >> 1) + offset + (span // 2) * (spot & 1), -1)
    chooser = jnp.where(
        lax.broadcasted_iota(jnp.int32, (count, span), 1) == target, 1.0, 0.0
    ).astype(jnp.bfloat16)
    placed = lax.dot_general(
        chooser, value, (((1,), (1,)), ((), ())), preferred_element_type=jnp.float32
    )
    column = spot % IMG_W
    moved = [
        jnp.where(column == 0, 0.0, pltpu.roll(placed, 1, 0)),
        placed,
        jnp.where(column == IMG_W - 1, 0.0, pltpu.roll(placed, count - 1, 0)),
    ]
    count = count - 2 * IMG_W
    tap_of = lax.broadcasted_iota(jnp.int32, (1, depth), 1) // TAP_ROWS
    taps = jnp.zeros((count, depth), jnp.float32)
    for dr in range(3):
        for dc in range(3):
            taps = jnp.where(
                tap_of == 3 * dr + dc, moved[dc][dr * IMG_W : dr * IMG_W + count], taps
            )
    hidden = jnp.dot(taps.astype(jnp.bfloat16), fold_ref[...], preferred_element_type=jnp.float32)

    line = lax.broadcasted_iota(jnp.int32, (count, 1), 0) // IMG_W + TILE_H * section - 1
    inside = (line >= 0) & (line < IMG_SPLIT * TILE_H)
    activated = jnp.where(inside, hidden * jax.nn.sigmoid(hidden), 0.0).astype(jnp.bfloat16)

    count = count - 2 * IMG_W
    column = lax.broadcasted_iota(jnp.int32, (count, 1), 0) % IMG_W
    summed = None
    for dc in (1, 0, 2):
        part = None
        for dr in range(3):
            term = jnp.dot(
                activated[dr * IMG_W : dr * IMG_W + count],
                two_ref[dr, dc],
                preferred_element_type=jnp.float32,
            )
            part = term if part is None else part + term
        if dc == 0:
            part = jnp.where(column == 0, 0.0, pltpu.roll(part, 1, 0))
        if dc == 2:
            part = jnp.where(column == IMG_W - 1, 0.0, pltpu.roll(part, count - 1, 0))
        summed = part if summed is None else summed + part
    out_ref[...] = summed.astype(jnp.bfloat16)


def near(array):
    return pltpu.with_memory_space_constraint(array, pltpu.VMEM)


def far(array):
    return pltpu.with_memory_space_constraint(array, pltpu.HBM)


def on_device(
    queries,
    new_keys,
    new_values,
    cache_keys,
    cache_values,
    cache_lengths,
    out_weight,
    codes,
    tile_slot,
    code_weight,
    conv_one,
    conv_two,
):
    tiles = lax.axis_size("rows")
    place = lax.axis_index("rows")
    rows, width = queries.shape
    channels = code_weight.shape[1]
    share = width // tiles
    per = 2 * share // LANES
    feature_rows = rows * per
    depth = message_rows(feature_rows)
    half = width // 2
    lines = 8
    groups = half // (lines * LANES)
    params = pltpu.CompilerParams(vmem_limit_bytes=VMEM_LIMIT)
    smem = pl.BlockSpec(memory_space=pltpu.SMEM)
    vmem = pl.BlockSpec(memory_space=pltpu.VMEM)
    anywhere = pl.BlockSpec(memory_space=pl.ANY)
    parity = (place % 2).reshape(1).astype(jnp.int32)

    outgoing, give = pl.pallas_call(
        functools.partial(attend_kernel, tiles=tiles, per=per, feature_rows=feature_rows),
        in_specs=[smem] * 3 + [anywhere] * 7,
        out_specs=[vmem, vmem],
        out_shape=[
            pltpu.VMEM((tiles, depth, LANES), jnp.bfloat16),
            pltpu.VMEM((share, half), out_weight.dtype),
        ],
        scratch_shapes=[
            pltpu.VMEM(queries.shape, queries.dtype),
            pltpu.VMEM(new_keys.shape, new_keys.dtype),
            pltpu.VMEM(new_values.shape, new_values.dtype),
            pltpu.VMEM((rows * cache_keys.shape[1], width), cache_keys.dtype),
            pltpu.VMEM((rows * cache_values.shape[1], width), cache_values.dtype),
            pltpu.VMEM(codes.shape, codes.dtype),
            pltpu.VMEM((tiles, depth, LANES), jnp.float32),
            pltpu.SemaphoreType.DMA((5 + 2 * rows,)),
        ],
        compiler_params=pltpu.CompilerParams(vmem_limit_bytes=56 * 1024 * 1024),
    )(
        cache_lengths,
        tile_slot,
        parity,
        far(queries),
        far(new_keys),
        far(new_values),
        far(cache_keys),
        far(cache_values),
        far(codes),
        far(out_weight),
    )
    order = [[member(at, tiles) for at in range(tiles)]]
    incoming = lax.all_to_all(
        outgoing, "rows", split_axis=0, concat_axis=0, axis_index_groups=order, tiled=True
    )
    other = lax.ppermute(give, "rows", [(i, i ^ 1) for i in range(tiles)])

    folded, own = pl.pallas_call(
        fold_kernel,
        in_specs=[smem, vmem, anywhere, anywhere, anywhere],
        out_specs=[vmem, vmem],
        out_shape=[
            jax.ShapeDtypeStruct((FOLD_ROWS, channels), jnp.bfloat16),
            pltpu.VMEM((share, half), out_weight.dtype),
        ],
        scratch_shapes=[
            pltpu.VMEM((8, channels), jnp.float32),
            pltpu.VMEM((FOLD_ROWS, channels), jnp.float32),
            pltpu.VMEM((9,) + conv_one.shape[2:], conv_one.dtype),
            pltpu.SemaphoreType.DMA((9,)),
            pltpu.SemaphoreType.DMA,
        ],
        compiler_params=params,
    )(parity, far(code_weight), far(conv_one), far(out_weight), near(outgoing))

    partials = pl.pallas_call(
        functools.partial(project_kernel, rows=rows, per=per),
        in_specs=[smem, vmem, vmem, vmem],
        out_shape=pltpu.VMEM((tiles, groups, rows * lines, LANES), jnp.bfloat16),
        scratch_shapes=[
            pltpu.VMEM((tiles * depth, LANES), jnp.float32),
            pltpu.VMEM((groups, tiles * rows * lines, LANES), jnp.float32),
        ],
        cost_estimate=pl.CostEstimate(
            flops=4 * tiles * rows * share * half,
            transcendentals=0,
            bytes_accessed=3 * conv_two.size,
        ),
        compiler_params=params,
    )(parity, near(incoming), near(own), near(other))
    gathered = lax.all_to_all(
        partials, "rows", split_axis=0, concat_axis=0, axis_index_groups=order, tiled=True
    )

    section = (place + IMG_SPLIT // 2) % tiles % IMG_SPLIT
    decoded = pl.pallas_call(
        functools.partial(decode_kernel, feature_rows=feature_rows),
        in_specs=[smem, vmem, vmem, vmem, anywhere],
        out_specs=vmem,
        out_shape=jax.ShapeDtypeStruct((TILE_H * IMG_W, channels), jnp.bfloat16),
        compiler_params=params,
    )(section.reshape(1).astype(jnp.int32), near(incoming), near(folded), near(conv_two), near(partials))

    mixed = pl.pallas_call(
        functools.partial(total_kernel, rows=rows),
        in_specs=[vmem],
        out_shape=jax.ShapeDtypeStruct((rows, width), jnp.bfloat16),
        scratch_shapes=[pltpu.VMEM((2 * groups, rows * lines, LANES), jnp.float32)],
        compiler_params=params,
    )(near(gathered))
    return (mixed, decoded.reshape(TILE_H, IMG_W, channels))


def solution(mesh):
    in_specs = (
        P(("groups", "rows"), None),
        P(("groups", "rows"), None),
        P(("groups", "rows"), None),
        P(("groups", "rows"), None, None),
        P(("groups", "rows"), None, None),
        P(("groups", "rows")),
        P("rows", None),
        P(("groups", "rows"), None),
        P(("groups", "rows")),
        P(),
        P(),
        P(),
    )
    out_specs = (P(("groups", "rows"), None), P(("groups", "rows"), None, None))
    return jax.shard_map(
        on_device, mesh=mesh, in_specs=in_specs, out_specs=out_specs, check_vma=False
    )
```

```python
import functools
import math

import jax
import jax.numpy as jnp
from jax import lax
from jax.experimental import pallas as pl
from jax.experimental.pallas import tpu as pltpu
from jax.sharding import PartitionSpec as P

HEAD_DIM = 128
FSQ_DIMS = 5
IMG_SPLIT = 4
TILE_H = 8
IMG_W = 48
LANES = 128
HALO = 2
ROW_WORDS = IMG_W // 2
TILE_ROWS = TILE_H + 2 * HALO
WINDOW = 3
PIECES = 2
CODE_ROWS = WINDOW * PIECES
TAP_ROWS = 24
FOLD_ROWS = 256
VMEM_LIMIT = 24 * 1024 * 1024


def window_start(section):
    return (TILE_H * ROW_WORDS * section - HALO * ROW_WORDS) // LANES


def member(at, tiles):
    return (at + tiles // 4 * 2) % tiles


def message_rows(features):
    return -(-(features + CODE_ROWS) // 16) * 16


def encode(code):
    fraction = (code & 127).astype(jnp.float32) * (1.0 / 128.0) + 1.0
    for bit in range(7):
        up = ((code >> (7 + bit)) & 1) == 1
        fraction = jnp.where(up, fraction * 2.0 ** (1 << bit), fraction)
        if bit == 5:
            fraction = fraction * 2.0**-64
    return jnp.where(((code >> 14) & 1) == 1, -fraction, fraction)


def decode_number(value):
    size = jnp.abs(value)
    code = jnp.where(value < 0.0, 1 << 14, 0)
    for bit in range(6, -1, -1):
        step = 1 << bit
        up = size >= 2.0 ** (step - 64)
        code = code + jnp.where(up, step << 7, 0)
        size = jnp.where(up, size * 2.0**-step, size)
    return code + ((size * 2.0**64 - 1.0) * 128.0).astype(jnp.int32)


def attend_kernel(
    lengths,
    slots,
    parity_ref,
    q_any,
    nk_any,
    nv_any,
    k_any,
    v_any,
    codes_any,
    weight_any,
    out_ref,
    give_ref,
    q_ref,
    nk_ref,
    nv_ref,
    k_ref,
    v_ref,
    codes_ref,
    msg,
    by_head,
    spread,
    sems,
    *,
    tiles,
    per,
    feature_rows,
):
    rows, width = q_ref.shape
    give_columns = give_ref.shape[1]
    small = [
        pltpu.make_async_copy(source, target, sems.at[at])
        for at, (source, target) in enumerate(
            ((q_any, q_ref), (nk_any, nk_ref), (nv_any, nv_ref), (codes_any, codes_ref))
        )
    ]
    cached = k_any.shape[1]
    keys, values = (
        [
            pltpu.make_async_copy(
                source.at[r], target.at[pl.ds(r * cached, cached)], sems.at[base + r]
            )
            for r in range(rows)
        ]
        for source, target, base in ((k_any, k_ref, 4), (v_any, v_ref, 4 + rows))
    )
    begin = pl.multiple_of((1 - parity_ref[0]) * give_columns, LANES)
    give = pltpu.make_async_copy(
        weight_any.at[:, pl.ds(begin, give_columns)], give_ref, sems.at[4 + 2 * rows]
    )
    for copy in small:
        copy.start()
    for copy in keys + values:
        copy.start()

    heads = width // HEAD_DIM
    factor = 1.0 / math.sqrt(HEAD_DIM)
    msg[...] = jnp.zeros_like(msg)
    for copy in small:
        copy.wait()

    words = codes_ref[...]
    blocks = words.shape[1] // LANES
    pieces = [encode(words & 32767), encode(words >> 15)]
    for slot in range(tiles // IMG_SPLIT):
        gains = [
            jnp.where(slots[r] == slot, 1.0, 0.0).astype(jnp.float32) for r in range(rows)
        ]
        for at, piece in enumerate(pieces):
            total = piece[0:1] * gains[0]
            for r in range(1, rows):
                total = total + piece[r : r + 1] * gains[r]
            for tile in range(tiles):
                number = (member(tile, tiles) + IMG_SPLIT // 2) % tiles
                if number // IMG_SPLIT != slot:
                    continue
                for step in range(WINDOW):
                    block = window_start(number % IMG_SPLIT) + step
                    if block < 0 or block >= blocks:
                        continue
                    place = feature_rows + at * WINDOW + step
                    msg[tile, place : place + 1, :] = total[:, block * LANES : (block + 1) * LANES]

    queries = q_ref[...].astype(jnp.float32)
    by_head[...] = jnp.zeros_like(by_head)
    for r in range(rows):
        for head in range(heads):
            by_head[r * heads + head : r * heads + head + 1, :] = queries[
                r : r + 1, head * LANES : (head + 1) * LANES
            ]
    turned = by_head[...].T
    column = lax.broadcasted_iota(jnp.int32, (1, LANES), 1)
    for head in range(heads):
        spread[head * LANES : (head + 1) * LANES, :] = jnp.where(
            column % heads == head, turned, 0.0
        ).astype(jnp.bfloat16)
    padding = jnp.zeros((16 - rows, width), jnp.float32)
    known = rows * cached
    k_ref[known:, :] = jnp.concatenate([nk_ref[...].astype(jnp.float32), padding], 0).astype(
        jnp.bfloat16
    )
    new_values = jnp.concatenate([nv_ref[...].astype(jnp.float32), padding], 0).astype(jnp.bfloat16)
    for copy in keys:
        copy.wait()
    products = jnp.dot(k_ref[...], spread[...], preferred_element_type=jnp.float32) * factor
    give.start()
    own_scores = products[known:]
    scores = products[:known]
    owner = column // heads
    own_at = lax.broadcasted_iota(jnp.int32, own_scores.shape, 0) == owner
    own_score = jnp.sum(jnp.where(own_at, own_scores, 0.0), 0, keepdims=True)
    limit = jnp.zeros(column.shape, jnp.int32)
    for r in range(rows):
        limit = jnp.where(owner == r, lengths[r], limit)
    position = lax.broadcasted_iota(jnp.int32, scores.shape, 0) - owner * cached
    live = (position >= 0) & (position < limit)
    scores = jnp.where(live, scores, jnp.float32(-1e30))
    highest = jnp.maximum(jnp.max(scores, 0, keepdims=True), own_score)
    cache_exp = jnp.where(live, jnp.exp(scores - highest), 0.0)
    own_exp = jnp.exp(own_score - highest)
    denom = jnp.sum(cache_exp, 0, keepdims=True) + own_exp
    cache_weight = (cache_exp / denom).T[: rows * heads].astype(jnp.bfloat16)
    own_weight = jnp.where(own_at, own_exp / denom, 0.0)
    own_weight = jnp.concatenate(
        [own_weight, jnp.zeros((LANES - own_weight.shape[0], LANES), jnp.float32)], 0
    ).T[: rows * heads, :16].astype(jnp.bfloat16)
    for copy in values:
        copy.wait()
    attended = jnp.dot(cache_weight, v_ref[...], preferred_element_type=jnp.float32) + jnp.dot(
        own_weight, new_values, preferred_element_type=jnp.float32
    )
    for tile in range(tiles):
        for r in range(rows):
            for step in range(per):
                head = member(tile, tiles) // 2 * per + step
                place = r * per + step
                msg[tile, place : place + 1, :] = attended[
                    r * heads + head : r * heads + head + 1, head * LANES : (head + 1) * LANES
                ]
    out_ref[...] = msg[...].astype(jnp.bfloat16)
    give.wait()


def project_kernel(parity_ref, in_ref, own_ref, other_ref, out_ref, held, total, *, rows, per):
    tiles, depth = in_ref.shape[:2]
    held[...] = in_ref[...].astype(jnp.float32).reshape(held.shape)
    groups = total.shape[0]
    lines = out_ref.shape[2] // rows
    share = own_ref.shape[0]
    lhs = []
    for row in range(rows):
        parts = [held[pl.ds(row * per + j, tiles, stride=depth), :] for j in range(per)]
        lhs.append(jnp.concatenate(parts, 1))
    lhs = jnp.concatenate(lhs, 0)
    even = parity_ref[0] == 0
    first, second = lhs[:, :share], lhs[:, share:]
    own = jnp.where(even, first, second).astype(jnp.bfloat16)
    other = jnp.where(even, second, first).astype(jnp.bfloat16)
    product = jnp.dot(own, own_ref[...], preferred_element_type=jnp.float32) + jnp.dot(
        other, other_ref[...], preferred_element_type=jnp.float32
    )
    for row in range(rows):
        for group in range(groups):
            for line in range(lines):
                begin = (group * lines + line) * LANES
                total[group, pl.ds(row * lines + line, tiles, stride=rows * lines), :] = product[
                    row * tiles : (row + 1) * tiles, begin : begin + LANES
                ]
    for group in range(groups):
        out_ref[:, group] = (
            total[group].astype(jnp.bfloat16).reshape(tiles, rows * lines, LANES)
        )


def total_kernel(in_ref, out_ref, held, *, rows):
    tiles, groups, depth, _ = in_ref.shape
    lines = depth // rows
    parts = in_ref[...].astype(jnp.float32).reshape(tiles // 2, 2 * groups, depth, LANES)
    held[...] = jnp.sum(parts, 0)
    for group in range(2 * groups):
        for line in range(lines):
            begin = (group * lines + line) * LANES
            out_ref[:, begin : begin + LANES] = held[
                group, pl.ds(line, rows, stride=lines), :
            ].astype(jnp.bfloat16)


def split_three(whole):
    high = whole.astype(jnp.bfloat16).astype(jnp.float32)
    middle = (whole - high).astype(jnp.bfloat16).astype(jnp.float32)
    return jnp.concatenate([high, middle, whole - high - middle], 0)


def fold_kernel(
    parity_ref, cw_ref, conv_ref, weight_ref, after_ref, out_ref, near_ref, levels_w, folded, held, sems, near_sem
):
    del after_ref
    taps = [(dr, dc) for dr in range(3) for dc in range(3)]
    copies = [
        pltpu.make_async_copy(conv_ref.at[dr, dc], held.at[at], sems.at[at])
        for at, (dr, dc) in enumerate(taps)
    ]
    for copy in copies:
        copy.start()
    begin = pl.multiple_of(parity_ref[0] * near_ref.shape[1], LANES)
    bring = pltpu.make_async_copy(
        weight_ref.at[:, pl.ds(begin, near_ref.shape[1])], near_ref, near_sem
    )
    bring.start()
    levels_w[...] = jnp.zeros_like(levels_w)
    levels_w[0:FSQ_DIMS, :] = cw_ref[...]
    left = split_three(levels_w[...]).astype(jnp.bfloat16)
    folded[...] = jnp.zeros_like(folded)
    for at, copy in enumerate(copies):
        copy.wait()
        parts = jnp.dot(left, held[at], preferred_element_type=jnp.float32)
        total = parts[0:8] + parts[8:16] + parts[16:24]
        folded[at * TAP_ROWS : (at + 1) * TAP_ROWS, :] = split_three(total)
    out_ref[...] = folded[...].astype(jnp.bfloat16)
    bring.wait()


def decode_kernel(
    section_ref, in_ref, fold_ref, two_any, after_ref, out_ref, two_ref, sems, *, feature_rows
):
    del after_ref
    copies = {}
    for dc in (1, 0, 2):
        for dr in range(3):
            copies[dr, dc] = pltpu.make_async_copy(
                two_any.at[dr, dc], two_ref.at[dr, dc], sems.at[dr, dc]
            )
            copies[dr, dc].start()
    section = section_ref[0]
    got = jnp.sum(in_ref[...].astype(jnp.float32), 0)
    pieces = []
    for at in range(PIECES):
        lines = [
            got[feature_rows + at * WINDOW + step : feature_rows + at * WINDOW + step + 1]
            for step in range(WINDOW)
        ]
        pieces.append(jnp.concatenate(lines, 1))
    codes = decode_number(jnp.concatenate(pieces, 1))
    span = codes.shape[1]
    depth = fold_ref.shape[0]
    level = lax.broadcasted_iota(jnp.int32, (8, span), 0)
    taken = level < FSQ_DIMS
    shift = jnp.where(taken, level * 3, 0)
    value = (2 * ((jnp.broadcast_to(codes, (8, span)) >> shift) & 7) - 7).astype(
        jnp.float32
    ) * 0.125
    value = jnp.where(taken, value, 0.0)
    value = jnp.concatenate([value] * (depth // 8), 0).astype(jnp.bfloat16)

    count = TILE_ROWS * IMG_W
    begin = TILE_H * ROW_WORDS * section - HALO * ROW_WORDS
    offset = begin & (LANES - 1)
    spot = lax.broadcasted_iota(jnp.int32, (count, 1), 0)
    line = spot // IMG_W + TILE_H * section - HALO
    inside = (line >= 0) & (line < IMG_SPLIT * TILE_H)
    target = jnp.where(inside, (spot >> 1) + offset + (span // 2) * (spot & 1), -1)
    chooser = jnp.where(
        lax.broadcasted_iota(jnp.int32, (count, span), 1) == target, 1.0, 0.0
    ).astype(jnp.bfloat16)
    placed = lax.dot_general(
        chooser, value, (((1,), (1,)), ((), ())), preferred_element_type=jnp.float32
    )
    column = spot % IMG_W
    moved = [
        jnp.where(column == 0, 0.0, pltpu.roll(placed, 1, 0)),
        placed,
        jnp.where(column == IMG_W - 1, 0.0, pltpu.roll(placed, count - 1, 0)),
    ]
    count = count - 2 * IMG_W
    tap_of = lax.broadcasted_iota(jnp.int32, (1, depth), 1) // TAP_ROWS
    taps = jnp.zeros((count, depth), jnp.float32)
    for dr in range(3):
        for dc in range(3):
            taps = jnp.where(
                tap_of == 3 * dr + dc, moved[dc][dr * IMG_W : dr * IMG_W + count], taps
            )
    hidden = jnp.dot(taps.astype(jnp.bfloat16), fold_ref[...], preferred_element_type=jnp.float32)

    line = lax.broadcasted_iota(jnp.int32, (count, 1), 0) // IMG_W + TILE_H * section - 1
    inside = (line >= 0) & (line < IMG_SPLIT * TILE_H)
    activated = jnp.where(inside, hidden * jax.nn.sigmoid(hidden), 0.0).astype(jnp.bfloat16)

    count = count - 2 * IMG_W
    column = lax.broadcasted_iota(jnp.int32, (count, 1), 0) % IMG_W
    summed = None
    for dc in (1, 0, 2):
        part = None
        for dr in range(3):
            copies[dr, dc].wait()
            term = jnp.dot(
                activated[dr * IMG_W : dr * IMG_W + count],
                two_ref[dr, dc],
                preferred_element_type=jnp.float32,
            )
            part = term if part is None else part + term
        if dc == 0:
            part = jnp.where(column == 0, 0.0, pltpu.roll(part, 1, 0))
        if dc == 2:
            part = jnp.where(column == IMG_W - 1, 0.0, pltpu.roll(part, count - 1, 0))
        summed = part if summed is None else summed + part
    out_ref[...] = summed.astype(jnp.bfloat16)


def near(array):
    return pltpu.with_memory_space_constraint(array, pltpu.VMEM)


def far(array):
    return pltpu.with_memory_space_constraint(array, pltpu.HBM)


def on_device(
    queries,
    new_keys,
    new_values,
    cache_keys,
    cache_values,
    cache_lengths,
    out_weight,
    codes,
    tile_slot,
    code_weight,
    conv_one,
    conv_two,
):
    tiles = lax.axis_size("rows")
    place = lax.axis_index("rows")
    rows, width = queries.shape
    channels = code_weight.shape[1]
    share = width // tiles
    per = 2 * share // LANES
    feature_rows = rows * per
    depth = message_rows(feature_rows)
    half = width // 2
    lines = 8
    groups = half // (lines * LANES)
    params = pltpu.CompilerParams(vmem_limit_bytes=VMEM_LIMIT)
    smem = pl.BlockSpec(memory_space=pltpu.SMEM)
    vmem = pl.BlockSpec(memory_space=pltpu.VMEM)
    anywhere = pl.BlockSpec(memory_space=pl.ANY)
    parity = (place % 2).reshape(1).astype(jnp.int32)

    outgoing, give = pl.pallas_call(
        functools.partial(attend_kernel, tiles=tiles, per=per, feature_rows=feature_rows),
        in_specs=[smem] * 3 + [anywhere] * 7,
        out_specs=[vmem, vmem],
        out_shape=[
            pltpu.VMEM((tiles, depth, LANES), jnp.bfloat16),
            pltpu.VMEM((share, half), out_weight.dtype),
        ],
        scratch_shapes=[
            pltpu.VMEM(queries.shape, queries.dtype),
            pltpu.VMEM(new_keys.shape, new_keys.dtype),
            pltpu.VMEM(new_values.shape, new_values.dtype),
            pltpu.VMEM((rows * cache_keys.shape[1] + 16, width), cache_keys.dtype),
            pltpu.VMEM((rows * cache_values.shape[1], width), cache_values.dtype),
            pltpu.VMEM(codes.shape, codes.dtype),
            pltpu.VMEM((tiles, depth, LANES), jnp.float32),
            pltpu.VMEM((LANES, LANES), jnp.float32),
            pltpu.VMEM((width, LANES), jnp.bfloat16),
            pltpu.SemaphoreType.DMA((5 + 2 * rows,)),
        ],
        compiler_params=pltpu.CompilerParams(vmem_limit_bytes=56 * 1024 * 1024),
    )(
        cache_lengths,
        tile_slot,
        parity,
        far(queries),
        far(new_keys),
        far(new_values),
        far(cache_keys),
        far(cache_values),
        far(codes),
        far(out_weight),
    )
    order = [[member(at, tiles) for at in range(tiles)]]
    incoming = lax.all_to_all(
        outgoing, "rows", split_axis=0, concat_axis=0, axis_index_groups=order, tiled=True
    )
    other = lax.ppermute(give, "rows", [(i, i ^ 1) for i in range(tiles)])

    folded, own = pl.pallas_call(
        fold_kernel,
        in_specs=[smem, vmem, anywhere, anywhere, anywhere],
        out_specs=[vmem, vmem],
        out_shape=[
            jax.ShapeDtypeStruct((FOLD_ROWS, channels), jnp.bfloat16),
            pltpu.VMEM((share, half), out_weight.dtype),
        ],
        scratch_shapes=[
            pltpu.VMEM((8, channels), jnp.float32),
            pltpu.VMEM((FOLD_ROWS, channels), jnp.float32),
            pltpu.VMEM((9,) + conv_one.shape[2:], conv_one.dtype),
            pltpu.SemaphoreType.DMA((9,)),
            pltpu.SemaphoreType.DMA,
        ],
        compiler_params=params,
    )(parity, far(code_weight), far(conv_one), far(out_weight), near(outgoing))

    partials = pl.pallas_call(
        functools.partial(project_kernel, rows=rows, per=per),
        in_specs=[smem, vmem, vmem, vmem],
        out_shape=pltpu.VMEM((tiles, groups, rows * lines, LANES), jnp.bfloat16),
        scratch_shapes=[
            pltpu.VMEM((tiles * depth, LANES), jnp.float32),
            pltpu.VMEM((groups, tiles * rows * lines, LANES), jnp.float32),
        ],
        compiler_params=params,
    )(parity, near(incoming), near(own), near(other))
    gathered = lax.all_to_all(
        partials, "rows", split_axis=0, concat_axis=0, axis_index_groups=order, tiled=True
    )

    section = (place + IMG_SPLIT // 2) % tiles % IMG_SPLIT
    decoded = pl.pallas_call(
        functools.partial(decode_kernel, feature_rows=feature_rows),
        in_specs=[smem, vmem, vmem, anywhere, anywhere],
        out_specs=vmem,
        out_shape=jax.ShapeDtypeStruct((TILE_H * IMG_W, channels), jnp.bfloat16),
        scratch_shapes=[
            pltpu.VMEM(conv_two.shape, conv_two.dtype),
            pltpu.SemaphoreType.DMA((3, 3)),
        ],
        compiler_params=params,
    )(section.reshape(1).astype(jnp.int32), near(incoming), near(folded), far(conv_two), near(partials))

    mixed = pl.pallas_call(
        functools.partial(total_kernel, rows=rows),
        in_specs=[vmem],
        out_shape=jax.ShapeDtypeStruct((rows, width), jnp.bfloat16),
        scratch_shapes=[pltpu.VMEM((2 * groups, rows * lines, LANES), jnp.float32)],
        compiler_params=params,
    )(near(gathered))
    return (mixed, decoded.reshape(TILE_H, IMG_W, channels))


def solution(mesh):
    in_specs = (
        P(("groups", "rows"), None),
        P(("groups", "rows"), None),
        P(("groups", "rows"), None),
        P(("groups", "rows"), None, None),
        P(("groups", "rows"), None, None),
        P(("groups", "rows")),
        P("rows", None),
        P(("groups", "rows"), None),
        P(("groups", "rows")),
        P(),
        P(),
        P(),
    )
    out_specs = (P(("groups", "rows"), None), P(("groups", "rows"), None, None))
    return jax.shard_map(
        on_device, mesh=mesh, in_specs=in_specs, out_specs=out_specs, check_vma=False
    )
```

```python
import functools
import math

import jax
import jax.numpy as jnp
from jax import lax
from jax.experimental import pallas as pl
from jax.experimental.pallas import tpu as pltpu
from jax.sharding import PartitionSpec as P

HEAD_DIM = 128
FSQ_DIMS = 5
IMG_SPLIT = 4
TILE_H = 8
IMG_W = 48
LANES = 128
HALO = 2
ROW_WORDS = IMG_W // 2
TILE_ROWS = TILE_H + 2 * HALO
WINDOW = 3
PIECES = 2
CODE_ROWS = WINDOW * PIECES
TAP_ROWS = 24
FOLD_ROWS = 256
TAPS = [(dr, dc) for dc in (1, 0, 2) for dr in range(3)]
EARLY = 4
VMEM_LIMIT = 24 * 1024 * 1024


def window_start(section):
    return (TILE_H * ROW_WORDS * section - HALO * ROW_WORDS) // LANES


def member(at, tiles):
    return (at + tiles // 4 * 2) % tiles


def message_rows(features):
    return -(-(features + CODE_ROWS) // 16) * 16


def encode(code):
    fraction = (code & 127).astype(jnp.float32) * (1.0 / 128.0) + 1.0
    for bit in range(7):
        up = ((code >> (7 + bit)) & 1) == 1
        fraction = jnp.where(up, fraction * 2.0 ** (1 << bit), fraction)
        if bit == 5:
            fraction = fraction * 2.0**-64
    return jnp.where(((code >> 14) & 1) == 1, -fraction, fraction)


def decode_number(value):
    size = jnp.abs(value)
    code = jnp.where(value < 0.0, 1 << 14, 0)
    for bit in range(6, -1, -1):
        step = 1 << bit
        up = size >= 2.0 ** (step - 64)
        code = code + jnp.where(up, step << 7, 0)
        size = jnp.where(up, size * 2.0**-step, size)
    return code + ((size * 2.0**64 - 1.0) * 128.0).astype(jnp.int32)


def attend_kernel(
    lengths,
    slots,
    q_any,
    nk_any,
    nv_any,
    k_any,
    v_any,
    codes_any,
    out_ref,
    q_ref,
    nk_ref,
    nv_ref,
    k_ref,
    v_ref,
    codes_ref,
    msg,
    by_head,
    spread,
    sems,
    *,
    tiles,
    per,
    feature_rows,
):
    rows, width = q_ref.shape
    small = [
        pltpu.make_async_copy(source, target, sems.at[at])
        for at, (source, target) in enumerate(
            ((q_any, q_ref), (nk_any, nk_ref), (nv_any, nv_ref), (codes_any, codes_ref))
        )
    ]
    cached = k_any.shape[1]
    keys, values = (
        [
            pltpu.make_async_copy(
                source.at[r], target.at[pl.ds(r * cached, cached)], sems.at[base + r]
            )
            for r in range(rows)
        ]
        for source, target, base in ((k_any, k_ref, 4), (v_any, v_ref, 4 + rows))
    )
    for copy in small:
        copy.start()
    for copy in keys:
        copy.start()

    heads = width // HEAD_DIM
    factor = 1.0 / math.sqrt(HEAD_DIM)
    msg[...] = jnp.zeros_like(msg)
    for copy in small:
        copy.wait()

    words = codes_ref[...]
    blocks = words.shape[1] // LANES
    pieces = [encode(words & 32767), encode(words >> 15)]
    for slot in range(tiles // IMG_SPLIT):
        gains = [
            jnp.where(slots[r] == slot, 1.0, 0.0).astype(jnp.float32) for r in range(rows)
        ]
        for at, piece in enumerate(pieces):
            total = piece[0:1] * gains[0]
            for r in range(1, rows):
                total = total + piece[r : r + 1] * gains[r]
            for tile in range(tiles):
                number = (member(tile, tiles) + IMG_SPLIT // 2) % tiles
                if number // IMG_SPLIT != slot:
                    continue
                for step in range(WINDOW):
                    block = window_start(number % IMG_SPLIT) + step
                    if block < 0 or block >= blocks:
                        continue
                    place = feature_rows + at * WINDOW + step
                    msg[tile, place : place + 1, :] = total[:, block * LANES : (block + 1) * LANES]

    queries = q_ref[...].astype(jnp.float32)
    by_head[...] = jnp.zeros_like(by_head)
    for r in range(rows):
        for head in range(heads):
            by_head[r * heads + head : r * heads + head + 1, :] = queries[
                r : r + 1, head * LANES : (head + 1) * LANES
            ]
    turned = by_head[...].T
    column = lax.broadcasted_iota(jnp.int32, (1, LANES), 1)
    for head in range(heads):
        spread[head * LANES : (head + 1) * LANES, :] = jnp.where(
            column % heads == head, turned, 0.0
        ).astype(jnp.bfloat16)
    padding = jnp.zeros((16 - rows, width), jnp.float32)
    known = rows * cached
    k_ref[known:, :] = jnp.concatenate([nk_ref[...].astype(jnp.float32), padding], 0).astype(
        jnp.bfloat16
    )
    new_values = jnp.concatenate([nv_ref[...].astype(jnp.float32), padding], 0).astype(jnp.bfloat16)
    for copy in values:
        copy.start()
    for copy in keys:
        copy.wait()
    products = jnp.dot(k_ref[...], spread[...], preferred_element_type=jnp.float32) * factor
    own_scores = products[known:]
    scores = products[:known]
    owner = column // heads
    own_at = lax.broadcasted_iota(jnp.int32, own_scores.shape, 0) == owner
    own_score = jnp.sum(jnp.where(own_at, own_scores, 0.0), 0, keepdims=True)
    limit = jnp.zeros(column.shape, jnp.int32)
    for r in range(rows):
        limit = jnp.where(owner == r, lengths[r], limit)
    position = lax.broadcasted_iota(jnp.int32, scores.shape, 0) - owner * cached
    live = (position >= 0) & (position < limit)
    scores = jnp.where(live, scores, jnp.float32(-1e30))
    highest = jnp.maximum(jnp.max(scores, 0, keepdims=True), own_score)
    cache_exp = jnp.where(live, jnp.exp(scores - highest), 0.0)
    own_exp = jnp.exp(own_score - highest)
    denom = jnp.sum(cache_exp, 0, keepdims=True) + own_exp
    cache_weight = (cache_exp / denom).T[: rows * heads].astype(jnp.bfloat16)
    own_weight = jnp.where(own_at, own_exp / denom, 0.0)
    own_weight = jnp.concatenate(
        [own_weight, jnp.zeros((LANES - own_weight.shape[0], LANES), jnp.float32)], 0
    ).T[: rows * heads, :16].astype(jnp.bfloat16)
    for copy in values:
        copy.wait()
    attended = jnp.dot(cache_weight, v_ref[...], preferred_element_type=jnp.float32) + jnp.dot(
        own_weight, new_values, preferred_element_type=jnp.float32
    )
    for tile in range(tiles):
        for r in range(rows):
            for step in range(per):
                head = member(tile, tiles) // 2 * per + step
                place = r * per + step
                msg[tile, place : place + 1, :] = attended[
                    r * heads + head : r * heads + head + 1, head * LANES : (head + 1) * LANES
                ]
    out_ref[...] = msg[...].astype(jnp.bfloat16)


def project_kernel(
    parity_ref,
    in_ref,
    own_ref,
    other_ref,
    two_any,
    out_ref,
    early_ref,
    held,
    total,
    sems,
    *,
    rows,
    per,
):
    copies = [
        pltpu.make_async_copy(two_any.at[dr, dc], early_ref.at[at], sems.at[at])
        for at, (dr, dc) in enumerate(TAPS[:EARLY])
    ]
    for copy in copies:
        copy.start()
    tiles, depth = in_ref.shape[:2]
    held[...] = in_ref[...].astype(jnp.float32).reshape(held.shape)
    groups = total.shape[0]
    lines = out_ref.shape[2] // rows
    share = own_ref.shape[0]
    lhs = []
    for row in range(rows):
        parts = [held[pl.ds(row * per + j, tiles, stride=depth), :] for j in range(per)]
        lhs.append(jnp.concatenate(parts, 1))
    lhs = jnp.concatenate(lhs, 0)
    even = parity_ref[0] == 0
    first, second = lhs[:, :share], lhs[:, share:]
    own = jnp.where(even, first, second).astype(jnp.bfloat16)
    other = jnp.where(even, second, first).astype(jnp.bfloat16)
    half = own_ref.shape[1]
    begin = pl.multiple_of(parity_ref[0] * half, LANES)
    product = jnp.dot(own, own_ref[...], preferred_element_type=jnp.float32) + jnp.dot(
        other, other_ref[:, pl.ds(begin, half)], preferred_element_type=jnp.float32
    )
    for row in range(rows):
        for group in range(groups):
            for line in range(lines):
                begin = (group * lines + line) * LANES
                total[group, pl.ds(row * lines + line, tiles, stride=rows * lines), :] = product[
                    row * tiles : (row + 1) * tiles, begin : begin + LANES
                ]
    for group in range(groups):
        out_ref[:, group] = (
            total[group].astype(jnp.bfloat16).reshape(tiles, rows * lines, LANES)
        )
    for copy in copies:
        copy.wait()


def total_kernel(in_ref, out_ref, held, *, rows):
    tiles, groups, depth, _ = in_ref.shape
    lines = depth // rows
    parts = in_ref[...].astype(jnp.float32).reshape(tiles // 2, 2 * groups, depth, LANES)
    held[...] = jnp.sum(parts, 0)
    for group in range(2 * groups):
        for line in range(lines):
            begin = (group * lines + line) * LANES
            out_ref[:, begin : begin + LANES] = held[
                group, pl.ds(line, rows, stride=lines), :
            ].astype(jnp.bfloat16)


def split_three(whole):
    high = whole.astype(jnp.bfloat16).astype(jnp.float32)
    middle = (whole - high).astype(jnp.bfloat16).astype(jnp.float32)
    return jnp.concatenate([high, middle, whole - high - middle], 0)


def fold_kernel(
    parity_ref, cw_ref, conv_ref, weight_ref, after_ref, out_ref, near_ref, levels_w, folded, held, sems, near_sem
):
    del after_ref
    taps = [(dr, dc) for dr in range(3) for dc in range(3)]
    copies = [
        pltpu.make_async_copy(conv_ref.at[dr, dc], held.at[at], sems.at[at])
        for at, (dr, dc) in enumerate(taps)
    ]
    for copy in copies:
        copy.start()
    begin = pl.multiple_of(parity_ref[0] * near_ref.shape[1], LANES)
    bring = pltpu.make_async_copy(
        weight_ref.at[:, pl.ds(begin, near_ref.shape[1])], near_ref, near_sem
    )
    bring.start()
    levels_w[...] = jnp.zeros_like(levels_w)
    levels_w[0:FSQ_DIMS, :] = cw_ref[...]
    left = split_three(levels_w[...]).astype(jnp.bfloat16)
    folded[...] = jnp.zeros_like(folded)
    for at, copy in enumerate(copies):
        copy.wait()
        parts = jnp.dot(left, held[at], preferred_element_type=jnp.float32)
        total = parts[0:8] + parts[8:16] + parts[16:24]
        folded[at * TAP_ROWS : (at + 1) * TAP_ROWS, :] = split_three(total)
    out_ref[...] = folded[...].astype(jnp.bfloat16)
    bring.wait()


def decode_kernel(
    section_ref, in_ref, fold_ref, early_ref, two_any, out_ref, late_ref, sems, *, feature_rows
):
    copies = [
        pltpu.make_async_copy(two_any.at[dr, dc], late_ref.at[at], sems.at[at])
        for at, (dr, dc) in enumerate(TAPS[EARLY:])
    ]
    for copy in copies:
        copy.start()
    section = section_ref[0]
    got = jnp.sum(in_ref[...].astype(jnp.float32), 0)
    pieces = []
    for at in range(PIECES):
        lines = [
            got[feature_rows + at * WINDOW + step : feature_rows + at * WINDOW + step + 1]
            for step in range(WINDOW)
        ]
        pieces.append(jnp.concatenate(lines, 1))
    codes = decode_number(jnp.concatenate(pieces, 1))
    span = codes.shape[1]
    depth = fold_ref.shape[0]
    level = lax.broadcasted_iota(jnp.int32, (8, span), 0)
    taken = level < FSQ_DIMS
    shift = jnp.where(taken, level * 3, 0)
    value = (2 * ((jnp.broadcast_to(codes, (8, span)) >> shift) & 7) - 7).astype(
        jnp.float32
    ) * 0.125
    value = jnp.where(taken, value, 0.0)
    value = jnp.concatenate([value] * (depth // 8), 0).astype(jnp.bfloat16)

    count = TILE_ROWS * IMG_W
    begin = TILE_H * ROW_WORDS * section - HALO * ROW_WORDS
    offset = begin & (LANES - 1)
    spot = lax.broadcasted_iota(jnp.int32, (count, 1), 0)
    line = spot // IMG_W + TILE_H * section - HALO
    inside = (line >= 0) & (line < IMG_SPLIT * TILE_H)
    target = jnp.where(inside, (spot >> 1) + offset + (span // 2) * (spot & 1), -1)
    chooser = jnp.where(
        lax.broadcasted_iota(jnp.int32, (count, span), 1) == target, 1.0, 0.0
    ).astype(jnp.bfloat16)
    placed = lax.dot_general(
        chooser, value, (((1,), (1,)), ((), ())), preferred_element_type=jnp.float32
    )
    column = spot % IMG_W
    moved = [
        jnp.where(column == 0, 0.0, pltpu.roll(placed, 1, 0)),
        placed,
        jnp.where(column == IMG_W - 1, 0.0, pltpu.roll(placed, count - 1, 0)),
    ]
    count = count - 2 * IMG_W
    tap_of = lax.broadcasted_iota(jnp.int32, (1, depth), 1) // TAP_ROWS
    taps = jnp.zeros((count, depth), jnp.float32)
    for dr in range(3):
        for dc in range(3):
            taps = jnp.where(
                tap_of == 3 * dr + dc, moved[dc][dr * IMG_W : dr * IMG_W + count], taps
            )
    hidden = jnp.dot(taps.astype(jnp.bfloat16), fold_ref[...], preferred_element_type=jnp.float32)

    line = lax.broadcasted_iota(jnp.int32, (count, 1), 0) // IMG_W + TILE_H * section - 1
    inside = (line >= 0) & (line < IMG_SPLIT * TILE_H)
    activated = jnp.where(inside, hidden * jax.nn.sigmoid(hidden), 0.0).astype(jnp.bfloat16)

    count = count - 2 * IMG_W
    column = lax.broadcasted_iota(jnp.int32, (count, 1), 0) % IMG_W
    summed = part = None
    for at, (dr, dc) in enumerate(TAPS):
        if at >= EARLY:
            copies[at - EARLY].wait()
        weight = early_ref[at] if at < EARLY else late_ref[at - EARLY]
        term = jnp.dot(
            activated[dr * IMG_W : dr * IMG_W + count], weight, preferred_element_type=jnp.float32
        )
        part = term if part is None else part + term
        if dr < 2:
            continue
        if dc == 0:
            part = jnp.where(column == 0, 0.0, pltpu.roll(part, 1, 0))
        if dc == 2:
            part = jnp.where(column == IMG_W - 1, 0.0, pltpu.roll(part, count - 1, 0))
        summed = part if summed is None else summed + part
        part = None
    out_ref[...] = summed.astype(jnp.bfloat16)


def near(array):
    return pltpu.with_memory_space_constraint(array, pltpu.VMEM)


def far(array):
    return pltpu.with_memory_space_constraint(array, pltpu.HBM)


def on_device(
    queries,
    new_keys,
    new_values,
    cache_keys,
    cache_values,
    cache_lengths,
    out_weight,
    codes,
    tile_slot,
    code_weight,
    conv_one,
    conv_two,
):
    tiles = lax.axis_size("rows")
    place = lax.axis_index("rows")
    rows, width = queries.shape
    channels = code_weight.shape[1]
    share = width // tiles
    per = 2 * share // LANES
    feature_rows = rows * per
    depth = message_rows(feature_rows)
    half = width // 2
    lines = 8
    groups = half // (lines * LANES)
    params = pltpu.CompilerParams(vmem_limit_bytes=VMEM_LIMIT)
    smem = pl.BlockSpec(memory_space=pltpu.SMEM)
    vmem = pl.BlockSpec(memory_space=pltpu.VMEM)
    anywhere = pl.BlockSpec(memory_space=pl.ANY)
    parity = (place % 2).reshape(1).astype(jnp.int32)

    outgoing = pl.pallas_call(
        functools.partial(attend_kernel, tiles=tiles, per=per, feature_rows=feature_rows),
        in_specs=[smem] * 2 + [anywhere] * 6,
        out_specs=vmem,
        out_shape=jax.ShapeDtypeStruct((tiles, depth, LANES), jnp.bfloat16),
        scratch_shapes=[
            pltpu.VMEM(queries.shape, queries.dtype),
            pltpu.VMEM(new_keys.shape, new_keys.dtype),
            pltpu.VMEM(new_values.shape, new_values.dtype),
            pltpu.VMEM((rows * cache_keys.shape[1] + 16, width), cache_keys.dtype),
            pltpu.VMEM((rows * cache_values.shape[1], width), cache_values.dtype),
            pltpu.VMEM(codes.shape, codes.dtype),
            pltpu.VMEM((tiles, depth, LANES), jnp.float32),
            pltpu.VMEM((LANES, LANES), jnp.float32),
            pltpu.VMEM((width, LANES), jnp.bfloat16),
            pltpu.SemaphoreType.DMA((4 + 2 * rows,)),
        ],
        compiler_params=pltpu.CompilerParams(vmem_limit_bytes=56 * 1024 * 1024),
    )(
        cache_lengths,
        tile_slot,
        far(queries),
        far(new_keys),
        far(new_values),
        far(cache_keys),
        far(cache_values),
        far(codes),
    )
    order = [[member(at, tiles) for at in range(tiles)]]
    incoming = lax.all_to_all(
        outgoing, "rows", split_axis=0, concat_axis=0, axis_index_groups=order, tiled=True
    )
    other = lax.ppermute(out_weight, "rows", [(i, i ^ 1) for i in range(tiles)])

    folded, own = pl.pallas_call(
        fold_kernel,
        in_specs=[smem, vmem, anywhere, anywhere, anywhere],
        out_specs=[vmem, vmem],
        out_shape=[
            jax.ShapeDtypeStruct((FOLD_ROWS, channels), jnp.bfloat16),
            pltpu.VMEM((share, half), out_weight.dtype),
        ],
        scratch_shapes=[
            pltpu.VMEM((8, channels), jnp.float32),
            pltpu.VMEM((FOLD_ROWS, channels), jnp.float32),
            pltpu.VMEM((9,) + conv_one.shape[2:], conv_one.dtype),
            pltpu.SemaphoreType.DMA((9,)),
            pltpu.SemaphoreType.DMA,
        ],
        compiler_params=params,
    )(parity, far(code_weight), far(conv_one), far(out_weight), near(outgoing))

    partials, early = pl.pallas_call(
        functools.partial(project_kernel, rows=rows, per=per),
        in_specs=[smem, vmem, vmem, vmem, anywhere],
        out_specs=[vmem, vmem],
        out_shape=[
            jax.ShapeDtypeStruct((tiles, groups, rows * lines, LANES), jnp.bfloat16),
            pltpu.VMEM((EARLY,) + conv_two.shape[2:], conv_two.dtype),
        ],
        scratch_shapes=[
            pltpu.VMEM((tiles * depth, LANES), jnp.float32),
            pltpu.VMEM((groups, tiles * rows * lines, LANES), jnp.float32),
            pltpu.SemaphoreType.DMA((EARLY,)),
        ],
        compiler_params=params,
    )(parity, near(incoming), near(own), near(other), far(conv_two))
    gathered = lax.all_to_all(
        partials, "rows", split_axis=0, concat_axis=0, axis_index_groups=order, tiled=True
    )

    section = (place + IMG_SPLIT // 2) % tiles % IMG_SPLIT
    decoded = pl.pallas_call(
        functools.partial(decode_kernel, feature_rows=feature_rows),
        in_specs=[smem, vmem, vmem, vmem, anywhere],
        out_specs=vmem,
        out_shape=jax.ShapeDtypeStruct((TILE_H * IMG_W, channels), jnp.bfloat16),
        scratch_shapes=[
            pltpu.VMEM((len(TAPS) - EARLY,) + conv_two.shape[2:], conv_two.dtype),
            pltpu.SemaphoreType.DMA((len(TAPS) - EARLY,)),
        ],
        compiler_params=params,
    )(section.reshape(1).astype(jnp.int32), near(incoming), near(folded), near(early), far(conv_two))

    mixed = pl.pallas_call(
        functools.partial(total_kernel, rows=rows),
        in_specs=[vmem],
        out_shape=jax.ShapeDtypeStruct((rows, width), jnp.bfloat16),
        scratch_shapes=[pltpu.VMEM((2 * groups, rows * lines, LANES), jnp.float32)],
        compiler_params=params,
    )(near(gathered))
    return (mixed, decoded.reshape(TILE_H, IMG_W, channels))


def solution(mesh):
    in_specs = (
        P(("groups", "rows"), None),
        P(("groups", "rows"), None),
        P(("groups", "rows"), None),
        P(("groups", "rows"), None, None),
        P(("groups", "rows"), None, None),
        P(("groups", "rows")),
        P("rows", None),
        P(("groups", "rows"), None),
        P(("groups", "rows")),
        P(),
        P(),
        P(),
    )
    out_specs = (P(("groups", "rows"), None), P(("groups", "rows"), None, None))
    return jax.shard_map(
        on_device, mesh=mesh, in_specs=in_specs, out_specs=out_specs, check_vma=False
    )
```

```python
import functools
import math

import jax
import jax.numpy as jnp
from jax import lax
from jax.experimental import pallas as pl
from jax.experimental.pallas import tpu as pltpu
from jax.sharding import PartitionSpec as P

HEAD_DIM = 128
FSQ_DIMS = 5
IMG_SPLIT = 4
TILE_H = 8
IMG_W = 48
LANES = 128
HALO = 2
ROW_WORDS = IMG_W // 2
TILE_ROWS = TILE_H + 2 * HALO
WINDOW = 3
PIECES = 2
CODE_ROWS = WINDOW * PIECES
TAP_ROWS = 24
FOLD_ROWS = 256
TAPS = [(dr, dc) for dc in (1, 0, 2) for dr in range(3)]
EARLY = 3
VMEM_LIMIT = 24 * 1024 * 1024


def window_start(section):
    return (TILE_H * ROW_WORDS * section - HALO * ROW_WORDS) // LANES


def member(at, tiles):
    return (at + tiles // 4 * 2) % tiles


def message_rows(features):
    return -(-(features + CODE_ROWS) // 16) * 16


def encode(code):
    fraction = (code & 127).astype(jnp.float32) * (1.0 / 128.0) + 1.0
    for bit in range(7):
        up = ((code >> (7 + bit)) & 1) == 1
        fraction = jnp.where(up, fraction * 2.0 ** (1 << bit), fraction)
        if bit == 5:
            fraction = fraction * 2.0**-64
    return jnp.where(((code >> 14) & 1) == 1, -fraction, fraction)


def decode_number(value):
    size = jnp.abs(value)
    code = jnp.where(value < 0.0, 1 << 14, 0)
    for bit in range(6, -1, -1):
        step = 1 << bit
        up = size >= 2.0 ** (step - 64)
        code = code + jnp.where(up, step << 7, 0)
        size = jnp.where(up, size * 2.0**-step, size)
    return code + ((size * 2.0**64 - 1.0) * 128.0).astype(jnp.int32)


def attend_kernel(
    lengths,
    slots,
    parity_ref,
    q_any,
    nk_any,
    nv_any,
    k_any,
    v_any,
    codes_any,
    weight_any,
    out_ref,
    give_ref,
    q_ref,
    nk_ref,
    nv_ref,
    k_ref,
    v_ref,
    codes_ref,
    msg,
    by_head,
    spread,
    sems,
    *,
    tiles,
    per,
    feature_rows,
):
    rows, width = q_ref.shape
    give_columns = give_ref.shape[1]
    small = [
        pltpu.make_async_copy(source, target, sems.at[at])
        for at, (source, target) in enumerate(
            ((q_any, q_ref), (nk_any, nk_ref), (nv_any, nv_ref), (codes_any, codes_ref))
        )
    ]
    cached = k_any.shape[1]
    keys, values = (
        [
            pltpu.make_async_copy(
                source.at[r], target.at[pl.ds(r * cached, cached)], sems.at[base + r]
            )
            for r in range(rows)
        ]
        for source, target, base in ((k_any, k_ref, 4), (v_any, v_ref, 4 + rows))
    )
    begin = pl.multiple_of((1 - parity_ref[0]) * give_columns, LANES)
    give = pltpu.make_async_copy(
        weight_any.at[:, pl.ds(begin, give_columns)], give_ref, sems.at[4 + 2 * rows]
    )
    for copy in small:
        copy.start()
    for copy in keys:
        copy.start()

    heads = width // HEAD_DIM
    factor = 1.0 / math.sqrt(HEAD_DIM)
    msg[...] = jnp.zeros_like(msg)
    for copy in small:
        copy.wait()

    words = codes_ref[...]
    blocks = words.shape[1] // LANES
    pieces = [encode(words & 32767), encode(words >> 15)]
    for slot in range(tiles // IMG_SPLIT):
        gains = [
            jnp.where(slots[r] == slot, 1.0, 0.0).astype(jnp.float32) for r in range(rows)
        ]
        for at, piece in enumerate(pieces):
            total = piece[0:1] * gains[0]
            for r in range(1, rows):
                total = total + piece[r : r + 1] * gains[r]
            for tile in range(tiles):
                number = (member(tile, tiles) + IMG_SPLIT // 2) % tiles
                if number // IMG_SPLIT != slot:
                    continue
                for step in range(WINDOW):
                    block = window_start(number % IMG_SPLIT) + step
                    if block < 0 or block >= blocks:
                        continue
                    place = feature_rows + at * WINDOW + step
                    msg[tile, place : place + 1, :] = total[:, block * LANES : (block + 1) * LANES]

    queries = q_ref[...].astype(jnp.float32)
    by_head[...] = jnp.zeros_like(by_head)
    for r in range(rows):
        for head in range(heads):
            by_head[r * heads + head : r * heads + head + 1, :] = queries[
                r : r + 1, head * LANES : (head + 1) * LANES
            ]
    turned = by_head[...].T
    column = lax.broadcasted_iota(jnp.int32, (1, LANES), 1)
    for head in range(heads):
        spread[head * LANES : (head + 1) * LANES, :] = jnp.where(
            column % heads == head, turned, 0.0
        ).astype(jnp.bfloat16)
    padding = jnp.zeros((16 - rows, width), jnp.float32)
    known = rows * cached
    k_ref[known:, :] = jnp.concatenate([nk_ref[...].astype(jnp.float32), padding], 0).astype(
        jnp.bfloat16
    )
    new_values = jnp.concatenate([nv_ref[...].astype(jnp.float32), padding], 0).astype(jnp.bfloat16)
    for copy in values:
        copy.start()
    for copy in keys:
        copy.wait()
    products = jnp.dot(k_ref[...], spread[...], preferred_element_type=jnp.float32) * factor
    give.start()
    own_scores = products[known:]
    scores = products[:known]
    owner = column // heads
    own_at = lax.broadcasted_iota(jnp.int32, own_scores.shape, 0) == owner
    own_score = jnp.sum(jnp.where(own_at, own_scores, 0.0), 0, keepdims=True)
    limit = jnp.zeros(column.shape, jnp.int32)
    for r in range(rows):
        limit = jnp.where(owner == r, lengths[r], limit)
    position = lax.broadcasted_iota(jnp.int32, scores.shape, 0) - owner * cached
    live = (position >= 0) & (position < limit)
    scores = jnp.where(live, scores, jnp.float32(-1e30))
    highest = jnp.maximum(jnp.max(scores, 0, keepdims=True), own_score)
    cache_exp = jnp.where(live, jnp.exp(scores - highest), 0.0)
    own_exp = jnp.exp(own_score - highest)
    denom = jnp.sum(cache_exp, 0, keepdims=True) + own_exp
    cache_weight = (cache_exp / denom).T[: rows * heads].astype(jnp.bfloat16)
    own_weight = jnp.where(own_at, own_exp / denom, 0.0)
    own_weight = jnp.concatenate(
        [own_weight, jnp.zeros((LANES - own_weight.shape[0], LANES), jnp.float32)], 0
    ).T[: rows * heads, :16].astype(jnp.bfloat16)
    for copy in values:
        copy.wait()
    attended = jnp.dot(cache_weight, v_ref[...], preferred_element_type=jnp.float32) + jnp.dot(
        own_weight, new_values, preferred_element_type=jnp.float32
    )
    for tile in range(tiles):
        for r in range(rows):
            for step in range(per):
                head = member(tile, tiles) // 2 * per + step
                place = r * per + step
                msg[tile, place : place + 1, :] = attended[
                    r * heads + head : r * heads + head + 1, head * LANES : (head + 1) * LANES
                ]
    out_ref[...] = msg[...].astype(jnp.bfloat16)
    give.wait()


def project_kernel(
    parity_ref,
    in_ref,
    own_ref,
    other_ref,
    two_any,
    out_ref,
    early_ref,
    held,
    total,
    sems,
    *,
    rows,
    per,
):
    copies = [
        pltpu.make_async_copy(two_any.at[dr, dc], early_ref.at[at], sems.at[at])
        for at, (dr, dc) in enumerate(TAPS[:EARLY])
    ]
    for copy in copies:
        copy.start()
    tiles, depth = in_ref.shape[:2]
    held[...] = in_ref[...].astype(jnp.float32).reshape(held.shape)
    groups = total.shape[0]
    lines = out_ref.shape[2] // rows
    share = own_ref.shape[0]
    lhs = []
    for row in range(rows):
        parts = [held[pl.ds(row * per + j, tiles, stride=depth), :] for j in range(per)]
        lhs.append(jnp.concatenate(parts, 1))
    lhs = jnp.concatenate(lhs, 0)
    even = parity_ref[0] == 0
    first, second = lhs[:, :share], lhs[:, share:]
    own = jnp.where(even, first, second).astype(jnp.bfloat16)
    other = jnp.where(even, second, first).astype(jnp.bfloat16)
    product = jnp.dot(own, own_ref[...], preferred_element_type=jnp.float32) + jnp.dot(
        other, other_ref[...], preferred_element_type=jnp.float32
    )
    for row in range(rows):
        for group in range(groups):
            for line in range(lines):
                begin = (group * lines + line) * LANES
                total[group, pl.ds(row * lines + line, tiles, stride=rows * lines), :] = product[
                    row * tiles : (row + 1) * tiles, begin : begin + LANES
                ]
    for group in range(groups):
        out_ref[:, group] = (
            total[group].astype(jnp.bfloat16).reshape(tiles, rows * lines, LANES)
        )
    for copy in copies:
        copy.wait()


def total_kernel(in_ref, out_ref, held, *, rows):
    tiles, groups, depth, _ = in_ref.shape
    lines = depth // rows
    parts = in_ref[...].astype(jnp.float32).reshape(tiles // 2, 2 * groups, depth, LANES)
    held[...] = jnp.sum(parts, 0)
    for group in range(2 * groups):
        for line in range(lines):
            begin = (group * lines + line) * LANES
            out_ref[:, begin : begin + LANES] = held[
                group, pl.ds(line, rows, stride=lines), :
            ].astype(jnp.bfloat16)


def split_three(whole):
    high = whole.astype(jnp.bfloat16).astype(jnp.float32)
    middle = (whole - high).astype(jnp.bfloat16).astype(jnp.float32)
    return jnp.concatenate([high, middle, whole - high - middle], 0)


def fold_kernel(
    parity_ref, cw_ref, conv_ref, weight_ref, after_ref, out_ref, near_ref, levels_w, folded, held, sems, near_sem
):
    del after_ref
    taps = [(dr, dc) for dr in range(3) for dc in range(3)]
    copies = [
        pltpu.make_async_copy(conv_ref.at[dr, dc], held.at[at], sems.at[at])
        for at, (dr, dc) in enumerate(taps)
    ]
    for copy in copies:
        copy.start()
    begin = pl.multiple_of(parity_ref[0] * near_ref.shape[1], LANES)
    bring = pltpu.make_async_copy(
        weight_ref.at[:, pl.ds(begin, near_ref.shape[1])], near_ref, near_sem
    )
    bring.start()
    levels_w[...] = jnp.zeros_like(levels_w)
    levels_w[0:FSQ_DIMS, :] = cw_ref[...]
    left = split_three(levels_w[...]).astype(jnp.bfloat16)
    folded[...] = jnp.zeros_like(folded)
    for at, copy in enumerate(copies):
        copy.wait()
        parts = jnp.dot(left, held[at], preferred_element_type=jnp.float32)
        total = parts[0:8] + parts[8:16] + parts[16:24]
        folded[at * TAP_ROWS : (at + 1) * TAP_ROWS, :] = split_three(total)
    out_ref[...] = folded[...].astype(jnp.bfloat16)
    bring.wait()


def decode_kernel(
    section_ref,
    in_ref,
    fold_ref,
    early_ref,
    two_any,
    after_ref,
    out_ref,
    late_ref,
    sems,
    *,
    feature_rows,
):
    del after_ref
    copies = [
        pltpu.make_async_copy(two_any.at[dr, dc], late_ref.at[at], sems.at[at])
        for at, (dr, dc) in enumerate(TAPS[EARLY:])
    ]
    for copy in copies:
        copy.start()
    section = section_ref[0]
    got = jnp.sum(in_ref[...].astype(jnp.float32), 0)
    pieces = []
    for at in range(PIECES):
        lines = [
            got[feature_rows + at * WINDOW + step : feature_rows + at * WINDOW + step + 1]
            for step in range(WINDOW)
        ]
        pieces.append(jnp.concatenate(lines, 1))
    codes = decode_number(jnp.concatenate(pieces, 1))
    span = codes.shape[1]
    depth = fold_ref.shape[0]
    level = lax.broadcasted_iota(jnp.int32, (8, span), 0)
    taken = level < FSQ_DIMS
    shift = jnp.where(taken, level * 3, 0)
    value = (2 * ((jnp.broadcast_to(codes, (8, span)) >> shift) & 7) - 7).astype(
        jnp.float32
    ) * 0.125
    value = jnp.where(taken, value, 0.0)
    value = jnp.concatenate([value] * (depth // 8), 0).astype(jnp.bfloat16)

    count = TILE_ROWS * IMG_W
    begin = TILE_H * ROW_WORDS * section - HALO * ROW_WORDS
    offset = begin & (LANES - 1)
    spot = lax.broadcasted_iota(jnp.int32, (count, 1), 0)
    line = spot // IMG_W + TILE_H * section - HALO
    inside = (line >= 0) & (line < IMG_SPLIT * TILE_H)
    target = jnp.where(inside, (spot >> 1) + offset + (span // 2) * (spot & 1), -1)
    chooser = jnp.where(
        lax.broadcasted_iota(jnp.int32, (count, span), 1) == target, 1.0, 0.0
    ).astype(jnp.bfloat16)
    placed = lax.dot_general(
        chooser, value, (((1,), (1,)), ((), ())), preferred_element_type=jnp.float32
    )
    column = spot % IMG_W
    moved = [
        jnp.where(column == 0, 0.0, pltpu.roll(placed, 1, 0)),
        placed,
        jnp.where(column == IMG_W - 1, 0.0, pltpu.roll(placed, count - 1, 0)),
    ]
    count = count - 2 * IMG_W
    tap_of = lax.broadcasted_iota(jnp.int32, (1, depth), 1) // TAP_ROWS
    taps = jnp.zeros((count, depth), jnp.float32)
    for dr in range(3):
        for dc in range(3):
            taps = jnp.where(
                tap_of == 3 * dr + dc, moved[dc][dr * IMG_W : dr * IMG_W + count], taps
            )
    hidden = jnp.dot(taps.astype(jnp.bfloat16), fold_ref[...], preferred_element_type=jnp.float32)

    line = lax.broadcasted_iota(jnp.int32, (count, 1), 0) // IMG_W + TILE_H * section - 1
    inside = (line >= 0) & (line < IMG_SPLIT * TILE_H)
    activated = jnp.where(inside, hidden * jax.nn.sigmoid(hidden), 0.0).astype(jnp.bfloat16)

    count = count - 2 * IMG_W
    column = lax.broadcasted_iota(jnp.int32, (count, 1), 0) % IMG_W
    summed = part = None
    for at, (dr, dc) in enumerate(TAPS):
        if at == EARLY:
            for copy in copies:
                copy.wait()
        weight = early_ref[at] if at < EARLY else late_ref[at - EARLY]
        term = jnp.dot(
            activated[dr * IMG_W : dr * IMG_W + count], weight, preferred_element_type=jnp.float32
        )
        part = term if part is None else part + term
        if dr < 2:
            continue
        if dc == 0:
            part = jnp.where(column == 0, 0.0, pltpu.roll(part, 1, 0))
        if dc == 2:
            part = jnp.where(column == IMG_W - 1, 0.0, pltpu.roll(part, count - 1, 0))
        summed = part if summed is None else summed + part
        part = None
    out_ref[...] = summed.astype(jnp.bfloat16)


def near(array):
    return pltpu.with_memory_space_constraint(array, pltpu.VMEM)


def far(array):
    return pltpu.with_memory_space_constraint(array, pltpu.HBM)


def on_device(
    queries,
    new_keys,
    new_values,
    cache_keys,
    cache_values,
    cache_lengths,
    out_weight,
    codes,
    tile_slot,
    code_weight,
    conv_one,
    conv_two,
):
    tiles = lax.axis_size("rows")
    place = lax.axis_index("rows")
    rows, width = queries.shape
    channels = code_weight.shape[1]
    share = width // tiles
    per = 2 * share // LANES
    feature_rows = rows * per
    depth = message_rows(feature_rows)
    half = width // 2
    lines = 8
    groups = half // (lines * LANES)
    params = pltpu.CompilerParams(vmem_limit_bytes=VMEM_LIMIT)
    smem = pl.BlockSpec(memory_space=pltpu.SMEM)
    vmem = pl.BlockSpec(memory_space=pltpu.VMEM)
    anywhere = pl.BlockSpec(memory_space=pl.ANY)
    parity = (place % 2).reshape(1).astype(jnp.int32)

    outgoing, give = pl.pallas_call(
        functools.partial(attend_kernel, tiles=tiles, per=per, feature_rows=feature_rows),
        in_specs=[smem] * 3 + [anywhere] * 7,
        out_specs=[vmem, vmem],
        out_shape=[
            pltpu.VMEM((tiles, depth, LANES), jnp.bfloat16),
            pltpu.VMEM((share, half), out_weight.dtype),
        ],
        scratch_shapes=[
            pltpu.VMEM(queries.shape, queries.dtype),
            pltpu.VMEM(new_keys.shape, new_keys.dtype),
            pltpu.VMEM(new_values.shape, new_values.dtype),
            pltpu.VMEM((rows * cache_keys.shape[1] + 16, width), cache_keys.dtype),
            pltpu.VMEM((rows * cache_values.shape[1], width), cache_values.dtype),
            pltpu.VMEM(codes.shape, codes.dtype),
            pltpu.VMEM((tiles, depth, LANES), jnp.float32),
            pltpu.VMEM((LANES, LANES), jnp.float32),
            pltpu.VMEM((width, LANES), jnp.bfloat16),
            pltpu.SemaphoreType.DMA((5 + 2 * rows,)),
        ],
        compiler_params=pltpu.CompilerParams(vmem_limit_bytes=56 * 1024 * 1024),
    )(
        cache_lengths,
        tile_slot,
        parity,
        far(queries),
        far(new_keys),
        far(new_values),
        far(cache_keys),
        far(cache_values),
        far(codes),
        far(out_weight),
    )
    order = [[member(at, tiles) for at in range(tiles)]]
    incoming = lax.all_to_all(
        outgoing, "rows", split_axis=0, concat_axis=0, axis_index_groups=order, tiled=True
    )
    other = lax.ppermute(give, "rows", [(i, i ^ 1) for i in range(tiles)])

    folded, own = pl.pallas_call(
        fold_kernel,
        in_specs=[smem, vmem, anywhere, anywhere, anywhere],
        out_specs=[vmem, vmem],
        out_shape=[
            jax.ShapeDtypeStruct((FOLD_ROWS, channels), jnp.bfloat16),
            pltpu.VMEM((share, half), out_weight.dtype),
        ],
        scratch_shapes=[
            pltpu.VMEM((8, channels), jnp.float32),
            pltpu.VMEM((FOLD_ROWS, channels), jnp.float32),
            pltpu.VMEM((9,) + conv_one.shape[2:], conv_one.dtype),
            pltpu.SemaphoreType.DMA((9,)),
            pltpu.SemaphoreType.DMA,
        ],
        compiler_params=params,
    )(parity, far(code_weight), far(conv_one), far(out_weight), near(outgoing))

    partials, early = pl.pallas_call(
        functools.partial(project_kernel, rows=rows, per=per),
        in_specs=[smem, vmem, vmem, vmem, anywhere],
        out_specs=[vmem, vmem],
        out_shape=[
            pltpu.VMEM((tiles, groups, rows * lines, LANES), jnp.bfloat16),
            pltpu.VMEM((EARLY,) + conv_two.shape[2:], conv_two.dtype),
        ],
        scratch_shapes=[
            pltpu.VMEM((tiles * depth, LANES), jnp.float32),
            pltpu.VMEM((groups, tiles * rows * lines, LANES), jnp.float32),
            pltpu.SemaphoreType.DMA((EARLY,)),
        ],
        compiler_params=params,
    )(parity, near(incoming), near(own), near(other), far(conv_two))
    gathered = lax.all_to_all(
        partials, "rows", split_axis=0, concat_axis=0, axis_index_groups=order, tiled=True
    )

    section = (place + IMG_SPLIT // 2) % tiles % IMG_SPLIT
    decoded = pl.pallas_call(
        functools.partial(decode_kernel, feature_rows=feature_rows),
        in_specs=[smem, vmem, vmem, vmem, anywhere, anywhere],
        out_specs=vmem,
        out_shape=jax.ShapeDtypeStruct((TILE_H * IMG_W, channels), jnp.bfloat16),
        scratch_shapes=[
            pltpu.VMEM((len(TAPS) - EARLY,) + conv_two.shape[2:], conv_two.dtype),
            pltpu.SemaphoreType.DMA((len(TAPS) - EARLY,)),
        ],
        compiler_params=params,
    )(section.reshape(1).astype(jnp.int32), near(incoming), near(folded), near(early), far(conv_two), near(partials))

    mixed = pl.pallas_call(
        functools.partial(total_kernel, rows=rows),
        in_specs=[vmem],
        out_shape=jax.ShapeDtypeStruct((rows, width), jnp.bfloat16),
        scratch_shapes=[pltpu.VMEM((2 * groups, rows * lines, LANES), jnp.float32)],
        compiler_params=params,
    )(near(gathered))
    return (mixed, decoded.reshape(TILE_H, IMG_W, channels))


def solution(mesh):
    in_specs = (
        P(("groups", "rows"), None),
        P(("groups", "rows"), None),
        P(("groups", "rows"), None),
        P(("groups", "rows"), None, None),
        P(("groups", "rows"), None, None),
        P(("groups", "rows")),
        P("rows", None),
        P(("groups", "rows"), None),
        P(("groups", "rows")),
        P(),
        P(),
        P(),
    )
    out_specs = (P(("groups", "rows"), None), P(("groups", "rows"), None, None))
    return jax.shard_map(
        on_device, mesh=mesh, in_specs=in_specs, out_specs=out_specs, check_vma=False
    )
```

```python
import functools
import math

import jax
import jax.numpy as jnp
from jax import lax
from jax.experimental import pallas as pl
from jax.experimental.pallas import tpu as pltpu
from jax.sharding import PartitionSpec as P

HEAD_DIM = 128
FSQ_DIMS = 5
IMG_SPLIT = 4
TILE_H = 8
IMG_W = 48
LANES = 128
HALO = 2
ROW_WORDS = IMG_W // 2
TILE_ROWS = TILE_H + 2 * HALO
WINDOW = 3
PIECES = 2
CODE_ROWS = WINDOW * PIECES
TAP_ROWS = 24
FOLD_ROWS = 256
TAPS = [(dr, dc) for dc in (1, 0, 2) for dr in range(3)]
EARLY = 3


def window_start(section):
    return (TILE_H * ROW_WORDS * section - HALO * ROW_WORDS) // LANES


def member(at, tiles):
    return (at + tiles // 4 * 2) % tiles


def message_rows(features):
    return -(-(features + CODE_ROWS) // 16) * 16


def encode(code):
    fraction = (code & 127).astype(jnp.float32) * (1.0 / 128.0) + 1.0
    for bit in range(7):
        up = ((code >> (7 + bit)) & 1) == 1
        fraction = jnp.where(up, fraction * 2.0 ** (1 << bit), fraction)
        if bit == 5:
            fraction = fraction * 2.0**-64
    return jnp.where(((code >> 14) & 1) == 1, -fraction, fraction)


def decode_number(value):
    size = jnp.abs(value)
    code = jnp.where(value < 0.0, 1 << 14, 0)
    for bit in range(6, -1, -1):
        step = 1 << bit
        up = size >= 2.0 ** (step - 64)
        code = code + jnp.where(up, step << 7, 0)
        size = jnp.where(up, size * 2.0**-step, size)
    return code + ((size * 2.0**64 - 1.0) * 128.0).astype(jnp.int32)


def attend_kernel(
    lengths,
    slots,
    parity_ref,
    q_any,
    nk_any,
    nv_any,
    k_any,
    v_any,
    codes_any,
    weight_any,
    out_ref,
    give_ref,
    q_ref,
    nk_ref,
    nv_ref,
    k_ref,
    v_ref,
    codes_ref,
    msg,
    by_head,
    spread,
    sems,
    *,
    tiles,
    per,
    feature_rows,
):
    rows, width = q_ref.shape
    give_columns = give_ref.shape[1]
    small = [
        pltpu.make_async_copy(source, target, sems.at[at])
        for at, (source, target) in enumerate(
            ((q_any, q_ref), (nk_any, nk_ref), (nv_any, nv_ref), (codes_any, codes_ref))
        )
    ]
    cached = k_any.shape[1]
    keys, values = (
        [
            pltpu.make_async_copy(
                source.at[r], target.at[pl.ds(r * cached, cached)], sems.at[base + r]
            )
            for r in range(rows)
        ]
        for source, target, base in ((k_any, k_ref, 4), (v_any, v_ref, 4 + rows))
    )
    begin = pl.multiple_of((1 - parity_ref[0]) * give_columns, LANES)
    give = pltpu.make_async_copy(
        weight_any.at[:, pl.ds(begin, give_columns)], give_ref, sems.at[4 + 2 * rows]
    )
    for copy in small:
        copy.start()
    for copy in keys:
        copy.start()

    heads = width // HEAD_DIM
    factor = 1.0 / math.sqrt(HEAD_DIM)
    msg[...] = jnp.zeros_like(msg)
    for copy in small:
        copy.wait()

    words = codes_ref[...]
    blocks = words.shape[1] // LANES
    pieces = [encode(words & 32767), encode(words >> 15)]
    for slot in range(tiles // IMG_SPLIT):
        gains = [
            jnp.where(slots[r] == slot, 1.0, 0.0).astype(jnp.float32) for r in range(rows)
        ]
        for at, piece in enumerate(pieces):
            total = piece[0:1] * gains[0]
            for r in range(1, rows):
                total = total + piece[r : r + 1] * gains[r]
            for tile in range(tiles):
                number = (member(tile, tiles) + IMG_SPLIT // 2) % tiles
                if number // IMG_SPLIT != slot:
                    continue
                for step in range(WINDOW):
                    block = window_start(number % IMG_SPLIT) + step
                    if block < 0 or block >= blocks:
                        continue
                    place = feature_rows + at * WINDOW + step
                    msg[tile, place : place + 1, :] = total[:, block * LANES : (block + 1) * LANES]

    queries = q_ref[...].astype(jnp.float32)
    by_head[...] = jnp.zeros_like(by_head)
    for r in range(rows):
        for head in range(heads):
            by_head[r * heads + head : r * heads + head + 1, :] = queries[
                r : r + 1, head * LANES : (head + 1) * LANES
            ]
    turned = by_head[...].T
    column = lax.broadcasted_iota(jnp.int32, (1, LANES), 1)
    for head in range(heads):
        spread[head * LANES : (head + 1) * LANES, :] = jnp.where(
            column % heads == head, turned, 0.0
        ).astype(jnp.bfloat16)
    padding = jnp.zeros((16 - rows, width), jnp.float32)
    known = rows * cached
    k_ref[known:, :] = jnp.concatenate([nk_ref[...].astype(jnp.float32), padding], 0).astype(
        jnp.bfloat16
    )
    new_values = jnp.concatenate([nv_ref[...].astype(jnp.float32), padding], 0).astype(jnp.bfloat16)
    for copy in values:
        copy.start()
    for copy in keys:
        copy.wait()
    products = jnp.dot(k_ref[...], spread[...], preferred_element_type=jnp.float32) * factor
    give.start()
    own_scores = products[known:]
    scores = products[:known]
    owner = column // heads
    own_at = lax.broadcasted_iota(jnp.int32, own_scores.shape, 0) == owner
    own_score = jnp.sum(jnp.where(own_at, own_scores, 0.0), 0, keepdims=True)
    limit = jnp.zeros(column.shape, jnp.int32)
    for r in range(rows):
        limit = jnp.where(owner == r, lengths[r], limit)
    position = lax.broadcasted_iota(jnp.int32, scores.shape, 0) - owner * cached
    live = (position >= 0) & (position < limit)
    scores = jnp.where(live, scores, jnp.float32(-1e30))
    highest = jnp.maximum(jnp.max(scores, 0, keepdims=True), own_score)
    cache_exp = jnp.where(live, jnp.exp(scores - highest), 0.0)
    own_exp = jnp.exp(own_score - highest)
    denom = jnp.sum(cache_exp, 0, keepdims=True) + own_exp
    cache_weight = (cache_exp / denom).T[: rows * heads].astype(jnp.bfloat16)
    own_weight = jnp.where(own_at, own_exp / denom, 0.0)
    own_weight = jnp.concatenate(
        [own_weight, jnp.zeros((LANES - own_weight.shape[0], LANES), jnp.float32)], 0
    ).T[: rows * heads, :16].astype(jnp.bfloat16)
    for copy in values:
        copy.wait()
    attended = jnp.dot(cache_weight, v_ref[...], preferred_element_type=jnp.float32) + jnp.dot(
        own_weight, new_values, preferred_element_type=jnp.float32
    )
    for tile in range(tiles):
        for r in range(rows):
            for step in range(per):
                head = member(tile, tiles) // 2 * per + step
                place = r * per + step
                msg[tile, place : place + 1, :] = attended[
                    r * heads + head : r * heads + head + 1, head * LANES : (head + 1) * LANES
                ]
    out_ref[...] = msg[...].astype(jnp.bfloat16)
    give.wait()


def project_kernel(
    parity_ref,
    in_ref,
    own_ref,
    other_ref,
    two_any,
    out_ref,
    early_ref,
    held,
    total,
    sems,
    *,
    rows,
    per,
):
    copies = [
        pltpu.make_async_copy(two_any.at[dr, dc], early_ref.at[at], sems.at[at])
        for at, (dr, dc) in enumerate(TAPS[:EARLY])
    ]
    for copy in copies:
        copy.start()
    tiles, depth = in_ref.shape[:2]
    held[...] = in_ref[...].astype(jnp.float32).reshape(held.shape)
    groups = total.shape[0]
    lines = out_ref.shape[2] // rows
    share = own_ref.shape[0]
    lhs = []
    for row in range(rows):
        parts = [held[pl.ds(row * per + j, tiles, stride=depth), :] for j in range(per)]
        lhs.append(jnp.concatenate(parts, 1))
    lhs = jnp.concatenate(lhs, 0)
    even = parity_ref[0] == 0
    first, second = lhs[:, :share], lhs[:, share:]
    own = jnp.where(even, first, second).astype(jnp.bfloat16)
    other = jnp.where(even, second, first).astype(jnp.bfloat16)
    product = jnp.dot(own, own_ref[...], preferred_element_type=jnp.float32) + jnp.dot(
        other, other_ref[...], preferred_element_type=jnp.float32
    )
    for row in range(rows):
        for group in range(groups):
            for line in range(lines):
                begin = (group * lines + line) * LANES
                total[group, pl.ds(row * lines + line, tiles, stride=rows * lines), :] = product[
                    row * tiles : (row + 1) * tiles, begin : begin + LANES
                ]
    for group in range(groups):
        out_ref[:, group] = (
            total[group].astype(jnp.bfloat16).reshape(tiles, rows * lines, LANES)
        )
    for copy in copies:
        copy.wait()


def total_kernel(in_ref, out_ref, held, *, rows):
    tiles, groups, depth, _ = in_ref.shape
    lines = depth // rows
    parts = in_ref[...].astype(jnp.float32).reshape(tiles // 2, 2 * groups, depth, LANES)
    held[...] = jnp.sum(parts, 0)
    for group in range(2 * groups):
        for line in range(lines):
            begin = (group * lines + line) * LANES
            out_ref[:, begin : begin + LANES] = held[
                group, pl.ds(line, rows, stride=lines), :
            ].astype(jnp.bfloat16)


def split_three(whole):
    high = whole.astype(jnp.bfloat16).astype(jnp.float32)
    middle = (whole - high).astype(jnp.bfloat16).astype(jnp.float32)
    return jnp.concatenate([high, middle, whole - high - middle], 0)


def fold_kernel(
    parity_ref, cw_ref, conv_ref, weight_ref, after_ref, out_ref, near_ref, levels_w, folded, held, sems, near_sem
):
    del after_ref
    taps = [(dr, dc) for dr in range(3) for dc in range(3)]
    copies = [
        pltpu.make_async_copy(conv_ref.at[dr, dc], held.at[at], sems.at[at])
        for at, (dr, dc) in enumerate(taps)
    ]
    for copy in copies:
        copy.start()
    begin = pl.multiple_of(parity_ref[0] * near_ref.shape[1], LANES)
    bring = pltpu.make_async_copy(
        weight_ref.at[:, pl.ds(begin, near_ref.shape[1])], near_ref, near_sem
    )
    bring.start()
    levels_w[...] = jnp.zeros_like(levels_w)
    levels_w[0:FSQ_DIMS, :] = cw_ref[...]
    left = split_three(levels_w[...]).astype(jnp.bfloat16)
    folded[...] = jnp.zeros_like(folded)
    for at, copy in enumerate(copies):
        copy.wait()
        parts = jnp.dot(left, held[at], preferred_element_type=jnp.float32)
        total = parts[0:8] + parts[8:16] + parts[16:24]
        folded[at * TAP_ROWS : (at + 1) * TAP_ROWS, :] = split_three(total)
    out_ref[...] = folded[...].astype(jnp.bfloat16)
    bring.wait()


def decode_kernel(
    section_ref,
    in_ref,
    fold_ref,
    early_ref,
    two_any,
    after_ref,
    out_ref,
    late_ref,
    sems,
    *,
    feature_rows,
):
    del after_ref
    copies = [
        pltpu.make_async_copy(two_any.at[dr, dc], late_ref.at[at], sems.at[at])
        for at, (dr, dc) in enumerate(TAPS[EARLY:])
    ]
    for copy in copies:
        copy.start()
    section = section_ref[0]
    got = jnp.sum(in_ref[...].astype(jnp.float32), 0)
    pieces = []
    for at in range(PIECES):
        lines = [
            got[feature_rows + at * WINDOW + step : feature_rows + at * WINDOW + step + 1]
            for step in range(WINDOW)
        ]
        pieces.append(jnp.concatenate(lines, 1))
    codes = decode_number(jnp.concatenate(pieces, 1))
    span = codes.shape[1]
    depth = fold_ref.shape[0]
    level = lax.broadcasted_iota(jnp.int32, (8, span), 0)
    taken = level < FSQ_DIMS
    shift = jnp.where(taken, level * 3, 0)
    value = (2 * ((jnp.broadcast_to(codes, (8, span)) >> shift) & 7) - 7).astype(
        jnp.float32
    ) * 0.125
    value = jnp.where(taken, value, 0.0)
    value = jnp.concatenate([value] * (depth // 8), 0).astype(jnp.bfloat16)

    count = TILE_ROWS * IMG_W
    begin = TILE_H * ROW_WORDS * section - HALO * ROW_WORDS
    offset = begin & (LANES - 1)
    spot = lax.broadcasted_iota(jnp.int32, (count, 1), 0)
    line = spot // IMG_W + TILE_H * section - HALO
    inside = (line >= 0) & (line < IMG_SPLIT * TILE_H)
    target = jnp.where(inside, (spot >> 1) + offset + (span // 2) * (spot & 1), -1)
    chooser = jnp.where(
        lax.broadcasted_iota(jnp.int32, (count, span), 1) == target, 1.0, 0.0
    ).astype(jnp.bfloat16)
    placed = lax.dot_general(
        chooser, value, (((1,), (1,)), ((), ())), preferred_element_type=jnp.float32
    )
    column = spot % IMG_W
    moved = [
        jnp.where(column == 0, 0.0, pltpu.roll(placed, 1, 0)),
        placed,
        jnp.where(column == IMG_W - 1, 0.0, pltpu.roll(placed, count - 1, 0)),
    ]
    count = count - 2 * IMG_W
    tap_of = lax.broadcasted_iota(jnp.int32, (1, depth), 1) // TAP_ROWS
    taps = jnp.zeros((count, depth), jnp.float32)
    for dr in range(3):
        for dc in range(3):
            taps = jnp.where(
                tap_of == 3 * dr + dc, moved[dc][dr * IMG_W : dr * IMG_W + count], taps
            )
    hidden = jnp.dot(taps.astype(jnp.bfloat16), fold_ref[...], preferred_element_type=jnp.float32)

    line = lax.broadcasted_iota(jnp.int32, (count, 1), 0) // IMG_W + TILE_H * section - 1
    inside = (line >= 0) & (line < IMG_SPLIT * TILE_H)
    activated = jnp.where(inside, hidden * jax.nn.sigmoid(hidden), 0.0).astype(jnp.bfloat16)

    count = count - 2 * IMG_W
    column = lax.broadcasted_iota(jnp.int32, (count, 1), 0) % IMG_W
    summed = part = None
    for at, (dr, dc) in enumerate(TAPS):
        if at == EARLY:
            for copy in copies:
                copy.wait()
        weight = early_ref[at] if at < EARLY else late_ref[at - EARLY]
        term = jnp.dot(
            activated[dr * IMG_W : dr * IMG_W + count], weight, preferred_element_type=jnp.float32
        )
        part = term if part is None else part + term
        if dr < 2:
            continue
        if dc == 0:
            part = jnp.where(column == 0, 0.0, pltpu.roll(part, 1, 0))
        if dc == 2:
            part = jnp.where(column == IMG_W - 1, 0.0, pltpu.roll(part, count - 1, 0))
        summed = part if summed is None else summed + part
        part = None
    out_ref[...] = summed.astype(jnp.bfloat16)


def limit(mebibytes):
    return pltpu.CompilerParams(vmem_limit_bytes=mebibytes * 1024 * 1024)


def near(array):
    return pltpu.with_memory_space_constraint(array, pltpu.VMEM)


def far(array):
    return pltpu.with_memory_space_constraint(array, pltpu.HBM)


def on_device(
    queries,
    new_keys,
    new_values,
    cache_keys,
    cache_values,
    cache_lengths,
    out_weight,
    codes,
    tile_slot,
    code_weight,
    conv_one,
    conv_two,
):
    tiles = lax.axis_size("rows")
    place = lax.axis_index("rows")
    rows, width = queries.shape
    channels = code_weight.shape[1]
    share = width // tiles
    per = 2 * share // LANES
    feature_rows = rows * per
    depth = message_rows(feature_rows)
    half = width // 2
    lines = 8
    groups = half // (lines * LANES)
    smem = pl.BlockSpec(memory_space=pltpu.SMEM)
    vmem = pl.BlockSpec(memory_space=pltpu.VMEM)
    anywhere = pl.BlockSpec(memory_space=pl.ANY)
    parity = (place % 2).reshape(1).astype(jnp.int32)

    outgoing, give = pl.pallas_call(
        functools.partial(attend_kernel, tiles=tiles, per=per, feature_rows=feature_rows),
        in_specs=[smem] * 3 + [anywhere] * 7,
        out_specs=[vmem, vmem],
        out_shape=[
            pltpu.VMEM((tiles, depth, LANES), jnp.bfloat16),
            pltpu.VMEM((share, half), out_weight.dtype),
        ],
        scratch_shapes=[
            pltpu.VMEM(queries.shape, queries.dtype),
            pltpu.VMEM(new_keys.shape, new_keys.dtype),
            pltpu.VMEM(new_values.shape, new_values.dtype),
            pltpu.VMEM((rows * cache_keys.shape[1] + 16, width), cache_keys.dtype),
            pltpu.VMEM((rows * cache_values.shape[1], width), cache_values.dtype),
            pltpu.VMEM(codes.shape, codes.dtype),
            pltpu.VMEM((tiles, depth, LANES), jnp.float32),
            pltpu.VMEM((LANES, LANES), jnp.float32),
            pltpu.VMEM((width, LANES), jnp.bfloat16),
            pltpu.SemaphoreType.DMA((5 + 2 * rows,)),
        ],
        compiler_params=limit(56),
    )(
        cache_lengths,
        tile_slot,
        parity,
        far(queries),
        far(new_keys),
        far(new_values),
        far(cache_keys),
        far(cache_values),
        far(codes),
        far(out_weight),
    )
    order = [[member(at, tiles) for at in range(tiles)]]
    incoming = lax.all_to_all(
        outgoing, "rows", split_axis=0, concat_axis=0, axis_index_groups=order, tiled=True
    )
    other = lax.ppermute(give, "rows", [(i, i ^ 1) for i in range(tiles)])

    folded, own = pl.pallas_call(
        fold_kernel,
        in_specs=[smem, vmem, anywhere, anywhere, anywhere],
        out_specs=[vmem, vmem],
        out_shape=[
            jax.ShapeDtypeStruct((FOLD_ROWS, channels), jnp.bfloat16),
            pltpu.VMEM((share, half), out_weight.dtype),
        ],
        scratch_shapes=[
            pltpu.VMEM((8, channels), jnp.float32),
            pltpu.VMEM((FOLD_ROWS, channels), jnp.float32),
            pltpu.VMEM((9,) + conv_one.shape[2:], conv_one.dtype),
            pltpu.SemaphoreType.DMA((9,)),
            pltpu.SemaphoreType.DMA,
        ],
        compiler_params=limit(12),
    )(parity, far(code_weight), far(conv_one), far(out_weight), near(outgoing))

    partials, early = pl.pallas_call(
        functools.partial(project_kernel, rows=rows, per=per),
        in_specs=[smem, vmem, vmem, vmem, anywhere],
        out_specs=[vmem, vmem],
        out_shape=[
            pltpu.VMEM((tiles, groups, rows * lines, LANES), jnp.bfloat16),
            pltpu.VMEM((EARLY,) + conv_two.shape[2:], conv_two.dtype),
        ],
        scratch_shapes=[
            pltpu.VMEM((tiles * depth, LANES), jnp.float32),
            pltpu.VMEM((groups, tiles * rows * lines, LANES), jnp.float32),
            pltpu.SemaphoreType.DMA((EARLY,)),
        ],
        compiler_params=limit(8),
    )(parity, near(incoming), near(own), near(other), far(conv_two))
    gathered = lax.all_to_all(
        partials, "rows", split_axis=0, concat_axis=0, axis_index_groups=order, tiled=True
    )

    section = (place + IMG_SPLIT // 2) % tiles % IMG_SPLIT
    decoded = pl.pallas_call(
        functools.partial(decode_kernel, feature_rows=feature_rows),
        in_specs=[smem, vmem, vmem, vmem, anywhere, anywhere],
        out_specs=vmem,
        out_shape=jax.ShapeDtypeStruct((TILE_H * IMG_W, channels), jnp.bfloat16),
        scratch_shapes=[
            pltpu.VMEM((len(TAPS) - EARLY,) + conv_two.shape[2:], conv_two.dtype),
            pltpu.SemaphoreType.DMA((len(TAPS) - EARLY,)),
        ],
        compiler_params=limit(16),
    )(section.reshape(1).astype(jnp.int32), near(incoming), near(folded), near(early), far(conv_two), near(partials))

    mixed = pl.pallas_call(
        functools.partial(total_kernel, rows=rows),
        in_specs=[vmem],
        out_shape=jax.ShapeDtypeStruct((rows, width), jnp.bfloat16),
        scratch_shapes=[pltpu.VMEM((2 * groups, rows * lines, LANES), jnp.float32)],
        compiler_params=limit(8),
    )(near(gathered))
    return (mixed, decoded.reshape(TILE_H, IMG_W, channels))


def solution(mesh):
    in_specs = (
        P(("groups", "rows"), None),
        P(("groups", "rows"), None),
        P(("groups", "rows"), None),
        P(("groups", "rows"), None, None),
        P(("groups", "rows"), None, None),
        P(("groups", "rows")),
        P("rows", None),
        P(("groups", "rows"), None),
        P(("groups", "rows")),
        P(),
        P(),
        P(),
    )
    out_specs = (P(("groups", "rows"), None), P(("groups", "rows"), None, None))
    return jax.shard_map(
        on_device, mesh=mesh, in_specs=in_specs, out_specs=out_specs, check_vma=False
    )
```

```python
import functools
import math

import jax
import jax.numpy as jnp
from jax import lax
from jax.experimental import pallas as pl
from jax.experimental.pallas import tpu as pltpu
from jax.sharding import PartitionSpec as P

HEAD_DIM = 128
FSQ_DIMS = 5
IMG_SPLIT = 4
TILE_H = 8
IMG_W = 48
LANES = 128
HALO = 2
ROW_WORDS = IMG_W // 2
TILE_ROWS = TILE_H + 2 * HALO
WINDOW = 3
PIECES = 2
CODE_ROWS = WINDOW * PIECES
TAP_ROWS = 24
FOLD_ROWS = 256
TAPS = [(dr, dc) for dc in (1, 0, 2) for dr in range(3)]
EARLY = 3
VMEM_LIMIT = 24 * 1024 * 1024


def window_start(section):
    return (TILE_H * ROW_WORDS * section - HALO * ROW_WORDS) // LANES


def member(at, tiles):
    return (at + tiles // 4 * 2) % tiles


def message_rows(features):
    return -(-(features + CODE_ROWS) // 16) * 16


def encode(code):
    fraction = (code & 127).astype(jnp.float32) * (1.0 / 128.0) + 1.0
    for bit in range(7):
        up = ((code >> (7 + bit)) & 1) == 1
        fraction = jnp.where(up, fraction * 2.0 ** (1 << bit), fraction)
        if bit == 5:
            fraction = fraction * 2.0**-64
    return jnp.where(((code >> 14) & 1) == 1, -fraction, fraction)


def decode_number(value):
    size = jnp.abs(value)
    code = jnp.where(value < 0.0, 1 << 14, 0)
    for bit in range(6, -1, -1):
        step = 1 << bit
        up = size >= 2.0 ** (step - 64)
        code = code + jnp.where(up, step << 7, 0)
        size = jnp.where(up, size * 2.0**-step, size)
    return code + ((size * 2.0**64 - 1.0) * 128.0).astype(jnp.int32)


def attend_kernel(
    lengths_any,
    slots_any,
    q_any,
    nk_any,
    nv_any,
    k_any,
    v_any,
    codes_any,
    weight_any,
    out_ref,
    give_ref,
    q_ref,
    nk_ref,
    nv_ref,
    k_ref,
    v_ref,
    codes_ref,
    msg,
    by_head,
    spread,
    lengths,
    slots,
    sems,
    *,
    tiles,
    per,
    feature_rows,
):
    rows, width = q_ref.shape
    give_columns = give_ref.shape[1]
    small = [
        pltpu.make_async_copy(source, target, sems.at[at])
        for at, (source, target) in enumerate(
            (
                (q_any, q_ref),
                (nk_any, nk_ref),
                (nv_any, nv_ref),
                (codes_any, codes_ref),
                (lengths_any, lengths),
                (slots_any, slots),
            )
        )
    ]
    cached = k_any.shape[1]
    keys, values = (
        [
            pltpu.make_async_copy(
                source.at[r], target.at[pl.ds(r * cached, cached)], sems.at[base + r]
            )
            for r in range(rows)
        ]
        for source, target, base in ((k_any, k_ref, 6), (v_any, v_ref, 6 + rows))
    )
    begin = pl.multiple_of((1 - lax.axis_index("rows") % 2) * give_columns, LANES)
    give = pltpu.make_async_copy(
        weight_any.at[:, pl.ds(begin, give_columns)], give_ref, sems.at[6 + 2 * rows]
    )
    for copy in small:
        copy.start()
    for copy in keys:
        copy.start()

    heads = width // HEAD_DIM
    factor = 1.0 / math.sqrt(HEAD_DIM)
    msg[...] = jnp.zeros_like(msg)
    for copy in small:
        copy.wait()

    words = codes_ref[...]
    blocks = words.shape[1] // LANES
    pieces = [encode(words & 32767), encode(words >> 15)]
    for slot in range(tiles // IMG_SPLIT):
        gains = [
            jnp.where(slots[r] == slot, 1.0, 0.0).astype(jnp.float32) for r in range(rows)
        ]
        for at, piece in enumerate(pieces):
            total = piece[0:1] * gains[0]
            for r in range(1, rows):
                total = total + piece[r : r + 1] * gains[r]
            for tile in range(tiles):
                number = (member(tile, tiles) + IMG_SPLIT // 2) % tiles
                if number // IMG_SPLIT != slot:
                    continue
                for step in range(WINDOW):
                    block = window_start(number % IMG_SPLIT) + step
                    if block < 0 or block >= blocks:
                        continue
                    place = feature_rows + at * WINDOW + step
                    msg[tile, place : place + 1, :] = total[:, block * LANES : (block + 1) * LANES]

    queries = q_ref[...].astype(jnp.float32)
    by_head[...] = jnp.zeros_like(by_head)
    for r in range(rows):
        for head in range(heads):
            by_head[r * heads + head : r * heads + head + 1, :] = queries[
                r : r + 1, head * LANES : (head + 1) * LANES
            ]
    turned = by_head[...].T
    column = lax.broadcasted_iota(jnp.int32, (1, LANES), 1)
    for head in range(heads):
        spread[head * LANES : (head + 1) * LANES, :] = jnp.where(
            column % heads == head, turned, 0.0
        ).astype(jnp.bfloat16)
    padding = jnp.zeros((16 - rows, width), jnp.float32)
    known = rows * cached
    k_ref[known:, :] = jnp.concatenate([nk_ref[...].astype(jnp.float32), padding], 0).astype(
        jnp.bfloat16
    )
    new_values = jnp.concatenate([nv_ref[...].astype(jnp.float32), padding], 0).astype(jnp.bfloat16)
    for copy in values:
        copy.start()
    for copy in keys:
        copy.wait()
    products = jnp.dot(k_ref[...], spread[...], preferred_element_type=jnp.float32) * factor
    give.start()
    own_scores = products[known:]
    scores = products[:known]
    owner = column // heads
    own_at = lax.broadcasted_iota(jnp.int32, own_scores.shape, 0) == owner
    own_score = jnp.sum(jnp.where(own_at, own_scores, 0.0), 0, keepdims=True)
    limit = jnp.zeros(column.shape, jnp.int32)
    for r in range(rows):
        limit = jnp.where(owner == r, lengths[r], limit)
    position = lax.broadcasted_iota(jnp.int32, scores.shape, 0) - owner * cached
    live = (position >= 0) & (position < limit)
    scores = jnp.where(live, scores, jnp.float32(-1e30))
    highest = jnp.maximum(jnp.max(scores, 0, keepdims=True), own_score)
    cache_exp = jnp.where(live, jnp.exp(scores - highest), 0.0)
    own_exp = jnp.exp(own_score - highest)
    denom = jnp.sum(cache_exp, 0, keepdims=True) + own_exp
    cache_weight = (cache_exp / denom).T[: rows * heads].astype(jnp.bfloat16)
    own_weight = jnp.where(own_at, own_exp / denom, 0.0)
    own_weight = jnp.concatenate(
        [own_weight, jnp.zeros((LANES - own_weight.shape[0], LANES), jnp.float32)], 0
    ).T[: rows * heads, :16].astype(jnp.bfloat16)
    for copy in values:
        copy.wait()
    attended = jnp.dot(cache_weight, v_ref[...], preferred_element_type=jnp.float32) + jnp.dot(
        own_weight, new_values, preferred_element_type=jnp.float32
    )
    for tile in range(tiles):
        for r in range(rows):
            for step in range(per):
                head = member(tile, tiles) // 2 * per + step
                place = r * per + step
                msg[tile, place : place + 1, :] = attended[
                    r * heads + head : r * heads + head + 1, head * LANES : (head + 1) * LANES
                ]
    out_ref[...] = msg[...].astype(jnp.bfloat16)
    give.wait()


def project_kernel(in_ref, own_ref, other_ref, out_ref, held, total, *, rows, per):
    tiles, depth = in_ref.shape[:2]
    held[...] = in_ref[...].astype(jnp.float32).reshape(held.shape)
    groups = total.shape[0]
    lines = out_ref.shape[2] // rows
    share = own_ref.shape[0]
    lhs = []
    for row in range(rows):
        parts = [held[pl.ds(row * per + j, tiles, stride=depth), :] for j in range(per)]
        lhs.append(jnp.concatenate(parts, 1))
    lhs = jnp.concatenate(lhs, 0)
    even = lax.axis_index("rows") % 2 == 0
    first, second = lhs[:, :share], lhs[:, share:]
    own = jnp.where(even, first, second).astype(jnp.bfloat16)
    other = jnp.where(even, second, first).astype(jnp.bfloat16)
    product = jnp.dot(own, own_ref[...], preferred_element_type=jnp.float32) + jnp.dot(
        other, other_ref[...], preferred_element_type=jnp.float32
    )
    for row in range(rows):
        for group in range(groups):
            for line in range(lines):
                begin = (group * lines + line) * LANES
                total[group, pl.ds(row * lines + line, tiles, stride=rows * lines), :] = product[
                    row * tiles : (row + 1) * tiles, begin : begin + LANES
                ]
    for group in range(groups):
        out_ref[:, group] = (
            total[group].astype(jnp.bfloat16).reshape(tiles, rows * lines, LANES)
        )


def total_kernel(in_ref, out_ref, held, *, rows):
    tiles, groups, depth, _ = in_ref.shape
    lines = depth // rows
    parts = in_ref[...].astype(jnp.float32).reshape(tiles // 2, 2 * groups, depth, LANES)
    held[...] = jnp.sum(parts, 0)
    for group in range(2 * groups):
        for line in range(lines):
            begin = (group * lines + line) * LANES
            out_ref[:, begin : begin + LANES] = held[
                group, pl.ds(line, rows, stride=lines), :
            ].astype(jnp.bfloat16)


def split_three(whole):
    high = whole.astype(jnp.bfloat16).astype(jnp.float32)
    middle = (whole - high).astype(jnp.bfloat16).astype(jnp.float32)
    return jnp.concatenate([high, middle, whole - high - middle], 0)


def fold_kernel(
    cw_ref, conv_ref, weight_ref, after_ref, out_ref, near_ref, levels_w, folded, held, sems, near_sem
):
    del after_ref
    taps = [(dr, dc) for dr in range(3) for dc in range(3)]
    copies = [
        pltpu.make_async_copy(conv_ref.at[dr, dc], held.at[at], sems.at[at])
        for at, (dr, dc) in enumerate(taps)
    ]
    for copy in copies:
        copy.start()
    begin = pl.multiple_of(lax.axis_index("rows") % 2 * near_ref.shape[1], LANES)
    bring = pltpu.make_async_copy(
        weight_ref.at[:, pl.ds(begin, near_ref.shape[1])], near_ref, near_sem
    )
    bring.start()
    levels_w[...] = jnp.zeros_like(levels_w)
    levels_w[0:FSQ_DIMS, :] = cw_ref[...]
    left = split_three(levels_w[...]).astype(jnp.bfloat16)
    folded[...] = jnp.zeros_like(folded)
    for at, copy in enumerate(copies):
        copy.wait()
        parts = jnp.dot(left, held[at], preferred_element_type=jnp.float32)
        total = parts[0:8] + parts[8:16] + parts[16:24]
        folded[at * TAP_ROWS : (at + 1) * TAP_ROWS, :] = split_three(total)
    out_ref[...] = folded[...].astype(jnp.bfloat16)
    bring.wait()


def decode_kernel(
    in_ref, fold_ref, two_any, after_ref, out_ref, two_ref, sems, *, feature_rows
):
    del after_ref
    copies = [
        pltpu.make_async_copy(two_any.at[dr, dc], two_ref.at[at], sems.at[at])
        for at, (dr, dc) in enumerate(TAPS)
    ]
    for copy in copies[:EARLY]:
        copy.start()
    tiles = lax.axis_size("rows")
    section = (lax.axis_index("rows") + IMG_SPLIT // 2) % tiles % IMG_SPLIT
    got = jnp.sum(in_ref[...].astype(jnp.float32), 0)
    pieces = []
    for at in range(PIECES):
        lines = [
            got[feature_rows + at * WINDOW + step : feature_rows + at * WINDOW + step + 1]
            for step in range(WINDOW)
        ]
        pieces.append(jnp.concatenate(lines, 1))
    codes = decode_number(jnp.concatenate(pieces, 1))
    span = codes.shape[1]
    depth = fold_ref.shape[0]
    level = lax.broadcasted_iota(jnp.int32, (8, span), 0)
    taken = level < FSQ_DIMS
    shift = jnp.where(taken, level * 3, 0)
    value = (2 * ((jnp.broadcast_to(codes, (8, span)) >> shift) & 7) - 7).astype(
        jnp.float32
    ) * 0.125
    value = jnp.where(taken, value, 0.0)
    value = jnp.concatenate([value] * (depth // 8), 0).astype(jnp.bfloat16)

    count = TILE_ROWS * IMG_W
    begin = TILE_H * ROW_WORDS * section - HALO * ROW_WORDS
    offset = begin & (LANES - 1)
    spot = lax.broadcasted_iota(jnp.int32, (count, 1), 0)
    line = spot // IMG_W + TILE_H * section - HALO
    inside = (line >= 0) & (line < IMG_SPLIT * TILE_H)
    target = jnp.where(inside, (spot >> 1) + offset + (span // 2) * (spot & 1), -1)
    chooser = jnp.where(
        lax.broadcasted_iota(jnp.int32, (count, span), 1) == target, 1.0, 0.0
    ).astype(jnp.bfloat16)
    placed = lax.dot_general(
        chooser, value, (((1,), (1,)), ((), ())), preferred_element_type=jnp.float32
    )
    for copy in copies[EARLY:]:
        copy.start()
    column = spot % IMG_W
    moved = [
        jnp.where(column == 0, 0.0, pltpu.roll(placed, 1, 0)),
        placed,
        jnp.where(column == IMG_W - 1, 0.0, pltpu.roll(placed, count - 1, 0)),
    ]
    count = count - 2 * IMG_W
    tap_of = lax.broadcasted_iota(jnp.int32, (1, depth), 1) // TAP_ROWS
    taps = jnp.zeros((count, depth), jnp.float32)
    for dr in range(3):
        for dc in range(3):
            taps = jnp.where(
                tap_of == 3 * dr + dc, moved[dc][dr * IMG_W : dr * IMG_W + count], taps
            )
    hidden = jnp.dot(taps.astype(jnp.bfloat16), fold_ref[...], preferred_element_type=jnp.float32)

    line = lax.broadcasted_iota(jnp.int32, (count, 1), 0) // IMG_W + TILE_H * section - 1
    inside = (line >= 0) & (line < IMG_SPLIT * TILE_H)
    activated = jnp.where(inside, hidden * jax.nn.sigmoid(hidden), 0.0).astype(jnp.bfloat16)

    count = count - 2 * IMG_W
    column = lax.broadcasted_iota(jnp.int32, (count, 1), 0) % IMG_W
    summed = part = None
    for at, (dr, dc) in enumerate(TAPS):
        if at == 0:
            for copy in copies[:EARLY]:
                copy.wait()
        if at == EARLY:
            for copy in copies[EARLY:]:
                copy.wait()
        term = jnp.dot(
            activated[dr * IMG_W : dr * IMG_W + count],
            two_ref[at],
            preferred_element_type=jnp.float32,
        )
        part = term if part is None else part + term
        if dr < 2:
            continue
        if dc == 0:
            part = jnp.where(column == 0, 0.0, pltpu.roll(part, 1, 0))
        if dc == 2:
            part = jnp.where(column == IMG_W - 1, 0.0, pltpu.roll(part, count - 1, 0))
        summed = part if summed is None else summed + part
        part = None
    out_ref[...] = summed.astype(jnp.bfloat16)


def near(array):
    return pltpu.with_memory_space_constraint(array, pltpu.VMEM)


def far(array):
    return pltpu.with_memory_space_constraint(array, pltpu.HBM)


def on_device(
    queries,
    new_keys,
    new_values,
    cache_keys,
    cache_values,
    cache_lengths,
    out_weight,
    codes,
    tile_slot,
    code_weight,
    conv_one,
    conv_two,
):
    tiles = lax.axis_size("rows")
    rows, width = queries.shape
    channels = code_weight.shape[1]
    share = width // tiles
    per = 2 * share // LANES
    feature_rows = rows * per
    depth = message_rows(feature_rows)
    half = width // 2
    lines = 8
    groups = half // (lines * LANES)
    params = pltpu.CompilerParams(vmem_limit_bytes=VMEM_LIMIT)
    vmem = pl.BlockSpec(memory_space=pltpu.VMEM)
    anywhere = pl.BlockSpec(memory_space=pl.ANY)

    outgoing, give = pl.pallas_call(
        functools.partial(attend_kernel, tiles=tiles, per=per, feature_rows=feature_rows),
        in_specs=[anywhere] * 9,
        out_specs=[vmem, vmem],
        out_shape=[
            pltpu.VMEM((tiles, depth, LANES), jnp.bfloat16),
            pltpu.VMEM((share, half), out_weight.dtype),
        ],
        scratch_shapes=[
            pltpu.VMEM(queries.shape, queries.dtype),
            pltpu.VMEM(new_keys.shape, new_keys.dtype),
            pltpu.VMEM(new_values.shape, new_values.dtype),
            pltpu.VMEM((rows * cache_keys.shape[1] + 16, width), cache_keys.dtype),
            pltpu.VMEM((rows * cache_values.shape[1], width), cache_values.dtype),
            pltpu.VMEM(codes.shape, codes.dtype),
            pltpu.VMEM((tiles, depth, LANES), jnp.float32),
            pltpu.VMEM((LANES, LANES), jnp.float32),
            pltpu.VMEM((width, LANES), jnp.bfloat16),
            pltpu.SMEM(cache_lengths.shape, cache_lengths.dtype),
            pltpu.SMEM(tile_slot.shape, tile_slot.dtype),
            pltpu.SemaphoreType.DMA((7 + 2 * rows,)),
        ],
        compiler_params=pltpu.CompilerParams(vmem_limit_bytes=56 * 1024 * 1024),
    )(
        far(cache_lengths),
        far(tile_slot),
        far(queries),
        far(new_keys),
        far(new_values),
        far(cache_keys),
        far(cache_values),
        far(codes),
        far(out_weight),
    )
    order = [[member(at, tiles) for at in range(tiles)]]
    incoming = lax.all_to_all(
        outgoing, "rows", split_axis=0, concat_axis=0, axis_index_groups=order, tiled=True
    )
    other = lax.ppermute(give, "rows", [(i, i ^ 1) for i in range(tiles)])

    folded, own = pl.pallas_call(
        fold_kernel,
        in_specs=[vmem, anywhere, anywhere, anywhere],
        out_specs=[vmem, vmem],
        out_shape=[
            jax.ShapeDtypeStruct((FOLD_ROWS, channels), jnp.bfloat16),
            pltpu.VMEM((share, half), out_weight.dtype),
        ],
        scratch_shapes=[
            pltpu.VMEM((8, channels), jnp.float32),
            pltpu.VMEM((FOLD_ROWS, channels), jnp.float32),
            pltpu.VMEM((9,) + conv_one.shape[2:], conv_one.dtype),
            pltpu.SemaphoreType.DMA((9,)),
            pltpu.SemaphoreType.DMA,
        ],
        compiler_params=params,
    )(far(code_weight), far(conv_one), far(out_weight), near(outgoing))

    partials = pl.pallas_call(
        functools.partial(project_kernel, rows=rows, per=per),
        in_specs=[vmem, vmem, vmem],
        out_shape=pltpu.VMEM((tiles, groups, rows * lines, LANES), jnp.bfloat16),
        scratch_shapes=[
            pltpu.VMEM((tiles * depth, LANES), jnp.float32),
            pltpu.VMEM((groups, tiles * rows * lines, LANES), jnp.float32),
        ],
        compiler_params=params,
    )(near(incoming), near(own), near(other))
    gathered = lax.all_to_all(
        partials, "rows", split_axis=0, concat_axis=0, axis_index_groups=order, tiled=True
    )

    decoded = pl.pallas_call(
        functools.partial(decode_kernel, feature_rows=feature_rows),
        in_specs=[vmem, vmem, anywhere, anywhere],
        out_specs=vmem,
        out_shape=jax.ShapeDtypeStruct((TILE_H * IMG_W, channels), jnp.bfloat16),
        scratch_shapes=[
            pltpu.VMEM((len(TAPS),) + conv_two.shape[2:], conv_two.dtype),
            pltpu.SemaphoreType.DMA((len(TAPS),)),
        ],
        compiler_params=params,
    )(near(incoming), near(folded), far(conv_two), near(partials))

    mixed = pl.pallas_call(
        functools.partial(total_kernel, rows=rows),
        in_specs=[vmem],
        out_shape=jax.ShapeDtypeStruct((rows, width), jnp.bfloat16),
        scratch_shapes=[pltpu.VMEM((2 * groups, rows * lines, LANES), jnp.float32)],
        compiler_params=params,
    )(near(gathered))
    return (mixed, decoded.reshape(TILE_H, IMG_W, channels))


def solution(mesh):
    in_specs = (
        P(("groups", "rows"), None),
        P(("groups", "rows"), None),
        P(("groups", "rows"), None),
        P(("groups", "rows"), None, None),
        P(("groups", "rows"), None, None),
        P(("groups", "rows")),
        P("rows", None),
        P(("groups", "rows"), None),
        P(("groups", "rows")),
        P(),
        P(),
        P(),
    )
    out_specs = (P(("groups", "rows"), None), P(("groups", "rows"), None, None))
    return jax.shard_map(
        on_device, mesh=mesh, in_specs=in_specs, out_specs=out_specs, check_vma=False
    )
```

```python
import functools
import math

import jax
import jax.numpy as jnp
from jax import lax
from jax.experimental import pallas as pl
from jax.experimental.pallas import tpu as pltpu
from jax.sharding import PartitionSpec as P

HEAD_DIM = 128
FSQ_DIMS = 5
IMG_SPLIT = 4
TILE_H = 8
IMG_W = 48
LANES = 128
HALO = 2
ROW_WORDS = IMG_W // 2
TILE_ROWS = TILE_H + 2 * HALO
WINDOW = 3
PIECES = 2
CODE_ROWS = WINDOW * PIECES
TAP_ROWS = 24
FOLD_ROWS = 256
TAPS = [(dr, dc) for dc in (1, 0, 2) for dr in range(3)]
EARLY = 3
VMEM_LIMIT = 24 * 1024 * 1024


def window_start(section):
    return (TILE_H * ROW_WORDS * section - HALO * ROW_WORDS) // LANES


def member(at, tiles):
    return (at + tiles // 4 * 2) % tiles


def message_rows(features):
    return -(-(features + CODE_ROWS) // 16) * 16


def encode(code):
    fraction = (code & 127).astype(jnp.float32) * (1.0 / 128.0) + 1.0
    for bit in range(7):
        up = ((code >> (7 + bit)) & 1) == 1
        fraction = jnp.where(up, fraction * 2.0 ** (1 << bit), fraction)
        if bit == 5:
            fraction = fraction * 2.0**-64
    return jnp.where(((code >> 14) & 1) == 1, -fraction, fraction)


def decode_number(value):
    size = jnp.abs(value)
    code = jnp.where(value < 0.0, 1 << 14, 0)
    for bit in range(6, -1, -1):
        step = 1 << bit
        up = size >= 2.0 ** (step - 64)
        code = code + jnp.where(up, step << 7, 0)
        size = jnp.where(up, size * 2.0**-step, size)
    return code + ((size * 2.0**64 - 1.0) * 128.0).astype(jnp.int32)


def attend_kernel(
    lengths_any,
    slots_any,
    q_any,
    nk_any,
    nv_any,
    k_any,
    v_any,
    codes_any,
    weight_any,
    out_ref,
    give_ref,
    q_ref,
    nk_ref,
    nv_ref,
    k_ref,
    v_ref,
    codes_ref,
    msg,
    by_head,
    spread,
    lengths,
    slots,
    sems,
    *,
    tiles,
    per,
    feature_rows,
):
    rows, width = q_ref.shape
    give_columns = give_ref.shape[1]
    small = [
        pltpu.make_async_copy(source, target, sems.at[at])
        for at, (source, target) in enumerate(
            (
                (q_any, q_ref),
                (nk_any, nk_ref),
                (nv_any, nv_ref),
                (codes_any, codes_ref),
                (lengths_any, lengths),
                (slots_any, slots),
            )
        )
    ]
    cached = k_any.shape[1]
    keys, values = (
        [
            pltpu.make_async_copy(
                source.at[r], target.at[pl.ds(r * cached, cached)], sems.at[base + r]
            )
            for r in range(rows)
        ]
        for source, target, base in ((k_any, k_ref, 6), (v_any, v_ref, 6 + rows))
    )
    begin = pl.multiple_of((1 - lax.axis_index("rows") % 2) * give_columns, LANES)
    give = pltpu.make_async_copy(
        weight_any.at[:, pl.ds(begin, give_columns)], give_ref, sems.at[6 + 2 * rows]
    )
    for copy in small:
        copy.start()
    for copy in keys:
        copy.start()

    heads = width // HEAD_DIM
    factor = 1.0 / math.sqrt(HEAD_DIM)
    msg[...] = jnp.zeros_like(msg)
    for copy in small:
        copy.wait()
    for copy in values:
        copy.start()

    queries = q_ref[...].astype(jnp.float32)
    by_head[...] = jnp.zeros_like(by_head)
    for r in range(rows):
        for head in range(heads):
            by_head[r * heads + head : r * heads + head + 1, :] = queries[
                r : r + 1, head * LANES : (head + 1) * LANES
            ]
    turned = by_head[...].T
    column = lax.broadcasted_iota(jnp.int32, (1, LANES), 1)
    for head in range(heads):
        spread[head * LANES : (head + 1) * LANES, :] = jnp.where(
            column % heads == head, turned, 0.0
        ).astype(jnp.bfloat16)
    padding = jnp.zeros((16 - rows, width), jnp.float32)
    known = rows * cached
    k_ref[known:, :] = jnp.concatenate([nk_ref[...].astype(jnp.float32), padding], 0).astype(
        jnp.bfloat16
    )
    v_ref[known:, :] = jnp.concatenate([nv_ref[...].astype(jnp.float32), padding], 0).astype(
        jnp.bfloat16
    )
    for copy in keys:
        copy.wait()
    products = jnp.dot(k_ref[...], spread[...], preferred_element_type=jnp.float32) * factor
    give.start()
    words = codes_ref[...]
    blocks = words.shape[1] // LANES
    pieces = [encode(words & 32767), encode(words >> 15)]
    for slot in range(tiles // IMG_SPLIT):
        gains = [
            jnp.where(slots[r] == slot, 1.0, 0.0).astype(jnp.float32) for r in range(rows)
        ]
        for at, piece in enumerate(pieces):
            total = piece[0:1] * gains[0]
            for r in range(1, rows):
                total = total + piece[r : r + 1] * gains[r]
            for tile in range(tiles):
                number = (member(tile, tiles) + IMG_SPLIT // 2) % tiles
                if number // IMG_SPLIT != slot:
                    continue
                for step in range(WINDOW):
                    block = window_start(number % IMG_SPLIT) + step
                    if block < 0 or block >= blocks:
                        continue
                    place = feature_rows + at * WINDOW + step
                    msg[tile, place : place + 1, :] = total[:, block * LANES : (block + 1) * LANES]

    own_scores = products[known:]
    scores = products[:known]
    owner = column // heads
    own_at = lax.broadcasted_iota(jnp.int32, own_scores.shape, 0) == owner
    own_score = jnp.sum(jnp.where(own_at, own_scores, 0.0), 0, keepdims=True)
    limit = jnp.zeros(column.shape, jnp.int32)
    for r in range(rows):
        limit = jnp.where(owner == r, lengths[r], limit)
    position = lax.broadcasted_iota(jnp.int32, scores.shape, 0) - owner * cached
    live = (position >= 0) & (position < limit)
    scores = jnp.where(live, scores, jnp.float32(-1e30))
    highest = jnp.maximum(jnp.max(scores, 0, keepdims=True), own_score)
    cache_exp = jnp.where(live, jnp.exp(scores - highest), 0.0)
    own_exp = jnp.exp(own_score - highest)
    denom = jnp.sum(cache_exp, 0, keepdims=True) + own_exp
    cache_weight = (cache_exp / denom).T[: rows * heads]
    own_weight = jnp.where(own_at, own_exp / denom, 0.0)
    own_weight = jnp.concatenate(
        [own_weight, jnp.zeros((LANES - own_weight.shape[0], LANES), jnp.float32)], 0
    ).T[: rows * heads, :16]
    weight = jnp.concatenate([cache_weight, own_weight], 1).astype(jnp.bfloat16)
    for copy in values:
        copy.wait()
    attended = jnp.dot(weight, v_ref[...], preferred_element_type=jnp.float32)
    for tile in range(tiles):
        for r in range(rows):
            for step in range(per):
                head = member(tile, tiles) // 2 * per + step
                place = r * per + step
                msg[tile, place : place + 1, :] = attended[
                    r * heads + head : r * heads + head + 1, head * LANES : (head + 1) * LANES
                ]
    out_ref[...] = msg[...].astype(jnp.bfloat16)
    give.wait()


def project_kernel(in_ref, own_ref, other_ref, out_ref, held, total, *, rows, per):
    tiles, depth = in_ref.shape[:2]
    held[...] = in_ref[...].astype(jnp.float32).reshape(held.shape)
    groups = total.shape[0]
    lines = out_ref.shape[2] // rows
    share = own_ref.shape[0]
    lhs = []
    for row in range(rows):
        parts = [held[pl.ds(row * per + j, tiles, stride=depth), :] for j in range(per)]
        lhs.append(jnp.concatenate(parts, 1))
    lhs = jnp.concatenate(lhs, 0)
    even = lax.axis_index("rows") % 2 == 0
    first, second = lhs[:, :share], lhs[:, share:]
    own = jnp.where(even, first, second).astype(jnp.bfloat16)
    other = jnp.where(even, second, first).astype(jnp.bfloat16)
    product = jnp.dot(own, own_ref[...], preferred_element_type=jnp.float32) + jnp.dot(
        other, other_ref[...], preferred_element_type=jnp.float32
    )
    for row in range(rows):
        for group in range(groups):
            for line in range(lines):
                begin = (group * lines + line) * LANES
                total[group, pl.ds(row * lines + line, tiles, stride=rows * lines), :] = product[
                    row * tiles : (row + 1) * tiles, begin : begin + LANES
                ]
    for group in range(groups):
        out_ref[:, group] = (
            total[group].astype(jnp.bfloat16).reshape(tiles, rows * lines, LANES)
        )


def total_kernel(in_ref, out_ref, held, *, rows):
    tiles, groups, depth, _ = in_ref.shape
    lines = depth // rows
    parts = in_ref[...].astype(jnp.float32).reshape(tiles // 2, 2 * groups, depth, LANES)
    held[...] = jnp.sum(parts, 0)
    for group in range(2 * groups):
        for line in range(lines):
            begin = (group * lines + line) * LANES
            out_ref[:, begin : begin + LANES] = held[
                group, pl.ds(line, rows, stride=lines), :
            ].astype(jnp.bfloat16)


def split_three(whole):
    high = whole.astype(jnp.bfloat16).astype(jnp.float32)
    middle = (whole - high).astype(jnp.bfloat16).astype(jnp.float32)
    return jnp.concatenate([high, middle, whole - high - middle], 0)


def fold_kernel(
    cw_ref, conv_ref, weight_ref, after_ref, out_ref, near_ref, levels_w, folded, held, sems, near_sem
):
    del after_ref
    taps = [(dr, dc) for dr in range(3) for dc in range(3)]
    copies = [
        pltpu.make_async_copy(conv_ref.at[dr, dc], held.at[at], sems.at[at])
        for at, (dr, dc) in enumerate(taps)
    ]
    for copy in copies:
        copy.start()
    begin = pl.multiple_of(lax.axis_index("rows") % 2 * near_ref.shape[1], LANES)
    bring = pltpu.make_async_copy(
        weight_ref.at[:, pl.ds(begin, near_ref.shape[1])], near_ref, near_sem
    )
    bring.start()
    levels_w[...] = jnp.zeros_like(levels_w)
    levels_w[0:FSQ_DIMS, :] = cw_ref[...]
    left = split_three(levels_w[...]).astype(jnp.bfloat16)
    folded[...] = jnp.zeros_like(folded)
    for at, copy in enumerate(copies):
        copy.wait()
        parts = jnp.dot(left, held[at], preferred_element_type=jnp.float32)
        total = parts[0:8] + parts[8:16] + parts[16:24]
        folded[at * TAP_ROWS : (at + 1) * TAP_ROWS, :] = split_three(total)
    out_ref[...] = folded[...].astype(jnp.bfloat16)
    bring.wait()


def decode_kernel(
    in_ref, fold_ref, two_any, after_ref, out_ref, two_ref, sems, *, feature_rows
):
    del after_ref
    copies = [
        pltpu.make_async_copy(two_any.at[dr, dc], two_ref.at[at], sems.at[at])
        for at, (dr, dc) in enumerate(TAPS)
    ]
    for copy in copies[:EARLY]:
        copy.start()
    tiles = lax.axis_size("rows")
    section = (lax.axis_index("rows") + IMG_SPLIT // 2) % tiles % IMG_SPLIT
    got = jnp.sum(in_ref[...].astype(jnp.float32), 0)
    pieces = []
    for at in range(PIECES):
        lines = [
            got[feature_rows + at * WINDOW + step : feature_rows + at * WINDOW + step + 1]
            for step in range(WINDOW)
        ]
        pieces.append(jnp.concatenate(lines, 1))
    codes = decode_number(jnp.concatenate(pieces, 1))
    span = codes.shape[1]
    depth = fold_ref.shape[0]
    level = lax.broadcasted_iota(jnp.int32, (8, span), 0)
    taken = level < FSQ_DIMS
    shift = jnp.where(taken, level * 3, 0)
    value = (2 * ((jnp.broadcast_to(codes, (8, span)) >> shift) & 7) - 7).astype(
        jnp.float32
    ) * 0.125
    value = jnp.where(taken, value, 0.0)
    value = jnp.concatenate([value] * (depth // 8), 0).astype(jnp.bfloat16)

    count = TILE_ROWS * IMG_W
    begin = TILE_H * ROW_WORDS * section - HALO * ROW_WORDS
    offset = begin & (LANES - 1)
    spot = lax.broadcasted_iota(jnp.int32, (count, 1), 0)
    line = spot // IMG_W + TILE_H * section - HALO
    inside = (line >= 0) & (line < IMG_SPLIT * TILE_H)
    target = jnp.where(inside, (spot >> 1) + offset + (span // 2) * (spot & 1), -1)
    chooser = jnp.where(
        lax.broadcasted_iota(jnp.int32, (count, span), 1) == target, 1.0, 0.0
    ).astype(jnp.bfloat16)
    placed = lax.dot_general(
        chooser, value, (((1,), (1,)), ((), ())), preferred_element_type=jnp.float32
    )
    for copy in copies[EARLY:]:
        copy.start()
    column = spot % IMG_W
    moved = [
        jnp.where(column == 0, 0.0, pltpu.roll(placed, 1, 0)),
        placed,
        jnp.where(column == IMG_W - 1, 0.0, pltpu.roll(placed, count - 1, 0)),
    ]
    count = count - 2 * IMG_W
    tap_of = lax.broadcasted_iota(jnp.int32, (1, depth), 1) // TAP_ROWS
    taps = jnp.zeros((count, depth), jnp.float32)
    for dr in range(3):
        for dc in range(3):
            taps = jnp.where(
                tap_of == 3 * dr + dc, moved[dc][dr * IMG_W : dr * IMG_W + count], taps
            )
    hidden = jnp.dot(taps.astype(jnp.bfloat16), fold_ref[...], preferred_element_type=jnp.float32)

    line = lax.broadcasted_iota(jnp.int32, (count, 1), 0) // IMG_W + TILE_H * section - 1
    inside = (line >= 0) & (line < IMG_SPLIT * TILE_H)
    activated = jnp.where(inside, hidden * jax.nn.sigmoid(hidden), 0.0).astype(jnp.bfloat16)

    count = count - 2 * IMG_W
    column = lax.broadcasted_iota(jnp.int32, (count, 1), 0) % IMG_W
    summed = part = None
    for at, (dr, dc) in enumerate(TAPS):
        if at == 0:
            for copy in copies[:EARLY]:
                copy.wait()
        if at == EARLY:
            for copy in copies[EARLY:]:
                copy.wait()
        term = jnp.dot(
            activated[dr * IMG_W : dr * IMG_W + count],
            two_ref[at],
            preferred_element_type=jnp.float32,
        )
        part = term if part is None else part + term
        if dr < 2:
            continue
        if dc == 0:
            part = jnp.where(column == 0, 0.0, pltpu.roll(part, 1, 0))
        if dc == 2:
            part = jnp.where(column == IMG_W - 1, 0.0, pltpu.roll(part, count - 1, 0))
        summed = part if summed is None else summed + part
        part = None
    out_ref[...] = summed.astype(jnp.bfloat16)


def near(array):
    return pltpu.with_memory_space_constraint(array, pltpu.VMEM)


def far(array):
    return pltpu.with_memory_space_constraint(array, pltpu.HBM)


def on_device(
    queries,
    new_keys,
    new_values,
    cache_keys,
    cache_values,
    cache_lengths,
    out_weight,
    codes,
    tile_slot,
    code_weight,
    conv_one,
    conv_two,
):
    tiles = lax.axis_size("rows")
    rows, width = queries.shape
    channels = code_weight.shape[1]
    share = width // tiles
    per = 2 * share // LANES
    feature_rows = rows * per
    depth = message_rows(feature_rows)
    half = width // 2
    lines = 8
    groups = half // (lines * LANES)
    params = pltpu.CompilerParams(vmem_limit_bytes=VMEM_LIMIT)
    vmem = pl.BlockSpec(memory_space=pltpu.VMEM)
    anywhere = pl.BlockSpec(memory_space=pl.ANY)

    outgoing, give = pl.pallas_call(
        functools.partial(attend_kernel, tiles=tiles, per=per, feature_rows=feature_rows),
        in_specs=[anywhere] * 9,
        out_specs=[vmem, vmem],
        out_shape=[
            pltpu.VMEM((tiles, depth, LANES), jnp.bfloat16),
            pltpu.VMEM((share, half), out_weight.dtype),
        ],
        scratch_shapes=[
            pltpu.VMEM(queries.shape, queries.dtype),
            pltpu.VMEM(new_keys.shape, new_keys.dtype),
            pltpu.VMEM(new_values.shape, new_values.dtype),
            pltpu.VMEM((rows * cache_keys.shape[1] + 16, width), cache_keys.dtype),
            pltpu.VMEM((rows * cache_values.shape[1] + 16, width), cache_values.dtype),
            pltpu.VMEM(codes.shape, codes.dtype),
            pltpu.VMEM((tiles, depth, LANES), jnp.float32),
            pltpu.VMEM((LANES, LANES), jnp.float32),
            pltpu.VMEM((width, LANES), jnp.bfloat16),
            pltpu.SMEM(cache_lengths.shape, cache_lengths.dtype),
            pltpu.SMEM(tile_slot.shape, tile_slot.dtype),
            pltpu.SemaphoreType.DMA((7 + 2 * rows,)),
        ],
        compiler_params=pltpu.CompilerParams(vmem_limit_bytes=56 * 1024 * 1024),
    )(
        far(cache_lengths),
        far(tile_slot),
        far(queries),
        far(new_keys),
        far(new_values),
        far(cache_keys),
        far(cache_values),
        far(codes),
        far(out_weight),
    )
    order = [[member(at, tiles) for at in range(tiles)]]
    incoming = lax.all_to_all(
        outgoing, "rows", split_axis=0, concat_axis=0, axis_index_groups=order, tiled=True
    )
    other = lax.ppermute(give, "rows", [(i, i ^ 1) for i in range(tiles)])

    folded, own = pl.pallas_call(
        fold_kernel,
        in_specs=[vmem, anywhere, anywhere, anywhere],
        out_specs=[vmem, vmem],
        out_shape=[
            jax.ShapeDtypeStruct((FOLD_ROWS, channels), jnp.bfloat16),
            pltpu.VMEM((share, half), out_weight.dtype),
        ],
        scratch_shapes=[
            pltpu.VMEM((8, channels), jnp.float32),
            pltpu.VMEM((FOLD_ROWS, channels), jnp.float32),
            pltpu.VMEM((9,) + conv_one.shape[2:], conv_one.dtype),
            pltpu.SemaphoreType.DMA((9,)),
            pltpu.SemaphoreType.DMA,
        ],
        compiler_params=params,
    )(far(code_weight), far(conv_one), far(out_weight), near(outgoing))

    partials = pl.pallas_call(
        functools.partial(project_kernel, rows=rows, per=per),
        in_specs=[vmem, vmem, vmem],
        out_shape=pltpu.VMEM((tiles, groups, rows * lines, LANES), jnp.bfloat16),
        scratch_shapes=[
            pltpu.VMEM((tiles * depth, LANES), jnp.float32),
            pltpu.VMEM((groups, tiles * rows * lines, LANES), jnp.float32),
        ],
        compiler_params=params,
    )(near(incoming), near(own), near(other))
    gathered = lax.all_to_all(
        partials, "rows", split_axis=0, concat_axis=0, axis_index_groups=order, tiled=True
    )

    decoded = pl.pallas_call(
        functools.partial(decode_kernel, feature_rows=feature_rows),
        in_specs=[vmem, vmem, anywhere, anywhere],
        out_specs=vmem,
        out_shape=jax.ShapeDtypeStruct((TILE_H * IMG_W, channels), jnp.bfloat16),
        scratch_shapes=[
            pltpu.VMEM((len(TAPS),) + conv_two.shape[2:], conv_two.dtype),
            pltpu.SemaphoreType.DMA((len(TAPS),)),
        ],
        compiler_params=params,
    )(near(incoming), near(folded), far(conv_two), near(partials))

    mixed = pl.pallas_call(
        functools.partial(total_kernel, rows=rows),
        in_specs=[vmem],
        out_shape=jax.ShapeDtypeStruct((rows, width), jnp.bfloat16),
        scratch_shapes=[pltpu.VMEM((2 * groups, rows * lines, LANES), jnp.float32)],
        compiler_params=params,
    )(near(gathered))
    return (mixed, decoded.reshape(TILE_H, IMG_W, channels))


def solution(mesh):
    in_specs = (
        P(("groups", "rows"), None),
        P(("groups", "rows"), None),
        P(("groups", "rows"), None),
        P(("groups", "rows"), None, None),
        P(("groups", "rows"), None, None),
        P(("groups", "rows")),
        P("rows", None),
        P(("groups", "rows"), None),
        P(("groups", "rows")),
        P(),
        P(),
        P(),
    )
    out_specs = (P(("groups", "rows"), None), P(("groups", "rows"), None, None))
    return jax.shard_map(
        on_device, mesh=mesh, in_specs=in_specs, out_specs=out_specs, check_vma=False
    )
```

```python
import functools
import math

import jax
import jax.numpy as jnp
from jax import lax
from jax.experimental import pallas as pl
from jax.experimental.pallas import tpu as pltpu
from jax.sharding import PartitionSpec as P

HEAD_DIM = 128
FSQ_DIMS = 5
IMG_SPLIT = 4
TILE_H = 8
IMG_W = 48
LANES = 128
HALO = 2
ROW_WORDS = IMG_W // 2
TILE_ROWS = TILE_H + 2 * HALO
WINDOW = 3
PIECES = 2
CODE_ROWS = WINDOW * PIECES
TAP_ROWS = 24
FOLD_ROWS = 256
TAPS = [(dr, dc) for dc in (1, 0, 2) for dr in range(3)]
EARLY = 3
VMEM_LIMIT = 24 * 1024 * 1024


def window_start(section):
    return (TILE_H * ROW_WORDS * section - HALO * ROW_WORDS) // LANES


def member(at, tiles):
    return (at + tiles // 4 * 2) % tiles


def message_rows(features):
    return -(-(features + CODE_ROWS) // 16) * 16


def encode(code):
    fraction = (code & 127).astype(jnp.float32) * (1.0 / 128.0) + 1.0
    for bit in range(7):
        up = ((code >> (7 + bit)) & 1) == 1
        fraction = jnp.where(up, fraction * 2.0 ** (1 << bit), fraction)
        if bit == 5:
            fraction = fraction * 2.0**-64
    return jnp.where(((code >> 14) & 1) == 1, -fraction, fraction)


def decode_number(value):
    size = jnp.abs(value)
    code = jnp.where(value < 0.0, 1 << 14, 0)
    for bit in range(6, -1, -1):
        step = 1 << bit
        up = size >= 2.0 ** (step - 64)
        code = code + jnp.where(up, step << 7, 0)
        size = jnp.where(up, size * 2.0**-step, size)
    return code + ((size * 2.0**64 - 1.0) * 128.0).astype(jnp.int32)


def attend_kernel(
    lengths_any,
    slots_any,
    q_any,
    nk_any,
    nv_any,
    k_any,
    v_any,
    codes_any,
    weight_any,
    out_ref,
    give_ref,
    q_ref,
    nk_ref,
    nv_ref,
    k_ref,
    v_ref,
    codes_ref,
    msg,
    by_head,
    spread,
    lengths,
    slots,
    sems,
    *,
    tiles,
    per,
    feature_rows,
):
    rows, width = q_ref.shape
    give_columns = give_ref.shape[1]
    small = [
        pltpu.make_async_copy(source, target, sems.at[at])
        for at, (source, target) in enumerate(
            (
                (q_any, q_ref),
                (nk_any, nk_ref),
                (nv_any, nv_ref),
                (codes_any, codes_ref),
                (lengths_any, lengths),
                (slots_any, slots),
            )
        )
    ]
    cached = k_any.shape[1]
    keys, values = (
        [
            pltpu.make_async_copy(
                source.at[r], target.at[pl.ds(r * cached, cached)], sems.at[base + r]
            )
            for r in range(rows)
        ]
        for source, target, base in ((k_any, k_ref, 6), (v_any, v_ref, 6 + rows))
    )
    begin = pl.multiple_of((1 - lax.axis_index("rows") % 2) * give_columns, LANES)
    give = pltpu.make_async_copy(
        weight_any.at[:, pl.ds(begin, give_columns)], give_ref, sems.at[6 + 2 * rows]
    )
    for copy in small + keys + values:
        copy.start()

    heads = width // HEAD_DIM
    factor = 1.0 / math.sqrt(HEAD_DIM)
    msg[...] = jnp.zeros_like(msg)
    for copy in small:
        copy.wait()

    queries = q_ref[...].astype(jnp.float32)
    by_head[...] = jnp.zeros_like(by_head)
    for r in range(rows):
        for head in range(heads):
            by_head[r * heads + head : r * heads + head + 1, :] = queries[
                r : r + 1, head * LANES : (head + 1) * LANES
            ]
    turned = by_head[...].T
    column = lax.broadcasted_iota(jnp.int32, (1, LANES), 1)
    for head in range(heads):
        spread[head * LANES : (head + 1) * LANES, :] = jnp.where(
            column % heads == head, turned, 0.0
        ).astype(jnp.bfloat16)
    padding = jnp.zeros((16 - rows, width), jnp.float32)
    known = rows * cached
    k_ref[known:, :] = jnp.concatenate([nk_ref[...].astype(jnp.float32), padding], 0).astype(
        jnp.bfloat16
    )
    v_ref[known:, :] = jnp.concatenate([nv_ref[...].astype(jnp.float32), padding], 0).astype(
        jnp.bfloat16
    )
    for copy in keys:
        copy.wait()
    products = jnp.dot(k_ref[...], spread[...], preferred_element_type=jnp.float32) * factor
    words = codes_ref[...]
    blocks = words.shape[1] // LANES
    pieces = [encode(words & 32767), encode(words >> 15)]
    for slot in range(tiles // IMG_SPLIT):
        gains = [
            jnp.where(slots[r] == slot, 1.0, 0.0).astype(jnp.float32) for r in range(rows)
        ]
        for at, piece in enumerate(pieces):
            total = piece[0:1] * gains[0]
            for r in range(1, rows):
                total = total + piece[r : r + 1] * gains[r]
            for tile in range(tiles):
                number = (member(tile, tiles) + IMG_SPLIT // 2) % tiles
                if number // IMG_SPLIT != slot:
                    continue
                for step in range(WINDOW):
                    block = window_start(number % IMG_SPLIT) + step
                    if block < 0 or block >= blocks:
                        continue
                    place = feature_rows + at * WINDOW + step
                    msg[tile, place : place + 1, :] = total[:, block * LANES : (block + 1) * LANES]

    own_scores = products[known:]
    scores = products[:known]
    owner = column // heads
    own_at = lax.broadcasted_iota(jnp.int32, own_scores.shape, 0) == owner
    own_score = jnp.sum(jnp.where(own_at, own_scores, 0.0), 0, keepdims=True)
    limit = jnp.zeros(column.shape, jnp.int32)
    for r in range(rows):
        limit = jnp.where(owner == r, lengths[r], limit)
    position = lax.broadcasted_iota(jnp.int32, scores.shape, 0) - owner * cached
    live = (position >= 0) & (position < limit)
    scores = jnp.where(live, scores, jnp.float32(-1e30))
    highest = jnp.maximum(jnp.max(scores, 0, keepdims=True), own_score)
    cache_exp = jnp.where(live, jnp.exp(scores - highest), 0.0)
    own_exp = jnp.exp(own_score - highest)
    denom = jnp.sum(cache_exp, 0, keepdims=True) + own_exp
    cache_weight = (cache_exp / denom).T[: rows * heads]
    own_weight = jnp.where(own_at, own_exp / denom, 0.0)
    own_weight = jnp.concatenate(
        [own_weight, jnp.zeros((LANES - own_weight.shape[0], LANES), jnp.float32)], 0
    ).T[: rows * heads, :16]
    weight = jnp.concatenate([cache_weight, own_weight], 1).astype(jnp.bfloat16)
    for copy in values:
        copy.wait()
    give.start()
    attended = jnp.dot(weight, v_ref[...], preferred_element_type=jnp.float32)
    for tile in range(tiles):
        for r in range(rows):
            for step in range(per):
                head = member(tile, tiles) // 2 * per + step
                place = r * per + step
                msg[tile, place : place + 1, :] = attended[
                    r * heads + head : r * heads + head + 1, head * LANES : (head + 1) * LANES
                ]
    out_ref[...] = msg[...].astype(jnp.bfloat16)
    give.wait()


def project_kernel(in_ref, own_ref, other_ref, out_ref, held, total, *, rows, per):
    tiles, depth = in_ref.shape[:2]
    held[...] = in_ref[...].astype(jnp.float32).reshape(held.shape)
    groups = total.shape[0]
    lines = out_ref.shape[2] // rows
    share = own_ref.shape[0]
    lhs = []
    for row in range(rows):
        parts = [held[pl.ds(row * per + j, tiles, stride=depth), :] for j in range(per)]
        lhs.append(jnp.concatenate(parts, 1))
    lhs = jnp.concatenate(lhs, 0)
    even = lax.axis_index("rows") % 2 == 0
    first, second = lhs[:, :share], lhs[:, share:]
    own = jnp.where(even, first, second).astype(jnp.bfloat16)
    other = jnp.where(even, second, first).astype(jnp.bfloat16)
    product = jnp.dot(own, own_ref[...], preferred_element_type=jnp.float32) + jnp.dot(
        other, other_ref[...], preferred_element_type=jnp.float32
    )
    for row in range(rows):
        for group in range(groups):
            for line in range(lines):
                begin = (group * lines + line) * LANES
                total[group, pl.ds(row * lines + line, tiles, stride=rows * lines), :] = product[
                    row * tiles : (row + 1) * tiles, begin : begin + LANES
                ]
    for group in range(groups):
        out_ref[:, group] = (
            total[group].astype(jnp.bfloat16).reshape(tiles, rows * lines, LANES)
        )


def total_kernel(in_ref, out_ref, held, *, rows):
    tiles, groups, depth, _ = in_ref.shape
    lines = depth // rows
    parts = in_ref[...].astype(jnp.float32).reshape(tiles // 2, 2 * groups, depth, LANES)
    held[...] = jnp.sum(parts, 0)
    for group in range(2 * groups):
        for line in range(lines):
            begin = (group * lines + line) * LANES
            out_ref[:, begin : begin + LANES] = held[
                group, pl.ds(line, rows, stride=lines), :
            ].astype(jnp.bfloat16)


def split_three(whole):
    high = whole.astype(jnp.bfloat16).astype(jnp.float32)
    middle = (whole - high).astype(jnp.bfloat16).astype(jnp.float32)
    return jnp.concatenate([high, middle, whole - high - middle], 0)


def fold_kernel(
    cw_ref, conv_ref, weight_ref, after_ref, out_ref, near_ref, levels_w, folded, held, sems, near_sem
):
    del after_ref
    taps = [(dr, dc) for dr in range(3) for dc in range(3)]
    copies = [
        pltpu.make_async_copy(conv_ref.at[dr, dc], held.at[at], sems.at[at])
        for at, (dr, dc) in enumerate(taps)
    ]
    for copy in copies:
        copy.start()
    begin = pl.multiple_of(lax.axis_index("rows") % 2 * near_ref.shape[1], LANES)
    bring = pltpu.make_async_copy(
        weight_ref.at[:, pl.ds(begin, near_ref.shape[1])], near_ref, near_sem
    )
    bring.start()
    levels_w[...] = jnp.zeros_like(levels_w)
    levels_w[0:FSQ_DIMS, :] = cw_ref[...]
    left = split_three(levels_w[...]).astype(jnp.bfloat16)
    folded[...] = jnp.zeros_like(folded)
    for at, copy in enumerate(copies):
        copy.wait()
        parts = jnp.dot(left, held[at], preferred_element_type=jnp.float32)
        total = parts[0:8] + parts[8:16] + parts[16:24]
        folded[at * TAP_ROWS : (at + 1) * TAP_ROWS, :] = split_three(total)
    out_ref[...] = folded[...].astype(jnp.bfloat16)
    bring.wait()


def decode_kernel(
    in_ref, fold_ref, two_any, after_ref, out_ref, two_ref, sems, *, feature_rows
):
    del after_ref
    copies = [
        pltpu.make_async_copy(two_any.at[dr, dc], two_ref.at[at], sems.at[at])
        for at, (dr, dc) in enumerate(TAPS)
    ]
    for copy in copies[:EARLY]:
        copy.start()
    tiles = lax.axis_size("rows")
    section = (lax.axis_index("rows") + IMG_SPLIT // 2) % tiles % IMG_SPLIT
    got = jnp.sum(in_ref[...].astype(jnp.float32), 0)
    pieces = []
    for at in range(PIECES):
        lines = [
            got[feature_rows + at * WINDOW + step : feature_rows + at * WINDOW + step + 1]
            for step in range(WINDOW)
        ]
        pieces.append(jnp.concatenate(lines, 1))
    codes = decode_number(jnp.concatenate(pieces, 1))
    span = codes.shape[1]
    depth = fold_ref.shape[0]
    level = lax.broadcasted_iota(jnp.int32, (8, span), 0)
    taken = level < FSQ_DIMS
    shift = jnp.where(taken, level * 3, 0)
    value = (2 * ((jnp.broadcast_to(codes, (8, span)) >> shift) & 7) - 7).astype(
        jnp.float32
    ) * 0.125
    value = jnp.where(taken, value, 0.0)
    value = jnp.concatenate([value] * (depth // 8), 0).astype(jnp.bfloat16)

    count = TILE_ROWS * IMG_W
    begin = TILE_H * ROW_WORDS * section - HALO * ROW_WORDS
    offset = begin & (LANES - 1)
    spot = lax.broadcasted_iota(jnp.int32, (count, 1), 0)
    line = spot // IMG_W + TILE_H * section - HALO
    inside = (line >= 0) & (line < IMG_SPLIT * TILE_H)
    target = jnp.where(inside, (spot >> 1) + offset + (span // 2) * (spot & 1), -1)
    chooser = jnp.where(
        lax.broadcasted_iota(jnp.int32, (count, span), 1) == target, 1.0, 0.0
    ).astype(jnp.bfloat16)
    placed = lax.dot_general(
        chooser, value, (((1,), (1,)), ((), ())), preferred_element_type=jnp.float32
    )
    for copy in copies[EARLY:]:
        copy.start()
    column = spot % IMG_W
    moved = [
        jnp.where(column == 0, 0.0, pltpu.roll(placed, 1, 0)),
        placed,
        jnp.where(column == IMG_W - 1, 0.0, pltpu.roll(placed, count - 1, 0)),
    ]
    count = count - 2 * IMG_W
    tap_of = lax.broadcasted_iota(jnp.int32, (1, depth), 1) // TAP_ROWS
    taps = jnp.zeros((count, depth), jnp.float32)
    for dr in range(3):
        for dc in range(3):
            taps = jnp.where(
                tap_of == 3 * dr + dc, moved[dc][dr * IMG_W : dr * IMG_W + count], taps
            )
    hidden = jnp.dot(taps.astype(jnp.bfloat16), fold_ref[...], preferred_element_type=jnp.float32)

    line = lax.broadcasted_iota(jnp.int32, (count, 1), 0) // IMG_W + TILE_H * section - 1
    inside = (line >= 0) & (line < IMG_SPLIT * TILE_H)
    activated = jnp.where(inside, hidden * jax.nn.sigmoid(hidden), 0.0).astype(jnp.bfloat16)

    count = count - 2 * IMG_W
    column = lax.broadcasted_iota(jnp.int32, (count, 1), 0) % IMG_W
    summed = part = None
    for at, (dr, dc) in enumerate(TAPS):
        if at == 0:
            for copy in copies[:EARLY]:
                copy.wait()
        if at == EARLY:
            for copy in copies[EARLY:]:
                copy.wait()
        term = jnp.dot(
            activated[dr * IMG_W : dr * IMG_W + count],
            two_ref[at],
            preferred_element_type=jnp.float32,
        )
        part = term if part is None else part + term
        if dr < 2:
            continue
        if dc == 0:
            part = jnp.where(column == 0, 0.0, pltpu.roll(part, 1, 0))
        if dc == 2:
            part = jnp.where(column == IMG_W - 1, 0.0, pltpu.roll(part, count - 1, 0))
        summed = part if summed is None else summed + part
        part = None
    out_ref[...] = summed.astype(jnp.bfloat16)


def near(array):
    return pltpu.with_memory_space_constraint(array, pltpu.VMEM)


def far(array):
    return pltpu.with_memory_space_constraint(array, pltpu.HBM)


def on_device(
    queries,
    new_keys,
    new_values,
    cache_keys,
    cache_values,
    cache_lengths,
    out_weight,
    codes,
    tile_slot,
    code_weight,
    conv_one,
    conv_two,
):
    tiles = lax.axis_size("rows")
    rows, width = queries.shape
    channels = code_weight.shape[1]
    share = width // tiles
    per = 2 * share // LANES
    feature_rows = rows * per
    depth = message_rows(feature_rows)
    half = width // 2
    lines = 8
    groups = half // (lines * LANES)
    params = pltpu.CompilerParams(vmem_limit_bytes=VMEM_LIMIT)
    vmem = pl.BlockSpec(memory_space=pltpu.VMEM)
    anywhere = pl.BlockSpec(memory_space=pl.ANY)

    outgoing, give = pl.pallas_call(
        functools.partial(attend_kernel, tiles=tiles, per=per, feature_rows=feature_rows),
        in_specs=[anywhere] * 9,
        out_specs=[vmem, vmem],
        out_shape=[
            pltpu.VMEM((tiles, depth, LANES), jnp.bfloat16),
            pltpu.VMEM((share, half), out_weight.dtype),
        ],
        scratch_shapes=[
            pltpu.VMEM(queries.shape, queries.dtype),
            pltpu.VMEM(new_keys.shape, new_keys.dtype),
            pltpu.VMEM(new_values.shape, new_values.dtype),
            pltpu.VMEM((rows * cache_keys.shape[1] + 16, width), cache_keys.dtype),
            pltpu.VMEM((rows * cache_values.shape[1] + 16, width), cache_values.dtype),
            pltpu.VMEM(codes.shape, codes.dtype),
            pltpu.VMEM((tiles, depth, LANES), jnp.float32),
            pltpu.VMEM((LANES, LANES), jnp.float32),
            pltpu.VMEM((width, LANES), jnp.bfloat16),
            pltpu.SMEM(cache_lengths.shape, cache_lengths.dtype),
            pltpu.SMEM(tile_slot.shape, tile_slot.dtype),
            pltpu.SemaphoreType.DMA((7 + 2 * rows,)),
        ],
        compiler_params=pltpu.CompilerParams(vmem_limit_bytes=56 * 1024 * 1024),
    )(
        far(cache_lengths),
        far(tile_slot),
        far(queries),
        far(new_keys),
        far(new_values),
        far(cache_keys),
        far(cache_values),
        far(codes),
        far(out_weight),
    )
    order = [[member(at, tiles) for at in range(tiles)]]
    incoming = lax.all_to_all(
        outgoing, "rows", split_axis=0, concat_axis=0, axis_index_groups=order, tiled=True
    )
    other = lax.ppermute(give, "rows", [(i, i ^ 1) for i in range(tiles)])

    folded, own = pl.pallas_call(
        fold_kernel,
        in_specs=[vmem, anywhere, anywhere, anywhere],
        out_specs=[vmem, vmem],
        out_shape=[
            jax.ShapeDtypeStruct((FOLD_ROWS, channels), jnp.bfloat16),
            pltpu.VMEM((share, half), out_weight.dtype),
        ],
        scratch_shapes=[
            pltpu.VMEM((8, channels), jnp.float32),
            pltpu.VMEM((FOLD_ROWS, channels), jnp.float32),
            pltpu.VMEM((9,) + conv_one.shape[2:], conv_one.dtype),
            pltpu.SemaphoreType.DMA((9,)),
            pltpu.SemaphoreType.DMA,
        ],
        compiler_params=params,
    )(far(code_weight), far(conv_one), far(out_weight), near(outgoing))

    partials = pl.pallas_call(
        functools.partial(project_kernel, rows=rows, per=per),
        in_specs=[vmem, vmem, vmem],
        out_shape=pltpu.VMEM((tiles, groups, rows * lines, LANES), jnp.bfloat16),
        scratch_shapes=[
            pltpu.VMEM((tiles * depth, LANES), jnp.float32),
            pltpu.VMEM((groups, tiles * rows * lines, LANES), jnp.float32),
        ],
        compiler_params=params,
    )(near(incoming), near(own), near(other))
    gathered = lax.all_to_all(
        partials, "rows", split_axis=0, concat_axis=0, axis_index_groups=order, tiled=True
    )

    decoded = pl.pallas_call(
        functools.partial(decode_kernel, feature_rows=feature_rows),
        in_specs=[vmem, vmem, anywhere, anywhere],
        out_specs=vmem,
        out_shape=jax.ShapeDtypeStruct((TILE_H * IMG_W, channels), jnp.bfloat16),
        scratch_shapes=[
            pltpu.VMEM((len(TAPS),) + conv_two.shape[2:], conv_two.dtype),
            pltpu.SemaphoreType.DMA((len(TAPS),)),
        ],
        compiler_params=params,
    )(near(incoming), near(folded), far(conv_two), near(partials))

    mixed = pl.pallas_call(
        functools.partial(total_kernel, rows=rows),
        in_specs=[vmem],
        out_shape=jax.ShapeDtypeStruct((rows, width), jnp.bfloat16),
        scratch_shapes=[pltpu.VMEM((2 * groups, rows * lines, LANES), jnp.float32)],
        compiler_params=params,
    )(near(gathered))
    return (mixed, decoded.reshape(TILE_H, IMG_W, channels))


def solution(mesh):
    in_specs = (
        P(("groups", "rows"), None),
        P(("groups", "rows"), None),
        P(("groups", "rows"), None),
        P(("groups", "rows"), None, None),
        P(("groups", "rows"), None, None),
        P(("groups", "rows")),
        P("rows", None),
        P(("groups", "rows"), None),
        P(("groups", "rows")),
        P(),
        P(),
        P(),
    )
    out_specs = (P(("groups", "rows"), None), P(("groups", "rows"), None, None))
    return jax.shard_map(
        on_device, mesh=mesh, in_specs=in_specs, out_specs=out_specs, check_vma=False
    )
```

```python
import functools
import math

import jax
import jax.numpy as jnp
from jax import lax
from jax.experimental import pallas as pl
from jax.experimental.pallas import tpu as pltpu
from jax.sharding import PartitionSpec as P

HEAD_DIM = 128
FSQ_DIMS = 5
IMG_SPLIT = 4
TILE_H = 8
IMG_W = 48
LANES = 128
HALO = 2
ROW_WORDS = IMG_W // 2
TILE_ROWS = TILE_H + 2 * HALO
WINDOW = 3
PIECES = 2
CODE_ROWS = WINDOW * PIECES
TAP_ROWS = 24
FOLD_ROWS = 256
TAPS = [(dr, dc) for dc in (1, 0, 2) for dr in range(3)]
EARLY = 3
VMEM_LIMIT = 24 * 1024 * 1024


def window_start(section):
    return (TILE_H * ROW_WORDS * section - HALO * ROW_WORDS) // LANES


def member(at, tiles):
    return (at + tiles // 4 * 2) % tiles


def message_rows(features):
    return -(-(features + CODE_ROWS) // 16) * 16


def encode(code):
    fraction = (code & 127).astype(jnp.float32) * (1.0 / 128.0) + 1.0
    for bit in range(7):
        up = ((code >> (7 + bit)) & 1) == 1
        fraction = jnp.where(up, fraction * 2.0 ** (1 << bit), fraction)
        if bit == 5:
            fraction = fraction * 2.0**-64
    return jnp.where(((code >> 14) & 1) == 1, -fraction, fraction)


def decode_number(value):
    size = jnp.abs(value)
    code = jnp.where(value < 0.0, 1 << 14, 0)
    for bit in range(6, -1, -1):
        step = 1 << bit
        up = size >= 2.0 ** (step - 64)
        code = code + jnp.where(up, step << 7, 0)
        size = jnp.where(up, size * 2.0**-step, size)
    return code + ((size * 2.0**64 - 1.0) * 128.0).astype(jnp.int32)


def attend_kernel(
    lengths_any,
    slots_any,
    q_any,
    nk_any,
    nv_any,
    k_any,
    v_any,
    codes_any,
    out_ref,
    q_ref,
    nk_ref,
    nv_ref,
    k_ref,
    v_ref,
    codes_ref,
    msg,
    by_head,
    spread,
    lengths,
    slots,
    sems,
    *,
    tiles,
    per,
    feature_rows,
):
    rows, width = q_ref.shape
    small = [
        pltpu.make_async_copy(source, target, sems.at[at])
        for at, (source, target) in enumerate(
            (
                (q_any, q_ref),
                (nk_any, nk_ref),
                (nv_any, nv_ref),
                (codes_any, codes_ref),
                (lengths_any, lengths),
                (slots_any, slots),
            )
        )
    ]
    cached = k_any.shape[1]
    keys, values = (
        [
            pltpu.make_async_copy(
                source.at[r], target.at[pl.ds(r * cached, cached)], sems.at[base + r]
            )
            for r in range(rows)
        ]
        for source, target, base in ((k_any, k_ref, 6), (v_any, v_ref, 6 + rows))
    )
    for copy in small:
        copy.start()
    for copy in keys:
        copy.start()

    heads = width // HEAD_DIM
    factor = 1.0 / math.sqrt(HEAD_DIM)
    msg[...] = jnp.zeros_like(msg)
    for copy in small:
        copy.wait()
    for copy in values:
        copy.start()

    queries = q_ref[...].astype(jnp.float32)
    by_head[...] = jnp.zeros_like(by_head)
    for r in range(rows):
        for head in range(heads):
            by_head[r * heads + head : r * heads + head + 1, :] = queries[
                r : r + 1, head * LANES : (head + 1) * LANES
            ]
    turned = by_head[...].T
    column = lax.broadcasted_iota(jnp.int32, (1, LANES), 1)
    for head in range(heads):
        spread[head * LANES : (head + 1) * LANES, :] = jnp.where(
            column % heads == head, turned, 0.0
        ).astype(jnp.bfloat16)
    padding = jnp.zeros((16 - rows, width), jnp.float32)
    known = rows * cached
    k_ref[known:, :] = jnp.concatenate([nk_ref[...].astype(jnp.float32), padding], 0).astype(
        jnp.bfloat16
    )
    v_ref[known:, :] = jnp.concatenate([nv_ref[...].astype(jnp.float32), padding], 0).astype(
        jnp.bfloat16
    )
    for copy in keys:
        copy.wait()
    products = jnp.dot(k_ref[...], spread[...], preferred_element_type=jnp.float32) * factor
    words = codes_ref[...]
    blocks = words.shape[1] // LANES
    pieces = [encode(words & 32767), encode(words >> 15)]
    for slot in range(tiles // IMG_SPLIT):
        gains = [
            jnp.where(slots[r] == slot, 1.0, 0.0).astype(jnp.float32) for r in range(rows)
        ]
        for at, piece in enumerate(pieces):
            total = piece[0:1] * gains[0]
            for r in range(1, rows):
                total = total + piece[r : r + 1] * gains[r]
            for tile in range(tiles):
                number = (member(tile, tiles) + IMG_SPLIT // 2) % tiles
                if number // IMG_SPLIT != slot:
                    continue
                for step in range(WINDOW):
                    block = window_start(number % IMG_SPLIT) + step
                    if block < 0 or block >= blocks:
                        continue
                    place = feature_rows + at * WINDOW + step
                    msg[tile, place : place + 1, :] = total[:, block * LANES : (block + 1) * LANES]

    own_scores = products[known:]
    scores = products[:known]
    owner = column // heads
    own_at = lax.broadcasted_iota(jnp.int32, own_scores.shape, 0) == owner
    own_score = jnp.sum(jnp.where(own_at, own_scores, 0.0), 0, keepdims=True)
    limit = jnp.zeros(column.shape, jnp.int32)
    for r in range(rows):
        limit = jnp.where(owner == r, lengths[r], limit)
    position = lax.broadcasted_iota(jnp.int32, scores.shape, 0) - owner * cached
    live = (position >= 0) & (position < limit)
    scores = jnp.where(live, scores, jnp.float32(-1e30))
    highest = jnp.maximum(jnp.max(scores, 0, keepdims=True), own_score)
    cache_exp = jnp.where(live, jnp.exp(scores - highest), 0.0)
    own_exp = jnp.exp(own_score - highest)
    denom = jnp.sum(cache_exp, 0, keepdims=True) + own_exp
    cache_weight = (cache_exp / denom).T[: rows * heads]
    own_weight = jnp.where(own_at, own_exp / denom, 0.0)
    own_weight = jnp.concatenate(
        [own_weight, jnp.zeros((LANES - own_weight.shape[0], LANES), jnp.float32)], 0
    ).T[: rows * heads, :16]
    weight = jnp.concatenate([cache_weight, own_weight], 1).astype(jnp.bfloat16)
    for copy in values:
        copy.wait()
    attended = jnp.dot(weight, v_ref[...], preferred_element_type=jnp.float32)
    for tile in range(tiles):
        for r in range(rows):
            for step in range(per):
                head = member(tile, tiles) // 2 * per + step
                place = r * per + step
                msg[tile, place : place + 1, :] = attended[
                    r * heads + head : r * heads + head + 1, head * LANES : (head + 1) * LANES
                ]
    out_ref[...] = msg[...].astype(jnp.bfloat16)


def project_kernel(in_ref, own_ref, other_ref, out_ref, held, total, *, rows, per):
    tiles, depth = in_ref.shape[:2]
    held[...] = in_ref[...].astype(jnp.float32).reshape(held.shape)
    groups = total.shape[0]
    lines = out_ref.shape[2] // rows
    share = own_ref.shape[0]
    lhs = []
    for row in range(rows):
        parts = [held[pl.ds(row * per + j, tiles, stride=depth), :] for j in range(per)]
        lhs.append(jnp.concatenate(parts, 1))
    lhs = jnp.concatenate(lhs, 0)
    even = lax.axis_index("rows") % 2 == 0
    first, second = lhs[:, :share], lhs[:, share:]
    own = jnp.where(even, first, second).astype(jnp.bfloat16)
    other = jnp.where(even, second, first).astype(jnp.bfloat16)
    product = jnp.dot(own, own_ref[...], preferred_element_type=jnp.float32) + jnp.dot(
        other, other_ref[...], preferred_element_type=jnp.float32
    )
    for row in range(rows):
        for group in range(groups):
            for line in range(lines):
                begin = (group * lines + line) * LANES
                total[group, pl.ds(row * lines + line, tiles, stride=rows * lines), :] = product[
                    row * tiles : (row + 1) * tiles, begin : begin + LANES
                ]
    for group in range(groups):
        out_ref[:, group] = (
            total[group].astype(jnp.bfloat16).reshape(tiles, rows * lines, LANES)
        )


def total_kernel(in_ref, out_ref, held, *, rows):
    tiles, groups, depth, _ = in_ref.shape
    lines = depth // rows
    parts = in_ref[...].astype(jnp.float32).reshape(tiles // 2, 2 * groups, depth, LANES)
    held[...] = jnp.sum(parts, 0)
    for group in range(2 * groups):
        for line in range(lines):
            begin = (group * lines + line) * LANES
            out_ref[:, begin : begin + LANES] = held[
                group, pl.ds(line, rows, stride=lines), :
            ].astype(jnp.bfloat16)


def split_three(whole):
    high = whole.astype(jnp.bfloat16).astype(jnp.float32)
    middle = (whole - high).astype(jnp.bfloat16).astype(jnp.float32)
    return jnp.concatenate([high, middle, whole - high - middle], 0)


def fold_kernel(
    cw_ref,
    conv_ref,
    weight_ref,
    other_ref,
    after_ref,
    out_ref,
    near_ref,
    near_other_ref,
    levels_w,
    folded,
    held,
    sems,
    near_sems,
):
    del after_ref
    taps = [(dr, dc) for dr in range(3) for dc in range(3)]
    copies = [
        pltpu.make_async_copy(conv_ref.at[dr, dc], held.at[at], sems.at[at])
        for at, (dr, dc) in enumerate(taps)
    ]
    for copy in copies:
        copy.start()
    begin = pl.multiple_of(lax.axis_index("rows") % 2 * near_ref.shape[1], LANES)
    columns = pl.ds(begin, near_ref.shape[1])
    brings = [
        pltpu.make_async_copy(source.at[:, columns], target, near_sems.at[at])
        for at, (source, target) in enumerate(((weight_ref, near_ref), (other_ref, near_other_ref)))
    ]
    for bring in brings:
        bring.start()
    levels_w[...] = jnp.zeros_like(levels_w)
    levels_w[0:FSQ_DIMS, :] = cw_ref[...]
    left = split_three(levels_w[...]).astype(jnp.bfloat16)
    folded[...] = jnp.zeros_like(folded)
    for at, copy in enumerate(copies):
        copy.wait()
        parts = jnp.dot(left, held[at], preferred_element_type=jnp.float32)
        total = parts[0:8] + parts[8:16] + parts[16:24]
        folded[at * TAP_ROWS : (at + 1) * TAP_ROWS, :] = split_three(total)
    out_ref[...] = folded[...].astype(jnp.bfloat16)
    for bring in brings:
        bring.wait()


def decode_kernel(
    in_ref, fold_ref, two_any, after_ref, out_ref, two_ref, sems, *, feature_rows
):
    del after_ref
    copies = [
        pltpu.make_async_copy(two_any.at[dr, dc], two_ref.at[at], sems.at[at])
        for at, (dr, dc) in enumerate(TAPS)
    ]
    for copy in copies[:EARLY]:
        copy.start()
    tiles = lax.axis_size("rows")
    section = (lax.axis_index("rows") + IMG_SPLIT // 2) % tiles % IMG_SPLIT
    got = jnp.sum(in_ref[...].astype(jnp.float32), 0)
    pieces = []
    for at in range(PIECES):
        lines = [
            got[feature_rows + at * WINDOW + step : feature_rows + at * WINDOW + step + 1]
            for step in range(WINDOW)
        ]
        pieces.append(jnp.concatenate(lines, 1))
    codes = decode_number(jnp.concatenate(pieces, 1))
    span = codes.shape[1]
    depth = fold_ref.shape[0]
    level = lax.broadcasted_iota(jnp.int32, (8, span), 0)
    taken = level < FSQ_DIMS
    shift = jnp.where(taken, level * 3, 0)
    value = (2 * ((jnp.broadcast_to(codes, (8, span)) >> shift) & 7) - 7).astype(
        jnp.float32
    ) * 0.125
    value = jnp.where(taken, value, 0.0)
    value = jnp.concatenate([value] * (depth // 8), 0).astype(jnp.bfloat16)

    count = TILE_ROWS * IMG_W
    begin = TILE_H * ROW_WORDS * section - HALO * ROW_WORDS
    offset = begin & (LANES - 1)
    spot = lax.broadcasted_iota(jnp.int32, (count, 1), 0)
    line = spot // IMG_W + TILE_H * section - HALO
    inside = (line >= 0) & (line < IMG_SPLIT * TILE_H)
    target = jnp.where(inside, (spot >> 1) + offset + (span // 2) * (spot & 1), -1)
    chooser = jnp.where(
        lax.broadcasted_iota(jnp.int32, (count, span), 1) == target, 1.0, 0.0
    ).astype(jnp.bfloat16)
    placed = lax.dot_general(
        chooser, value, (((1,), (1,)), ((), ())), preferred_element_type=jnp.float32
    )
    for copy in copies[EARLY:]:
        copy.start()
    column = spot % IMG_W
    moved = [
        jnp.where(column == 0, 0.0, pltpu.roll(placed, 1, 0)),
        placed,
        jnp.where(column == IMG_W - 1, 0.0, pltpu.roll(placed, count - 1, 0)),
    ]
    count = count - 2 * IMG_W
    tap_of = lax.broadcasted_iota(jnp.int32, (1, depth), 1) // TAP_ROWS
    taps = jnp.zeros((count, depth), jnp.float32)
    for dr in range(3):
        for dc in range(3):
            taps = jnp.where(
                tap_of == 3 * dr + dc, moved[dc][dr * IMG_W : dr * IMG_W + count], taps
            )
    hidden = jnp.dot(taps.astype(jnp.bfloat16), fold_ref[...], preferred_element_type=jnp.float32)

    line = lax.broadcasted_iota(jnp.int32, (count, 1), 0) // IMG_W + TILE_H * section - 1
    inside = (line >= 0) & (line < IMG_SPLIT * TILE_H)
    activated = jnp.where(inside, hidden * jax.nn.sigmoid(hidden), 0.0).astype(jnp.bfloat16)

    count = count - 2 * IMG_W
    column = lax.broadcasted_iota(jnp.int32, (count, 1), 0) % IMG_W
    summed = part = None
    for at, (dr, dc) in enumerate(TAPS):
        if at == 0:
            for copy in copies[:EARLY]:
                copy.wait()
        if at == EARLY:
            for copy in copies[EARLY:]:
                copy.wait()
        term = jnp.dot(
            activated[dr * IMG_W : dr * IMG_W + count],
            two_ref[at],
            preferred_element_type=jnp.float32,
        )
        part = term if part is None else part + term
        if dr < 2:
            continue
        if dc == 0:
            part = jnp.where(column == 0, 0.0, pltpu.roll(part, 1, 0))
        if dc == 2:
            part = jnp.where(column == IMG_W - 1, 0.0, pltpu.roll(part, count - 1, 0))
        summed = part if summed is None else summed + part
        part = None
    out_ref[...] = summed.astype(jnp.bfloat16)


def near(array):
    return pltpu.with_memory_space_constraint(array, pltpu.VMEM)


def far(array):
    return pltpu.with_memory_space_constraint(array, pltpu.HBM)


def on_device(
    queries,
    new_keys,
    new_values,
    cache_keys,
    cache_values,
    cache_lengths,
    out_weight,
    codes,
    tile_slot,
    code_weight,
    conv_one,
    conv_two,
):
    tiles = lax.axis_size("rows")
    rows, width = queries.shape
    channels = code_weight.shape[1]
    share = width // tiles
    per = 2 * share // LANES
    feature_rows = rows * per
    depth = message_rows(feature_rows)
    half = width // 2
    lines = 8
    groups = half // (lines * LANES)
    params = pltpu.CompilerParams(vmem_limit_bytes=VMEM_LIMIT)
    vmem = pl.BlockSpec(memory_space=pltpu.VMEM)
    anywhere = pl.BlockSpec(memory_space=pl.ANY)

    outgoing = pl.pallas_call(
        functools.partial(attend_kernel, tiles=tiles, per=per, feature_rows=feature_rows),
        in_specs=[anywhere] * 8,
        out_specs=vmem,
        out_shape=jax.ShapeDtypeStruct((tiles, depth, LANES), jnp.bfloat16),
        scratch_shapes=[
            pltpu.VMEM(queries.shape, queries.dtype),
            pltpu.VMEM(new_keys.shape, new_keys.dtype),
            pltpu.VMEM(new_values.shape, new_values.dtype),
            pltpu.VMEM((rows * cache_keys.shape[1] + 16, width), cache_keys.dtype),
            pltpu.VMEM((rows * cache_values.shape[1] + 16, width), cache_values.dtype),
            pltpu.VMEM(codes.shape, codes.dtype),
            pltpu.VMEM((tiles, depth, LANES), jnp.float32),
            pltpu.VMEM((LANES, LANES), jnp.float32),
            pltpu.VMEM((width, LANES), jnp.bfloat16),
            pltpu.SMEM(cache_lengths.shape, cache_lengths.dtype),
            pltpu.SMEM(tile_slot.shape, tile_slot.dtype),
            pltpu.SemaphoreType.DMA((6 + 2 * rows,)),
        ],
        compiler_params=pltpu.CompilerParams(vmem_limit_bytes=56 * 1024 * 1024),
    )(
        far(cache_lengths),
        far(tile_slot),
        far(queries),
        far(new_keys),
        far(new_values),
        far(cache_keys),
        far(cache_values),
        far(codes),
    )
    order = [[member(at, tiles) for at in range(tiles)]]
    incoming = lax.all_to_all(
        outgoing, "rows", split_axis=0, concat_axis=0, axis_index_groups=order, tiled=True
    )
    other = lax.ppermute(out_weight, "rows", [(i, i ^ 1) for i in range(tiles)])

    folded, own, other = pl.pallas_call(
        fold_kernel,
        in_specs=[vmem] + [anywhere] * 4,
        out_specs=[vmem] * 3,
        out_shape=[
            jax.ShapeDtypeStruct((FOLD_ROWS, channels), jnp.bfloat16),
            pltpu.VMEM((share, half), out_weight.dtype),
            pltpu.VMEM((share, half), out_weight.dtype),
        ],
        scratch_shapes=[
            pltpu.VMEM((8, channels), jnp.float32),
            pltpu.VMEM((FOLD_ROWS, channels), jnp.float32),
            pltpu.VMEM((9,) + conv_one.shape[2:], conv_one.dtype),
            pltpu.SemaphoreType.DMA((9,)),
            pltpu.SemaphoreType.DMA((2,)),
        ],
        compiler_params=params,
    )(far(code_weight), far(conv_one), far(out_weight), far(other), far(outgoing))

    partials = pl.pallas_call(
        functools.partial(project_kernel, rows=rows, per=per),
        in_specs=[vmem, vmem, vmem],
        out_shape=pltpu.VMEM((tiles, groups, rows * lines, LANES), jnp.bfloat16),
        scratch_shapes=[
            pltpu.VMEM((tiles * depth, LANES), jnp.float32),
            pltpu.VMEM((groups, tiles * rows * lines, LANES), jnp.float32),
        ],
        compiler_params=params,
    )(near(incoming), near(own), near(other))
    gathered = lax.all_to_all(
        partials, "rows", split_axis=0, concat_axis=0, axis_index_groups=order, tiled=True
    )

    decoded = pl.pallas_call(
        functools.partial(decode_kernel, feature_rows=feature_rows),
        in_specs=[vmem, vmem, anywhere, anywhere],
        out_specs=vmem,
        out_shape=jax.ShapeDtypeStruct((TILE_H * IMG_W, channels), jnp.bfloat16),
        scratch_shapes=[
            pltpu.VMEM((len(TAPS),) + conv_two.shape[2:], conv_two.dtype),
            pltpu.SemaphoreType.DMA((len(TAPS),)),
        ],
        compiler_params=params,
    )(near(incoming), near(folded), far(conv_two), near(partials))

    mixed = pl.pallas_call(
        functools.partial(total_kernel, rows=rows),
        in_specs=[vmem],
        out_shape=jax.ShapeDtypeStruct((rows, width), jnp.bfloat16),
        scratch_shapes=[pltpu.VMEM((2 * groups, rows * lines, LANES), jnp.float32)],
        compiler_params=params,
    )(near(gathered))
    return (mixed, decoded.reshape(TILE_H, IMG_W, channels))


def solution(mesh):
    in_specs = (
        P(("groups", "rows"), None),
        P(("groups", "rows"), None),
        P(("groups", "rows"), None),
        P(("groups", "rows"), None, None),
        P(("groups", "rows"), None, None),
        P(("groups", "rows")),
        P("rows", None),
        P(("groups", "rows"), None),
        P(("groups", "rows")),
        P(),
        P(),
        P(),
    )
    out_specs = (P(("groups", "rows"), None), P(("groups", "rows"), None, None))
    return jax.shard_map(
        on_device, mesh=mesh, in_specs=in_specs, out_specs=out_specs, check_vma=False
    )
```

```python
import functools
import math

import jax
import jax.numpy as jnp
from jax import lax
from jax.experimental import pallas as pl
from jax.experimental.pallas import tpu as pltpu
from jax.sharding import PartitionSpec as P

HEAD_DIM = 128
FSQ_DIMS = 5
IMG_SPLIT = 4
TILE_H = 8
IMG_W = 48
LANES = 128
HALO = 2
ROW_WORDS = IMG_W // 2
TILE_ROWS = TILE_H + 2 * HALO
WINDOW = 3
PIECES = 2
CODE_ROWS = WINDOW * PIECES
TAP_ROWS = 24
FOLD_ROWS = 256
TAPS = [(dr, dc) for dc in (1, 0, 2) for dr in range(3)]
EARLY = 3
VMEM_LIMIT = 24 * 1024 * 1024


def window_start(section):
    return (TILE_H * ROW_WORDS * section - HALO * ROW_WORDS) // LANES


def member(at, tiles):
    return (at + tiles // 4 * 2) % tiles


def message_rows(features):
    return -(-(features + CODE_ROWS) // 16) * 16


def encode(code):
    fraction = (code & 127).astype(jnp.float32) * (1.0 / 128.0) + 1.0
    for bit in range(7):
        up = ((code >> (7 + bit)) & 1) == 1
        fraction = jnp.where(up, fraction * 2.0 ** (1 << bit), fraction)
        if bit == 5:
            fraction = fraction * 2.0**-64
    return jnp.where(((code >> 14) & 1) == 1, -fraction, fraction)


def decode_number(value):
    size = jnp.abs(value)
    code = jnp.where(value < 0.0, 1 << 14, 0)
    for bit in range(6, -1, -1):
        step = 1 << bit
        up = size >= 2.0 ** (step - 64)
        code = code + jnp.where(up, step << 7, 0)
        size = jnp.where(up, size * 2.0**-step, size)
    return code + ((size * 2.0**64 - 1.0) * 128.0).astype(jnp.int32)


def attend_kernel(
    lengths_any,
    slots_any,
    q_any,
    nk_any,
    nv_any,
    k_any,
    v_any,
    codes_any,
    out_ref,
    q_ref,
    nk_ref,
    nv_ref,
    k_ref,
    v_ref,
    codes_ref,
    msg,
    by_head,
    spread,
    lengths,
    slots,
    sems,
    *,
    tiles,
    per,
    feature_rows,
):
    rows, width = q_ref.shape
    small = [
        pltpu.make_async_copy(source, target, sems.at[at])
        for at, (source, target) in enumerate(
            (
                (q_any, q_ref),
                (nk_any, nk_ref),
                (nv_any, nv_ref),
                (codes_any, codes_ref),
                (lengths_any, lengths),
                (slots_any, slots),
            )
        )
    ]
    cached = k_any.shape[1]
    keys, values = (
        [
            pltpu.make_async_copy(
                source.at[r], target.at[pl.ds(r * cached, cached)], sems.at[base + r]
            )
            for r in range(rows)
        ]
        for source, target, base in ((k_any, k_ref, 6), (v_any, v_ref, 6 + rows))
    )
    for copy in small + keys + values:
        copy.start()

    heads = width // HEAD_DIM
    factor = 1.0 / math.sqrt(HEAD_DIM)
    msg[...] = jnp.zeros_like(msg)
    for copy in small:
        copy.wait()

    queries = q_ref[...].astype(jnp.float32)
    by_head[...] = jnp.zeros_like(by_head)
    for r in range(rows):
        for head in range(heads):
            by_head[r * heads + head : r * heads + head + 1, :] = queries[
                r : r + 1, head * LANES : (head + 1) * LANES
            ]
    turned = by_head[...].T
    column = lax.broadcasted_iota(jnp.int32, (1, LANES), 1)
    for head in range(heads):
        spread[head * LANES : (head + 1) * LANES, :] = jnp.where(
            column % heads == head, turned, 0.0
        ).astype(jnp.bfloat16)
    padding = jnp.zeros((16 - rows, width), jnp.float32)
    known = rows * cached
    k_ref[known:, :] = jnp.concatenate([nk_ref[...].astype(jnp.float32), padding], 0).astype(
        jnp.bfloat16
    )
    v_ref[known:, :] = jnp.concatenate([nv_ref[...].astype(jnp.float32), padding], 0).astype(
        jnp.bfloat16
    )
    for copy in keys:
        copy.wait()
    products = jnp.dot(k_ref[...], spread[...], preferred_element_type=jnp.float32) * factor
    words = codes_ref[...]
    blocks = words.shape[1] // LANES
    pieces = [encode(words & 32767), encode(words >> 15)]
    for slot in range(tiles // IMG_SPLIT):
        gains = [
            jnp.where(slots[r] == slot, 1.0, 0.0).astype(jnp.float32) for r in range(rows)
        ]
        for at, piece in enumerate(pieces):
            total = piece[0:1] * gains[0]
            for r in range(1, rows):
                total = total + piece[r : r + 1] * gains[r]
            for tile in range(tiles):
                number = (member(tile, tiles) + IMG_SPLIT // 2) % tiles
                if number // IMG_SPLIT != slot:
                    continue
                for step in range(WINDOW):
                    block = window_start(number % IMG_SPLIT) + step
                    if block < 0 or block >= blocks:
                        continue
                    place = feature_rows + at * WINDOW + step
                    msg[tile, place : place + 1, :] = total[:, block * LANES : (block + 1) * LANES]

    own_scores = products[known:]
    scores = products[:known]
    owner = column // heads
    own_at = lax.broadcasted_iota(jnp.int32, own_scores.shape, 0) == owner
    own_score = jnp.sum(jnp.where(own_at, own_scores, 0.0), 0, keepdims=True)
    limit = jnp.zeros(column.shape, jnp.int32)
    for r in range(rows):
        limit = jnp.where(owner == r, lengths[r], limit)
    position = lax.broadcasted_iota(jnp.int32, scores.shape, 0) - owner * cached
    live = (position >= 0) & (position < limit)
    scores = jnp.where(live, scores, jnp.float32(-1e30))
    highest = jnp.maximum(jnp.max(scores, 0, keepdims=True), own_score)
    cache_exp = jnp.where(live, jnp.exp(scores - highest), 0.0)
    own_exp = jnp.exp(own_score - highest)
    denom = jnp.sum(cache_exp, 0, keepdims=True) + own_exp
    cache_weight = (cache_exp / denom).T[: rows * heads]
    own_weight = jnp.where(own_at, own_exp / denom, 0.0)
    own_weight = jnp.concatenate(
        [own_weight, jnp.zeros((LANES - own_weight.shape[0], LANES), jnp.float32)], 0
    ).T[: rows * heads, :16]
    weight = jnp.concatenate([cache_weight, own_weight], 1).astype(jnp.bfloat16)
    for copy in values:
        copy.wait()
    attended = jnp.dot(weight, v_ref[...], preferred_element_type=jnp.float32)
    for tile in range(tiles):
        for r in range(rows):
            for step in range(per):
                head = member(tile, tiles) // 2 * per + step
                place = r * per + step
                msg[tile, place : place + 1, :] = attended[
                    r * heads + head : r * heads + head + 1, head * LANES : (head + 1) * LANES
                ]
    out_ref[...] = msg[...].astype(jnp.bfloat16)


def project_kernel(in_ref, own_ref, other_ref, out_ref, held, total, *, rows, per):
    tiles, depth = in_ref.shape[:2]
    held[...] = in_ref[...].astype(jnp.float32).reshape(held.shape)
    groups = total.shape[0]
    lines = out_ref.shape[2] // rows
    share = own_ref.shape[0]
    lhs = []
    for row in range(rows):
        parts = [held[pl.ds(row * per + j, tiles, stride=depth), :] for j in range(per)]
        lhs.append(jnp.concatenate(parts, 1))
    lhs = jnp.concatenate(lhs, 0)
    even = lax.axis_index("rows") % 2 == 0
    first, second = lhs[:, :share], lhs[:, share:]
    own = jnp.where(even, first, second).astype(jnp.bfloat16)
    other = jnp.where(even, second, first).astype(jnp.bfloat16)
    product = jnp.dot(own, own_ref[...], preferred_element_type=jnp.float32) + jnp.dot(
        other, other_ref[...], preferred_element_type=jnp.float32
    )
    for row in range(rows):
        for group in range(groups):
            for line in range(lines):
                begin = (group * lines + line) * LANES
                total[group, pl.ds(row * lines + line, tiles, stride=rows * lines), :] = product[
                    row * tiles : (row + 1) * tiles, begin : begin + LANES
                ]
    for group in range(groups):
        out_ref[:, group] = (
            total[group].astype(jnp.bfloat16).reshape(tiles, rows * lines, LANES)
        )


def total_kernel(in_ref, out_ref, held, *, rows):
    tiles, groups, depth, _ = in_ref.shape
    lines = depth // rows
    parts = in_ref[...].astype(jnp.float32).reshape(tiles // 2, 2 * groups, depth, LANES)
    held[...] = jnp.sum(parts, 0)
    for group in range(2 * groups):
        for line in range(lines):
            begin = (group * lines + line) * LANES
            out_ref[:, begin : begin + LANES] = held[
                group, pl.ds(line, rows, stride=lines), :
            ].astype(jnp.bfloat16)


def split_three(whole):
    high = whole.astype(jnp.bfloat16).astype(jnp.float32)
    middle = (whole - high).astype(jnp.bfloat16).astype(jnp.float32)
    return jnp.concatenate([high, middle, whole - high - middle], 0)


def fold_kernel(
    cw_ref,
    conv_ref,
    weight_ref,
    other_ref,
    after_ref,
    out_ref,
    near_ref,
    near_other_ref,
    levels_w,
    folded,
    held,
    sems,
    near_sems,
):
    del after_ref
    taps = [(dr, dc) for dr in range(3) for dc in range(3)]
    copies = [
        pltpu.make_async_copy(conv_ref.at[dr, dc], held.at[at], sems.at[at])
        for at, (dr, dc) in enumerate(taps)
    ]
    for copy in copies:
        copy.start()
    begin = pl.multiple_of(lax.axis_index("rows") % 2 * near_ref.shape[1], LANES)
    columns = pl.ds(begin, near_ref.shape[1])
    brings = [
        pltpu.make_async_copy(source.at[:, columns], target, near_sems.at[at])
        for at, (source, target) in enumerate(((weight_ref, near_ref), (other_ref, near_other_ref)))
    ]
    for bring in brings:
        bring.start()
    levels_w[...] = jnp.zeros_like(levels_w)
    levels_w[0:FSQ_DIMS, :] = cw_ref[...]
    left = split_three(levels_w[...]).astype(jnp.bfloat16)
    folded[...] = jnp.zeros_like(folded)
    for at, copy in enumerate(copies):
        copy.wait()
        parts = jnp.dot(left, held[at], preferred_element_type=jnp.float32)
        total = parts[0:8] + parts[8:16] + parts[16:24]
        folded[at * TAP_ROWS : (at + 1) * TAP_ROWS, :] = split_three(total)
    out_ref[...] = folded[...].astype(jnp.bfloat16)
    for bring in brings:
        bring.wait()


def decode_kernel(
    in_ref, fold_ref, two_any, after_ref, out_ref, two_ref, sems, *, feature_rows
):
    del after_ref
    copies = [
        pltpu.make_async_copy(two_any.at[dr, dc], two_ref.at[at], sems.at[at])
        for at, (dr, dc) in enumerate(TAPS)
    ]
    for copy in copies[:EARLY]:
        copy.start()
    tiles = lax.axis_size("rows")
    section = (lax.axis_index("rows") + IMG_SPLIT // 2) % tiles % IMG_SPLIT
    got = jnp.sum(in_ref[...].astype(jnp.float32), 0)
    pieces = []
    for at in range(PIECES):
        lines = [
            got[feature_rows + at * WINDOW + step : feature_rows + at * WINDOW + step + 1]
            for step in range(WINDOW)
        ]
        pieces.append(jnp.concatenate(lines, 1))
    codes = decode_number(jnp.concatenate(pieces, 1))
    span = codes.shape[1]
    depth = fold_ref.shape[0]
    level = lax.broadcasted_iota(jnp.int32, (8, span), 0)
    taken = level < FSQ_DIMS
    shift = jnp.where(taken, level * 3, 0)
    value = (2 * ((jnp.broadcast_to(codes, (8, span)) >> shift) & 7) - 7).astype(
        jnp.float32
    ) * 0.125
    value = jnp.where(taken, value, 0.0)
    value = jnp.concatenate([value] * (depth // 8), 0).astype(jnp.bfloat16)

    count = TILE_ROWS * IMG_W
    begin = TILE_H * ROW_WORDS * section - HALO * ROW_WORDS
    offset = begin & (LANES - 1)
    spot = lax.broadcasted_iota(jnp.int32, (count, 1), 0)
    line = spot // IMG_W + TILE_H * section - HALO
    inside = (line >= 0) & (line < IMG_SPLIT * TILE_H)
    target = jnp.where(inside, (spot >> 1) + offset + (span // 2) * (spot & 1), -1)
    chooser = jnp.where(
        lax.broadcasted_iota(jnp.int32, (count, span), 1) == target, 1.0, 0.0
    ).astype(jnp.bfloat16)
    placed = lax.dot_general(
        chooser, value, (((1,), (1,)), ((), ())), preferred_element_type=jnp.float32
    )
    for copy in copies[EARLY:]:
        copy.start()
    column = spot % IMG_W
    moved = [
        jnp.where(column == 0, 0.0, pltpu.roll(placed, 1, 0)),
        placed,
        jnp.where(column == IMG_W - 1, 0.0, pltpu.roll(placed, count - 1, 0)),
    ]
    count = count - 2 * IMG_W
    tap_of = lax.broadcasted_iota(jnp.int32, (1, depth), 1) // TAP_ROWS
    taps = jnp.zeros((count, depth), jnp.float32)
    for dr in range(3):
        for dc in range(3):
            taps = jnp.where(
                tap_of == 3 * dr + dc, moved[dc][dr * IMG_W : dr * IMG_W + count], taps
            )
    hidden = jnp.dot(taps.astype(jnp.bfloat16), fold_ref[...], preferred_element_type=jnp.float32)

    line = lax.broadcasted_iota(jnp.int32, (count, 1), 0) // IMG_W + TILE_H * section - 1
    inside = (line >= 0) & (line < IMG_SPLIT * TILE_H)
    activated = jnp.where(inside, hidden * jax.nn.sigmoid(hidden), 0.0).astype(jnp.bfloat16)

    count = count - 2 * IMG_W
    column = lax.broadcasted_iota(jnp.int32, (count, 1), 0) % IMG_W
    summed = part = None
    for at, (dr, dc) in enumerate(TAPS):
        if at == 0:
            for copy in copies[:EARLY]:
                copy.wait()
        if at == EARLY:
            for copy in copies[EARLY:]:
                copy.wait()
        term = jnp.dot(
            activated[dr * IMG_W : dr * IMG_W + count],
            two_ref[at],
            preferred_element_type=jnp.float32,
        )
        part = term if part is None else part + term
        if dr < 2:
            continue
        if dc == 0:
            part = jnp.where(column == 0, 0.0, pltpu.roll(part, 1, 0))
        if dc == 2:
            part = jnp.where(column == IMG_W - 1, 0.0, pltpu.roll(part, count - 1, 0))
        summed = part if summed is None else summed + part
        part = None
    out_ref[...] = summed.astype(jnp.bfloat16)


def near(array):
    return pltpu.with_memory_space_constraint(array, pltpu.VMEM)


def far(array):
    return pltpu.with_memory_space_constraint(array, pltpu.HBM)


def on_device(
    queries,
    new_keys,
    new_values,
    cache_keys,
    cache_values,
    cache_lengths,
    out_weight,
    codes,
    tile_slot,
    code_weight,
    conv_one,
    conv_two,
):
    tiles = lax.axis_size("rows")
    rows, width = queries.shape
    channels = code_weight.shape[1]
    share = width // tiles
    per = 2 * share // LANES
    feature_rows = rows * per
    depth = message_rows(feature_rows)
    half = width // 2
    lines = 8
    groups = half // (lines * LANES)
    params = pltpu.CompilerParams(vmem_limit_bytes=VMEM_LIMIT)
    vmem = pl.BlockSpec(memory_space=pltpu.VMEM)
    anywhere = pl.BlockSpec(memory_space=pl.ANY)

    outgoing = pl.pallas_call(
        functools.partial(attend_kernel, tiles=tiles, per=per, feature_rows=feature_rows),
        in_specs=[anywhere] * 8,
        out_specs=vmem,
        out_shape=jax.ShapeDtypeStruct((tiles, depth, LANES), jnp.bfloat16),
        scratch_shapes=[
            pltpu.VMEM(queries.shape, queries.dtype),
            pltpu.VMEM(new_keys.shape, new_keys.dtype),
            pltpu.VMEM(new_values.shape, new_values.dtype),
            pltpu.VMEM((rows * cache_keys.shape[1] + 16, width), cache_keys.dtype),
            pltpu.VMEM((rows * cache_values.shape[1] + 16, width), cache_values.dtype),
            pltpu.VMEM(codes.shape, codes.dtype),
            pltpu.VMEM((tiles, depth, LANES), jnp.float32),
            pltpu.VMEM((LANES, LANES), jnp.float32),
            pltpu.VMEM((width, LANES), jnp.bfloat16),
            pltpu.SMEM(cache_lengths.shape, cache_lengths.dtype),
            pltpu.SMEM(tile_slot.shape, tile_slot.dtype),
            pltpu.SemaphoreType.DMA((6 + 2 * rows,)),
        ],
        compiler_params=pltpu.CompilerParams(vmem_limit_bytes=56 * 1024 * 1024),
    )(
        far(cache_lengths),
        far(tile_slot),
        far(queries),
        far(new_keys),
        far(new_values),
        far(cache_keys),
        far(cache_values),
        far(codes),
    )
    order = [[member(at, tiles) for at in range(tiles)]]
    incoming = lax.all_to_all(
        outgoing, "rows", split_axis=0, concat_axis=0, axis_index_groups=order, tiled=True
    )
    other = lax.ppermute(out_weight, "rows", [(i, i ^ 1) for i in range(tiles)])

    folded, own, other = pl.pallas_call(
        fold_kernel,
        in_specs=[vmem] + [anywhere] * 4,
        out_specs=[vmem] * 3,
        out_shape=[
            jax.ShapeDtypeStruct((FOLD_ROWS, channels), jnp.bfloat16),
            pltpu.VMEM((share, half), out_weight.dtype),
            pltpu.VMEM((share, half), out_weight.dtype),
        ],
        scratch_shapes=[
            pltpu.VMEM((8, channels), jnp.float32),
            pltpu.VMEM((FOLD_ROWS, channels), jnp.float32),
            pltpu.VMEM((9,) + conv_one.shape[2:], conv_one.dtype),
            pltpu.SemaphoreType.DMA((9,)),
            pltpu.SemaphoreType.DMA((2,)),
        ],
        compiler_params=params,
    )(far(code_weight), far(conv_one), far(out_weight), far(other), far(outgoing))

    partials = pl.pallas_call(
        functools.partial(project_kernel, rows=rows, per=per),
        in_specs=[vmem, vmem, vmem],
        out_shape=pltpu.VMEM((tiles, groups, rows * lines, LANES), jnp.bfloat16),
        scratch_shapes=[
            pltpu.VMEM((tiles * depth, LANES), jnp.float32),
            pltpu.VMEM((groups, tiles * rows * lines, LANES), jnp.float32),
        ],
        compiler_params=params,
    )(near(incoming), near(own), near(other))
    gathered = lax.all_to_all(
        partials, "rows", split_axis=0, concat_axis=0, axis_index_groups=order, tiled=True
    )

    decoded = pl.pallas_call(
        functools.partial(decode_kernel, feature_rows=feature_rows),
        in_specs=[vmem, vmem, anywhere, anywhere],
        out_specs=vmem,
        out_shape=jax.ShapeDtypeStruct((TILE_H * IMG_W, channels), jnp.bfloat16),
        scratch_shapes=[
            pltpu.VMEM((len(TAPS),) + conv_two.shape[2:], conv_two.dtype),
            pltpu.SemaphoreType.DMA((len(TAPS),)),
        ],
        compiler_params=params,
    )(near(incoming), near(folded), far(conv_two), near(partials))

    mixed = pl.pallas_call(
        functools.partial(total_kernel, rows=rows),
        in_specs=[vmem],
        out_shape=jax.ShapeDtypeStruct((rows, width), jnp.bfloat16),
        scratch_shapes=[pltpu.VMEM((2 * groups, rows * lines, LANES), jnp.float32)],
        compiler_params=params,
    )(near(gathered))
    return (mixed, decoded.reshape(TILE_H, IMG_W, channels))


def solution(mesh):
    in_specs = (
        P(("groups", "rows"), None),
        P(("groups", "rows"), None),
        P(("groups", "rows"), None),
        P(("groups", "rows"), None, None),
        P(("groups", "rows"), None, None),
        P(("groups", "rows")),
        P("rows", None),
        P(("groups", "rows"), None),
        P(("groups", "rows")),
        P(),
        P(),
        P(),
    )
    out_specs = (P(("groups", "rows"), None), P(("groups", "rows"), None, None))
    return jax.shard_map(
        on_device, mesh=mesh, in_specs=in_specs, out_specs=out_specs, check_vma=False
    )
```

```python
import functools
import math

import jax
import jax.numpy as jnp
from jax import lax
from jax.experimental import pallas as pl
from jax.experimental.pallas import tpu as pltpu
from jax.sharding import PartitionSpec as P

HEAD_DIM = 128
FSQ_DIMS = 5
IMG_SPLIT = 4
TILE_H = 8
IMG_W = 48
LANES = 128
HALO = 2
ROW_WORDS = IMG_W // 2
TILE_ROWS = TILE_H + 2 * HALO
WINDOW = 3
PIECES = 2
CODE_ROWS = WINDOW * PIECES
TAP_ROWS = 24
FOLD_ROWS = 256
TAPS = [(dr, dc) for dc in (1, 0, 2) for dr in range(3)]
EARLY = 3
VMEM_LIMIT = 24 * 1024 * 1024


def window_start(section):
    return (TILE_H * ROW_WORDS * section - HALO * ROW_WORDS) // LANES


def member(at, tiles):
    return (at + tiles // 4 * 2) % tiles


def message_rows(features):
    return -(-(features + CODE_ROWS) // 16) * 16


def encode(code):
    fraction = (code & 127).astype(jnp.float32) * (1.0 / 128.0) + 1.0
    for bit in range(7):
        up = ((code >> (7 + bit)) & 1) == 1
        fraction = jnp.where(up, fraction * 2.0 ** (1 << bit), fraction)
        if bit == 5:
            fraction = fraction * 2.0**-64
    return jnp.where(((code >> 14) & 1) == 1, -fraction, fraction)


def decode_number(value):
    size = jnp.abs(value)
    code = jnp.where(value < 0.0, 1 << 14, 0)
    for bit in range(6, -1, -1):
        step = 1 << bit
        up = size >= 2.0 ** (step - 64)
        code = code + jnp.where(up, step << 7, 0)
        size = jnp.where(up, size * 2.0**-step, size)
    return code + ((size * 2.0**64 - 1.0) * 128.0).astype(jnp.int32)


def attend_kernel(
    lengths_any,
    slots_any,
    q_any,
    nk_any,
    nv_any,
    k_any,
    v_any,
    codes_any,
    out_ref,
    q_ref,
    nk_ref,
    nv_ref,
    k_ref,
    v_ref,
    codes_ref,
    msg,
    by_head,
    spread,
    lengths,
    slots,
    sems,
    *,
    tiles,
    per,
    feature_rows,
):
    rows, width = q_ref.shape
    small = [
        pltpu.make_async_copy(source, target, sems.at[at])
        for at, (source, target) in enumerate(
            (
                (q_any, q_ref),
                (nk_any, nk_ref),
                (nv_any, nv_ref),
                (codes_any, codes_ref),
                (lengths_any, lengths),
                (slots_any, slots),
            )
        )
    ]
    cached = k_any.shape[1]
    keys, values = (
        [
            pltpu.make_async_copy(
                source.at[r], target.at[pl.ds(r * cached, cached)], sems.at[base + r]
            )
            for r in range(rows)
        ]
        for source, target, base in ((k_any, k_ref, 6), (v_any, v_ref, 6 + rows))
    )
    for copy in small + keys + values:
        copy.start()

    heads = width // HEAD_DIM
    factor = 1.0 / math.sqrt(HEAD_DIM)
    msg[...] = jnp.zeros_like(msg)
    for copy in small:
        copy.wait()

    queries = q_ref[...].astype(jnp.float32)
    by_head[...] = jnp.zeros_like(by_head)
    for r in range(rows):
        for head in range(heads):
            by_head[r * heads + head : r * heads + head + 1, :] = queries[
                r : r + 1, head * LANES : (head + 1) * LANES
            ]
    turned = by_head[...].T
    column = lax.broadcasted_iota(jnp.int32, (1, LANES), 1)
    for head in range(heads):
        spread[head * LANES : (head + 1) * LANES, :] = jnp.where(
            column % heads == head, turned, 0.0
        ).astype(jnp.bfloat16)
    padding = jnp.zeros((16 - rows, width), jnp.float32)
    known = rows * cached
    k_ref[known:, :] = jnp.concatenate([nk_ref[...].astype(jnp.float32), padding], 0).astype(
        jnp.bfloat16
    )
    v_ref[known:, :] = jnp.concatenate([nv_ref[...].astype(jnp.float32), padding], 0).astype(
        jnp.bfloat16
    )
    for copy in keys:
        copy.wait()
    products = jnp.dot(k_ref[...], spread[...], preferred_element_type=jnp.float32) * factor
    words = codes_ref[...]
    blocks = words.shape[1] // LANES
    pieces = [encode(words & 32767), encode(words >> 15)]
    for slot in range(tiles // IMG_SPLIT):
        gains = [
            jnp.where(slots[r] == slot, 1.0, 0.0).astype(jnp.float32) for r in range(rows)
        ]
        for at, piece in enumerate(pieces):
            total = piece[0:1] * gains[0]
            for r in range(1, rows):
                total = total + piece[r : r + 1] * gains[r]
            for tile in range(tiles):
                number = (member(tile, tiles) + IMG_SPLIT // 2) % tiles
                if number // IMG_SPLIT != slot:
                    continue
                for step in range(WINDOW):
                    block = window_start(number % IMG_SPLIT) + step
                    if block < 0 or block >= blocks:
                        continue
                    place = feature_rows + at * WINDOW + step
                    msg[tile, place : place + 1, :] = total[:, block * LANES : (block + 1) * LANES]

    own_scores = products[known:]
    scores = products[:known]
    owner = column // heads
    own_at = lax.broadcasted_iota(jnp.int32, own_scores.shape, 0) == owner
    own_score = jnp.sum(jnp.where(own_at, own_scores, 0.0), 0, keepdims=True)
    limit = jnp.zeros(column.shape, jnp.int32)
    for r in range(rows):
        limit = jnp.where(owner == r, lengths[r], limit)
    position = lax.broadcasted_iota(jnp.int32, scores.shape, 0) - owner * cached
    live = (position >= 0) & (position < limit)
    scores = jnp.where(live, scores, jnp.float32(-1e30))
    highest = jnp.maximum(jnp.max(scores, 0, keepdims=True), own_score)
    cache_exp = jnp.where(live, jnp.exp(scores - highest), 0.0)
    own_exp = jnp.exp(own_score - highest)
    denom = jnp.sum(cache_exp, 0, keepdims=True) + own_exp
    cache_weight = (cache_exp / denom).T[: rows * heads]
    own_weight = jnp.where(own_at, own_exp / denom, 0.0)
    own_weight = jnp.concatenate(
        [own_weight, jnp.zeros((LANES - own_weight.shape[0], LANES), jnp.float32)], 0
    ).T[: rows * heads, :16]
    weight = jnp.concatenate([cache_weight, own_weight], 1).astype(jnp.bfloat16)
    for copy in values:
        copy.wait()
    attended = jnp.dot(weight, v_ref[...], preferred_element_type=jnp.float32)
    for tile in range(tiles):
        for r in range(rows):
            for step in range(per):
                head = member(tile, tiles) // 2 * per + step
                place = r * per + step
                msg[tile, place : place + 1, :] = attended[
                    r * heads + head : r * heads + head + 1, head * LANES : (head + 1) * LANES
                ]
    out_ref[...] = msg[...].astype(jnp.bfloat16)


def project_kernel(in_ref, own_ref, other_ref, out_any, held, total, out_ref, sems, *, rows, per):
    tiles, depth = in_ref.shape[:2]
    held[...] = in_ref[...].astype(jnp.float32).reshape(held.shape)
    groups = total.shape[0]
    lines = out_any.shape[2] // rows
    share = own_ref.shape[0]
    lhs = []
    for row in range(rows):
        parts = [held[pl.ds(row * per + j, tiles, stride=depth), :] for j in range(per)]
        lhs.append(jnp.concatenate(parts, 1))
    lhs = jnp.concatenate(lhs, 0)
    even = lax.axis_index("rows") % 2 == 0
    first, second = lhs[:, :share], lhs[:, share:]
    own = jnp.where(even, first, second).astype(jnp.bfloat16)
    other = jnp.where(even, second, first).astype(jnp.bfloat16)
    reach = lines * LANES
    copies = []
    for group in range(groups):
        columns = slice(group * reach, (group + 1) * reach)
        product = jnp.dot(own, own_ref[:, columns], preferred_element_type=jnp.float32) + jnp.dot(
            other, other_ref[:, columns], preferred_element_type=jnp.float32
        )
        for row in range(rows):
            for line in range(lines):
                total[group, pl.ds(row * lines + line, tiles, stride=rows * lines), :] = product[
                    row * tiles : (row + 1) * tiles, line * LANES : (line + 1) * LANES
                ]
        out_ref[group] = total[group].astype(jnp.bfloat16).reshape(tiles, rows * lines, LANES)
        copies.append(pltpu.make_async_copy(out_ref.at[group], out_any.at[:, group], sems.at[group]))
        copies[-1].start()
    for copy in copies:
        copy.wait()


def total_kernel(in_ref, out_ref, held, *, rows):
    tiles, groups, depth, _ = in_ref.shape
    lines = depth // rows
    parts = in_ref[...].astype(jnp.float32).reshape(tiles // 2, 2 * groups, depth, LANES)
    held[...] = jnp.sum(parts, 0)
    for group in range(2 * groups):
        for line in range(lines):
            begin = (group * lines + line) * LANES
            out_ref[:, begin : begin + LANES] = held[
                group, pl.ds(line, rows, stride=lines), :
            ].astype(jnp.bfloat16)


def split_three(whole):
    high = whole.astype(jnp.bfloat16).astype(jnp.float32)
    middle = (whole - high).astype(jnp.bfloat16).astype(jnp.float32)
    return jnp.concatenate([high, middle, whole - high - middle], 0)


def fold_kernel(
    cw_ref,
    conv_ref,
    weight_ref,
    other_ref,
    after_ref,
    out_ref,
    near_ref,
    near_other_ref,
    levels_w,
    folded,
    held,
    sems,
    near_sems,
):
    del after_ref
    taps = [(dr, dc) for dr in range(3) for dc in range(3)]
    copies = [
        pltpu.make_async_copy(conv_ref.at[dr, dc], held.at[at], sems.at[at])
        for at, (dr, dc) in enumerate(taps)
    ]
    for copy in copies:
        copy.start()
    begin = pl.multiple_of(lax.axis_index("rows") % 2 * near_ref.shape[1], LANES)
    columns = pl.ds(begin, near_ref.shape[1])
    brings = [
        pltpu.make_async_copy(source.at[:, columns], target, near_sems.at[at])
        for at, (source, target) in enumerate(((weight_ref, near_ref), (other_ref, near_other_ref)))
    ]
    for bring in brings:
        bring.start()
    levels_w[...] = jnp.zeros_like(levels_w)
    levels_w[0:FSQ_DIMS, :] = cw_ref[...]
    left = split_three(levels_w[...]).astype(jnp.bfloat16)
    folded[...] = jnp.zeros_like(folded)
    for at, copy in enumerate(copies):
        copy.wait()
        parts = jnp.dot(left, held[at], preferred_element_type=jnp.float32)
        total = parts[0:8] + parts[8:16] + parts[16:24]
        folded[at * TAP_ROWS : (at + 1) * TAP_ROWS, :] = split_three(total)
    out_ref[...] = folded[...].astype(jnp.bfloat16)
    for bring in brings:
        bring.wait()


def decode_kernel(
    in_ref, fold_ref, two_any, after_ref, out_ref, two_ref, sems, *, feature_rows
):
    del after_ref
    copies = [
        pltpu.make_async_copy(two_any.at[dr, dc], two_ref.at[at], sems.at[at])
        for at, (dr, dc) in enumerate(TAPS)
    ]
    for copy in copies[:EARLY]:
        copy.start()
    tiles = lax.axis_size("rows")
    section = (lax.axis_index("rows") + IMG_SPLIT // 2) % tiles % IMG_SPLIT
    got = jnp.sum(in_ref[...].astype(jnp.float32), 0)
    pieces = []
    for at in range(PIECES):
        lines = [
            got[feature_rows + at * WINDOW + step : feature_rows + at * WINDOW + step + 1]
            for step in range(WINDOW)
        ]
        pieces.append(jnp.concatenate(lines, 1))
    codes = decode_number(jnp.concatenate(pieces, 1))
    span = codes.shape[1]
    depth = fold_ref.shape[0]
    level = lax.broadcasted_iota(jnp.int32, (8, span), 0)
    taken = level < FSQ_DIMS
    shift = jnp.where(taken, level * 3, 0)
    value = (2 * ((jnp.broadcast_to(codes, (8, span)) >> shift) & 7) - 7).astype(
        jnp.float32
    ) * 0.125
    value = jnp.where(taken, value, 0.0)
    value = jnp.concatenate([value] * (depth // 8), 0).astype(jnp.bfloat16)

    count = TILE_ROWS * IMG_W
    begin = TILE_H * ROW_WORDS * section - HALO * ROW_WORDS
    offset = begin & (LANES - 1)
    spot = lax.broadcasted_iota(jnp.int32, (count, 1), 0)
    line = spot // IMG_W + TILE_H * section - HALO
    inside = (line >= 0) & (line < IMG_SPLIT * TILE_H)
    target = jnp.where(inside, (spot >> 1) + offset + (span // 2) * (spot & 1), -1)
    chooser = jnp.where(
        lax.broadcasted_iota(jnp.int32, (count, span), 1) == target, 1.0, 0.0
    ).astype(jnp.bfloat16)
    placed = lax.dot_general(
        chooser, value, (((1,), (1,)), ((), ())), preferred_element_type=jnp.float32
    )
    for copy in copies[EARLY:]:
        copy.start()
    column = spot % IMG_W
    moved = [
        jnp.where(column == 0, 0.0, pltpu.roll(placed, 1, 0)),
        placed,
        jnp.where(column == IMG_W - 1, 0.0, pltpu.roll(placed, count - 1, 0)),
    ]
    count = count - 2 * IMG_W
    tap_of = lax.broadcasted_iota(jnp.int32, (1, depth), 1) // TAP_ROWS
    taps = jnp.zeros((count, depth), jnp.float32)
    for dr in range(3):
        for dc in range(3):
            taps = jnp.where(
                tap_of == 3 * dr + dc, moved[dc][dr * IMG_W : dr * IMG_W + count], taps
            )
    hidden = jnp.dot(taps.astype(jnp.bfloat16), fold_ref[...], preferred_element_type=jnp.float32)

    line = lax.broadcasted_iota(jnp.int32, (count, 1), 0) // IMG_W + TILE_H * section - 1
    inside = (line >= 0) & (line < IMG_SPLIT * TILE_H)
    activated = jnp.where(inside, hidden * jax.nn.sigmoid(hidden), 0.0).astype(jnp.bfloat16)

    count = count - 2 * IMG_W
    column = lax.broadcasted_iota(jnp.int32, (count, 1), 0) % IMG_W
    summed = part = None
    for at, (dr, dc) in enumerate(TAPS):
        if at == 0:
            for copy in copies[:EARLY]:
                copy.wait()
        if at == EARLY:
            for copy in copies[EARLY:]:
                copy.wait()
        term = jnp.dot(
            activated[dr * IMG_W : dr * IMG_W + count],
            two_ref[at],
            preferred_element_type=jnp.float32,
        )
        part = term if part is None else part + term
        if dr < 2:
            continue
        if dc == 0:
            part = jnp.where(column == 0, 0.0, pltpu.roll(part, 1, 0))
        if dc == 2:
            part = jnp.where(column == IMG_W - 1, 0.0, pltpu.roll(part, count - 1, 0))
        summed = part if summed is None else summed + part
        part = None
    out_ref[...] = summed.astype(jnp.bfloat16)


def near(array):
    return pltpu.with_memory_space_constraint(array, pltpu.VMEM)


def far(array):
    return pltpu.with_memory_space_constraint(array, pltpu.HBM)


def on_device(
    queries,
    new_keys,
    new_values,
    cache_keys,
    cache_values,
    cache_lengths,
    out_weight,
    codes,
    tile_slot,
    code_weight,
    conv_one,
    conv_two,
):
    tiles = lax.axis_size("rows")
    rows, width = queries.shape
    channels = code_weight.shape[1]
    share = width // tiles
    per = 2 * share // LANES
    feature_rows = rows * per
    depth = message_rows(feature_rows)
    half = width // 2
    lines = 8
    groups = half // (lines * LANES)
    params = pltpu.CompilerParams(vmem_limit_bytes=VMEM_LIMIT)
    vmem = pl.BlockSpec(memory_space=pltpu.VMEM)
    anywhere = pl.BlockSpec(memory_space=pl.ANY)

    outgoing = pl.pallas_call(
        functools.partial(attend_kernel, tiles=tiles, per=per, feature_rows=feature_rows),
        in_specs=[anywhere] * 8,
        out_specs=vmem,
        out_shape=jax.ShapeDtypeStruct((tiles, depth, LANES), jnp.bfloat16),
        scratch_shapes=[
            pltpu.VMEM(queries.shape, queries.dtype),
            pltpu.VMEM(new_keys.shape, new_keys.dtype),
            pltpu.VMEM(new_values.shape, new_values.dtype),
            pltpu.VMEM((rows * cache_keys.shape[1] + 16, width), cache_keys.dtype),
            pltpu.VMEM((rows * cache_values.shape[1] + 16, width), cache_values.dtype),
            pltpu.VMEM(codes.shape, codes.dtype),
            pltpu.VMEM((tiles, depth, LANES), jnp.float32),
            pltpu.VMEM((LANES, LANES), jnp.float32),
            pltpu.VMEM((width, LANES), jnp.bfloat16),
            pltpu.SMEM(cache_lengths.shape, cache_lengths.dtype),
            pltpu.SMEM(tile_slot.shape, tile_slot.dtype),
            pltpu.SemaphoreType.DMA((6 + 2 * rows,)),
        ],
        compiler_params=pltpu.CompilerParams(vmem_limit_bytes=56 * 1024 * 1024),
    )(
        far(cache_lengths),
        far(tile_slot),
        far(queries),
        far(new_keys),
        far(new_values),
        far(cache_keys),
        far(cache_values),
        far(codes),
    )
    order = [[member(at, tiles) for at in range(tiles)]]
    incoming = lax.all_to_all(
        outgoing, "rows", split_axis=0, concat_axis=0, axis_index_groups=order, tiled=True
    )
    other = lax.ppermute(out_weight, "rows", [(i, i ^ 1) for i in range(tiles)])

    folded, own, other = pl.pallas_call(
        fold_kernel,
        in_specs=[vmem] + [anywhere] * 4,
        out_specs=[vmem] * 3,
        out_shape=[
            jax.ShapeDtypeStruct((FOLD_ROWS, channels), jnp.bfloat16),
            pltpu.VMEM((share, half), out_weight.dtype),
            pltpu.VMEM((share, half), out_weight.dtype),
        ],
        scratch_shapes=[
            pltpu.VMEM((8, channels), jnp.float32),
            pltpu.VMEM((FOLD_ROWS, channels), jnp.float32),
            pltpu.VMEM((9,) + conv_one.shape[2:], conv_one.dtype),
            pltpu.SemaphoreType.DMA((9,)),
            pltpu.SemaphoreType.DMA((2,)),
        ],
        compiler_params=params,
    )(far(code_weight), far(conv_one), far(out_weight), far(other), far(outgoing))

    partials = pl.pallas_call(
        functools.partial(project_kernel, rows=rows, per=per),
        in_specs=[vmem, vmem, vmem],
        out_specs=anywhere,
        out_shape=jax.ShapeDtypeStruct((tiles, groups, rows * lines, LANES), jnp.bfloat16),
        scratch_shapes=[
            pltpu.VMEM((tiles * depth, LANES), jnp.float32),
            pltpu.VMEM((groups, tiles * rows * lines, LANES), jnp.float32),
            pltpu.VMEM((groups, tiles, rows * lines, LANES), jnp.bfloat16),
            pltpu.SemaphoreType.DMA((groups,)),
        ],
        compiler_params=params,
    )(near(incoming), near(own), near(other))
    gathered = lax.all_to_all(
        partials, "rows", split_axis=0, concat_axis=0, axis_index_groups=order, tiled=True
    )

    decoded = pl.pallas_call(
        functools.partial(decode_kernel, feature_rows=feature_rows),
        in_specs=[vmem, vmem, anywhere, anywhere],
        out_specs=vmem,
        out_shape=jax.ShapeDtypeStruct((TILE_H * IMG_W, channels), jnp.bfloat16),
        scratch_shapes=[
            pltpu.VMEM((len(TAPS),) + conv_two.shape[2:], conv_two.dtype),
            pltpu.SemaphoreType.DMA((len(TAPS),)),
        ],
        compiler_params=params,
    )(near(incoming), near(folded), far(conv_two), far(partials))

    mixed = pl.pallas_call(
        functools.partial(total_kernel, rows=rows),
        in_specs=[vmem],
        out_shape=jax.ShapeDtypeStruct((rows, width), jnp.bfloat16),
        scratch_shapes=[pltpu.VMEM((2 * groups, rows * lines, LANES), jnp.float32)],
        compiler_params=params,
    )(near(gathered))
    return (mixed, decoded.reshape(TILE_H, IMG_W, channels))


def solution(mesh):
    in_specs = (
        P(("groups", "rows"), None),
        P(("groups", "rows"), None),
        P(("groups", "rows"), None),
        P(("groups", "rows"), None, None),
        P(("groups", "rows"), None, None),
        P(("groups", "rows")),
        P("rows", None),
        P(("groups", "rows"), None),
        P(("groups", "rows")),
        P(),
        P(),
        P(),
    )
    out_specs = (P(("groups", "rows"), None), P(("groups", "rows"), None, None))
    return jax.shard_map(
        on_device, mesh=mesh, in_specs=in_specs, out_specs=out_specs, check_vma=False
    )
```

```python
import functools
import math

import jax
import jax.numpy as jnp
from jax import lax
from jax.experimental import pallas as pl
from jax.experimental.pallas import tpu as pltpu
from jax.sharding import PartitionSpec as P

HEAD_DIM = 128
FSQ_DIMS = 5
IMG_SPLIT = 4
TILE_H = 8
IMG_W = 48
LANES = 128
HALO = 2
ROW_WORDS = IMG_W // 2
TILE_ROWS = TILE_H + 2 * HALO
WINDOW = 3
PIECES = 2
CODE_ROWS = WINDOW * PIECES
TAP_ROWS = 24
FOLD_ROWS = 256
TAPS = [(dr, dc) for dc in (1, 0, 2) for dr in range(3)]
EARLY = 3
VMEM_LIMIT = 24 * 1024 * 1024


def window_start(section):
    return (TILE_H * ROW_WORDS * section - HALO * ROW_WORDS) // LANES


def member(at, tiles):
    return (at + tiles // 4 * 2) % tiles


def message_rows(features):
    return -(-(features + CODE_ROWS) // 16) * 16


def encode(code):
    fraction = (code & 127).astype(jnp.float32) * (1.0 / 128.0) + 1.0
    for bit in range(7):
        up = ((code >> (7 + bit)) & 1) == 1
        fraction = jnp.where(up, fraction * 2.0 ** (1 << bit), fraction)
        if bit == 5:
            fraction = fraction * 2.0**-64
    return jnp.where(((code >> 14) & 1) == 1, -fraction, fraction)


def decode_number(value):
    size = jnp.abs(value)
    code = jnp.where(value < 0.0, 1 << 14, 0)
    for bit in range(6, -1, -1):
        step = 1 << bit
        up = size >= 2.0 ** (step - 64)
        code = code + jnp.where(up, step << 7, 0)
        size = jnp.where(up, size * 2.0**-step, size)
    return code + ((size * 2.0**64 - 1.0) * 128.0).astype(jnp.int32)


def attend_kernel(
    lengths_any,
    slots_any,
    q_any,
    nk_any,
    nv_any,
    k_any,
    v_any,
    codes_any,
    out_ref,
    q_ref,
    nk_ref,
    nv_ref,
    k_ref,
    v_ref,
    codes_ref,
    msg,
    by_head,
    spread,
    lengths,
    slots,
    sems,
    *,
    tiles,
    per,
    feature_rows,
):
    rows, width = q_ref.shape
    small = [
        pltpu.make_async_copy(source, target, sems.at[at])
        for at, (source, target) in enumerate(
            (
                (q_any, q_ref),
                (nk_any, nk_ref),
                (nv_any, nv_ref),
                (codes_any, codes_ref),
                (lengths_any, lengths),
                (slots_any, slots),
            )
        )
    ]
    cached = k_any.shape[1]
    keys, values = (
        [
            pltpu.make_async_copy(
                source.at[r], target.at[pl.ds(r * cached, cached)], sems.at[base + r]
            )
            for r in range(rows)
        ]
        for source, target, base in ((k_any, k_ref, 6), (v_any, v_ref, 6 + rows))
    )
    for copy in small + keys + values:
        copy.start()

    heads = width // HEAD_DIM
    factor = 1.0 / math.sqrt(HEAD_DIM)
    msg[...] = jnp.zeros_like(msg)
    for copy in small:
        copy.wait()

    queries = q_ref[...].astype(jnp.float32)
    by_head[...] = jnp.zeros_like(by_head)
    for r in range(rows):
        for head in range(heads):
            by_head[r * heads + head : r * heads + head + 1, :] = queries[
                r : r + 1, head * LANES : (head + 1) * LANES
            ]
    turned = by_head[...].T
    column = lax.broadcasted_iota(jnp.int32, (1, LANES), 1)
    for head in range(heads):
        spread[head * LANES : (head + 1) * LANES, :] = jnp.where(
            column % heads == head, turned, 0.0
        ).astype(jnp.bfloat16)
    padding = jnp.zeros((16 - rows, width), jnp.float32)
    known = rows * cached
    k_ref[known:, :] = jnp.concatenate([nk_ref[...].astype(jnp.float32), padding], 0).astype(
        jnp.bfloat16
    )
    v_ref[known:, :] = jnp.concatenate([nv_ref[...].astype(jnp.float32), padding], 0).astype(
        jnp.bfloat16
    )
    words = codes_ref[...]
    blocks = words.shape[1] // LANES
    pieces = [encode(words & 32767), encode(words >> 15)]
    for slot in range(tiles // IMG_SPLIT):
        gains = [
            jnp.where(slots[r] == slot, 1.0, 0.0).astype(jnp.float32) for r in range(rows)
        ]
        for at, piece in enumerate(pieces):
            total = piece[0:1] * gains[0]
            for r in range(1, rows):
                total = total + piece[r : r + 1] * gains[r]
            for tile in range(tiles):
                number = (member(tile, tiles) + IMG_SPLIT // 2) % tiles
                if number // IMG_SPLIT != slot:
                    continue
                for step in range(WINDOW):
                    block = window_start(number % IMG_SPLIT) + step
                    if block < 0 or block >= blocks:
                        continue
                    place = feature_rows + at * WINDOW + step
                    msg[tile, place : place + 1, :] = total[:, block * LANES : (block + 1) * LANES]

    for copy in keys:
        copy.wait()
    products = jnp.dot(k_ref[...], spread[...], preferred_element_type=jnp.float32) * factor
    own_scores = products[known:]
    scores = products[:known]
    owner = column // heads
    own_at = lax.broadcasted_iota(jnp.int32, own_scores.shape, 0) == owner
    own_score = jnp.sum(jnp.where(own_at, own_scores, 0.0), 0, keepdims=True)
    limit = jnp.zeros(column.shape, jnp.int32)
    for r in range(rows):
        limit = jnp.where(owner == r, lengths[r], limit)
    position = lax.broadcasted_iota(jnp.int32, scores.shape, 0) - owner * cached
    live = (position >= 0) & (position < limit)
    scores = jnp.where(live, scores, jnp.float32(-1e30))
    highest = jnp.maximum(jnp.max(scores, 0, keepdims=True), own_score)
    cache_exp = jnp.where(live, jnp.exp(scores - highest), 0.0)
    own_exp = jnp.exp(own_score - highest)
    denom = jnp.sum(cache_exp, 0, keepdims=True) + own_exp
    cache_weight = (cache_exp / denom).T[: rows * heads]
    own_weight = jnp.where(own_at, own_exp / denom, 0.0)
    own_weight = jnp.concatenate(
        [own_weight, jnp.zeros((LANES - own_weight.shape[0], LANES), jnp.float32)], 0
    ).T[: rows * heads, :16]
    weight = jnp.concatenate([cache_weight, own_weight], 1).astype(jnp.bfloat16)
    for copy in values:
        copy.wait()
    attended = jnp.dot(weight, v_ref[...], preferred_element_type=jnp.float32)
    for tile in range(tiles):
        for r in range(rows):
            for step in range(per):
                head = member(tile, tiles) // 2 * per + step
                place = r * per + step
                msg[tile, place : place + 1, :] = attended[
                    r * heads + head : r * heads + head + 1, head * LANES : (head + 1) * LANES
                ]
    out_ref[...] = msg[...].astype(jnp.bfloat16)


def project_kernel(in_ref, own_ref, other_ref, out_any, held, total, out_ref, sems, *, rows, per):
    tiles, depth = in_ref.shape[:2]
    held[...] = in_ref[...].astype(jnp.float32).reshape(held.shape)
    groups = total.shape[0]
    lines = out_any.shape[2] // rows
    share = own_ref.shape[0]
    lhs = []
    for row in range(rows):
        parts = [held[pl.ds(row * per + j, tiles, stride=depth), :] for j in range(per)]
        lhs.append(jnp.concatenate(parts, 1))
    lhs = jnp.concatenate(lhs, 0)
    even = lax.axis_index("rows") % 2 == 0
    first, second = lhs[:, :share], lhs[:, share:]
    own = jnp.where(even, first, second).astype(jnp.bfloat16)
    other = jnp.where(even, second, first).astype(jnp.bfloat16)
    reach = lines * LANES
    copies = []
    for group in range(groups):
        columns = slice(group * reach, (group + 1) * reach)
        product = jnp.dot(own, own_ref[:, columns], preferred_element_type=jnp.float32) + jnp.dot(
            other, other_ref[:, columns], preferred_element_type=jnp.float32
        )
        for row in range(rows):
            for line in range(lines):
                total[group, pl.ds(row * lines + line, tiles, stride=rows * lines), :] = product[
                    row * tiles : (row + 1) * tiles, line * LANES : (line + 1) * LANES
                ]
        out_ref[group] = total[group].astype(jnp.bfloat16).reshape(tiles, rows * lines, LANES)
        copies.append(pltpu.make_async_copy(out_ref.at[group], out_any.at[:, group], sems.at[group]))
        copies[-1].start()
    for copy in copies:
        copy.wait()


def total_kernel(in_ref, out_ref, held, *, rows):
    tiles, groups, depth, _ = in_ref.shape
    lines = depth // rows
    parts = in_ref[...].astype(jnp.float32).reshape(tiles // 2, 2 * groups, depth, LANES)
    held[...] = jnp.sum(parts, 0)
    for group in range(2 * groups):
        for line in range(lines):
            begin = (group * lines + line) * LANES
            out_ref[:, begin : begin + LANES] = held[
                group, pl.ds(line, rows, stride=lines), :
            ].astype(jnp.bfloat16)


def split_three(whole):
    high = whole.astype(jnp.bfloat16).astype(jnp.float32)
    middle = (whole - high).astype(jnp.bfloat16).astype(jnp.float32)
    return jnp.concatenate([high, middle, whole - high - middle], 0)


def fold_kernel(
    cw_ref,
    conv_ref,
    weight_ref,
    other_ref,
    after_ref,
    out_ref,
    near_ref,
    near_other_ref,
    levels_w,
    folded,
    held,
    sems,
    near_sems,
):
    del after_ref
    taps = [(dr, dc) for dr in range(3) for dc in range(3)]
    copies = [
        pltpu.make_async_copy(conv_ref.at[dr, dc], held.at[at], sems.at[at])
        for at, (dr, dc) in enumerate(taps)
    ]
    for copy in copies:
        copy.start()
    begin = pl.multiple_of(lax.axis_index("rows") % 2 * near_ref.shape[1], LANES)
    columns = pl.ds(begin, near_ref.shape[1])
    brings = [
        pltpu.make_async_copy(source.at[:, columns], target, near_sems.at[at])
        for at, (source, target) in enumerate(((weight_ref, near_ref), (other_ref, near_other_ref)))
    ]
    for bring in brings:
        bring.start()
    levels_w[...] = jnp.zeros_like(levels_w)
    levels_w[0:FSQ_DIMS, :] = cw_ref[...]
    left = split_three(levels_w[...]).astype(jnp.bfloat16)
    folded[...] = jnp.zeros_like(folded)
    for at, copy in enumerate(copies):
        copy.wait()
        parts = jnp.dot(left, held[at], preferred_element_type=jnp.float32)
        total = parts[0:8] + parts[8:16] + parts[16:24]
        folded[at * TAP_ROWS : (at + 1) * TAP_ROWS, :] = split_three(total)
    out_ref[...] = folded[...].astype(jnp.bfloat16)
    for bring in brings:
        bring.wait()


def decode_kernel(
    in_ref, fold_ref, two_any, after_ref, out_ref, two_ref, sems, *, feature_rows
):
    del after_ref
    copies = [
        pltpu.make_async_copy(two_any.at[dr, dc], two_ref.at[at], sems.at[at])
        for at, (dr, dc) in enumerate(TAPS)
    ]
    for copy in copies[:EARLY]:
        copy.start()
    tiles = lax.axis_size("rows")
    section = (lax.axis_index("rows") + IMG_SPLIT // 2) % tiles % IMG_SPLIT
    got = jnp.sum(in_ref[...].astype(jnp.float32), 0)
    pieces = []
    for at in range(PIECES):
        lines = [
            got[feature_rows + at * WINDOW + step : feature_rows + at * WINDOW + step + 1]
            for step in range(WINDOW)
        ]
        pieces.append(jnp.concatenate(lines, 1))
    codes = decode_number(jnp.concatenate(pieces, 1))
    span = codes.shape[1]
    depth = fold_ref.shape[0]
    level = lax.broadcasted_iota(jnp.int32, (8, span), 0)
    taken = level < FSQ_DIMS
    shift = jnp.where(taken, level * 3, 0)
    value = (2 * ((jnp.broadcast_to(codes, (8, span)) >> shift) & 7) - 7).astype(
        jnp.float32
    ) * 0.125
    value = jnp.where(taken, value, 0.0)
    value = jnp.concatenate([value] * (depth // 8), 0).astype(jnp.bfloat16)

    count = TILE_ROWS * IMG_W
    begin = TILE_H * ROW_WORDS * section - HALO * ROW_WORDS
    offset = begin & (LANES - 1)
    spot = lax.broadcasted_iota(jnp.int32, (count, 1), 0)
    line = spot // IMG_W + TILE_H * section - HALO
    inside = (line >= 0) & (line < IMG_SPLIT * TILE_H)
    target = jnp.where(inside, (spot >> 1) + offset + (span // 2) * (spot & 1), -1)
    chooser = jnp.where(
        lax.broadcasted_iota(jnp.int32, (count, span), 1) == target, 1.0, 0.0
    ).astype(jnp.bfloat16)
    placed = lax.dot_general(
        chooser, value, (((1,), (1,)), ((), ())), preferred_element_type=jnp.float32
    )
    for copy in copies[EARLY:]:
        copy.start()
    column = spot % IMG_W
    moved = [
        jnp.where(column == 0, 0.0, pltpu.roll(placed, 1, 0)),
        placed,
        jnp.where(column == IMG_W - 1, 0.0, pltpu.roll(placed, count - 1, 0)),
    ]
    count = count - 2 * IMG_W
    tap_of = lax.broadcasted_iota(jnp.int32, (1, depth), 1) // TAP_ROWS
    taps = jnp.zeros((count, depth), jnp.float32)
    for dr in range(3):
        for dc in range(3):
            taps = jnp.where(
                tap_of == 3 * dr + dc, moved[dc][dr * IMG_W : dr * IMG_W + count], taps
            )
    hidden = jnp.dot(taps.astype(jnp.bfloat16), fold_ref[...], preferred_element_type=jnp.float32)

    line = lax.broadcasted_iota(jnp.int32, (count, 1), 0) // IMG_W + TILE_H * section - 1
    inside = (line >= 0) & (line < IMG_SPLIT * TILE_H)
    activated = jnp.where(inside, hidden * jax.nn.sigmoid(hidden), 0.0).astype(jnp.bfloat16)

    count = count - 2 * IMG_W
    column = lax.broadcasted_iota(jnp.int32, (count, 1), 0) % IMG_W
    summed = part = None
    for at, (dr, dc) in enumerate(TAPS):
        if at == 0:
            for copy in copies[:EARLY]:
                copy.wait()
        if at == EARLY:
            for copy in copies[EARLY:]:
                copy.wait()
        term = jnp.dot(
            activated[dr * IMG_W : dr * IMG_W + count],
            two_ref[at],
            preferred_element_type=jnp.float32,
        )
        part = term if part is None else part + term
        if dr < 2:
            continue
        if dc == 0:
            part = jnp.where(column == 0, 0.0, pltpu.roll(part, 1, 0))
        if dc == 2:
            part = jnp.where(column == IMG_W - 1, 0.0, pltpu.roll(part, count - 1, 0))
        summed = part if summed is None else summed + part
        part = None
    out_ref[...] = summed.astype(jnp.bfloat16)


def near(array):
    return pltpu.with_memory_space_constraint(array, pltpu.VMEM)


def far(array):
    return pltpu.with_memory_space_constraint(array, pltpu.HBM)


def on_device(
    queries,
    new_keys,
    new_values,
    cache_keys,
    cache_values,
    cache_lengths,
    out_weight,
    codes,
    tile_slot,
    code_weight,
    conv_one,
    conv_two,
):
    tiles = lax.axis_size("rows")
    rows, width = queries.shape
    channels = code_weight.shape[1]
    share = width // tiles
    per = 2 * share // LANES
    feature_rows = rows * per
    depth = message_rows(feature_rows)
    half = width // 2
    lines = 8
    groups = half // (lines * LANES)
    params = pltpu.CompilerParams(vmem_limit_bytes=VMEM_LIMIT)
    vmem = pl.BlockSpec(memory_space=pltpu.VMEM)
    anywhere = pl.BlockSpec(memory_space=pl.ANY)

    outgoing = pl.pallas_call(
        functools.partial(attend_kernel, tiles=tiles, per=per, feature_rows=feature_rows),
        in_specs=[anywhere] * 8,
        out_specs=vmem,
        out_shape=jax.ShapeDtypeStruct((tiles, depth, LANES), jnp.bfloat16),
        scratch_shapes=[
            pltpu.VMEM(queries.shape, queries.dtype),
            pltpu.VMEM(new_keys.shape, new_keys.dtype),
            pltpu.VMEM(new_values.shape, new_values.dtype),
            pltpu.VMEM((rows * cache_keys.shape[1] + 16, width), cache_keys.dtype),
            pltpu.VMEM((rows * cache_values.shape[1] + 16, width), cache_values.dtype),
            pltpu.VMEM(codes.shape, codes.dtype),
            pltpu.VMEM((tiles, depth, LANES), jnp.float32),
            pltpu.VMEM((LANES, LANES), jnp.float32),
            pltpu.VMEM((width, LANES), jnp.bfloat16),
            pltpu.SMEM(cache_lengths.shape, cache_lengths.dtype),
            pltpu.SMEM(tile_slot.shape, tile_slot.dtype),
            pltpu.SemaphoreType.DMA((6 + 2 * rows,)),
        ],
        compiler_params=pltpu.CompilerParams(vmem_limit_bytes=56 * 1024 * 1024),
    )(
        far(cache_lengths),
        far(tile_slot),
        far(queries),
        far(new_keys),
        far(new_values),
        far(cache_keys),
        far(cache_values),
        far(codes),
    )
    order = [[member(at, tiles) for at in range(tiles)]]
    incoming = lax.all_to_all(
        outgoing, "rows", split_axis=0, concat_axis=0, axis_index_groups=order, tiled=True
    )
    other = lax.ppermute(out_weight, "rows", [(i, i ^ 1) for i in range(tiles)])

    folded, own, other = pl.pallas_call(
        fold_kernel,
        in_specs=[vmem] + [anywhere] * 4,
        out_specs=[vmem] * 3,
        out_shape=[
            jax.ShapeDtypeStruct((FOLD_ROWS, channels), jnp.bfloat16),
            pltpu.VMEM((share, half), out_weight.dtype),
            pltpu.VMEM((share, half), out_weight.dtype),
        ],
        scratch_shapes=[
            pltpu.VMEM((8, channels), jnp.float32),
            pltpu.VMEM((FOLD_ROWS, channels), jnp.float32),
            pltpu.VMEM((9,) + conv_one.shape[2:], conv_one.dtype),
            pltpu.SemaphoreType.DMA((9,)),
            pltpu.SemaphoreType.DMA((2,)),
        ],
        compiler_params=params,
    )(far(code_weight), far(conv_one), far(out_weight), far(other), far(outgoing))

    partials = pl.pallas_call(
        functools.partial(project_kernel, rows=rows, per=per),
        in_specs=[vmem, vmem, vmem],
        out_specs=anywhere,
        out_shape=jax.ShapeDtypeStruct((tiles, groups, rows * lines, LANES), jnp.bfloat16),
        scratch_shapes=[
            pltpu.VMEM((tiles * depth, LANES), jnp.float32),
            pltpu.VMEM((groups, tiles * rows * lines, LANES), jnp.float32),
            pltpu.VMEM((groups, tiles, rows * lines, LANES), jnp.bfloat16),
            pltpu.SemaphoreType.DMA((groups,)),
        ],
        compiler_params=params,
    )(near(incoming), near(own), near(other))
    gathered = lax.all_to_all(
        partials, "rows", split_axis=0, concat_axis=0, axis_index_groups=order, tiled=True
    )

    decoded = pl.pallas_call(
        functools.partial(decode_kernel, feature_rows=feature_rows),
        in_specs=[vmem, vmem, anywhere, anywhere],
        out_specs=vmem,
        out_shape=jax.ShapeDtypeStruct((TILE_H * IMG_W, channels), jnp.bfloat16),
        scratch_shapes=[
            pltpu.VMEM((len(TAPS),) + conv_two.shape[2:], conv_two.dtype),
            pltpu.SemaphoreType.DMA((len(TAPS),)),
        ],
        compiler_params=params,
    )(near(incoming), near(folded), far(conv_two), far(partials))

    mixed = pl.pallas_call(
        functools.partial(total_kernel, rows=rows),
        in_specs=[vmem],
        out_shape=jax.ShapeDtypeStruct((rows, width), jnp.bfloat16),
        scratch_shapes=[pltpu.VMEM((2 * groups, rows * lines, LANES), jnp.float32)],
        compiler_params=params,
    )(near(gathered))
    return (mixed, decoded.reshape(TILE_H, IMG_W, channels))


def solution(mesh):
    in_specs = (
        P(("groups", "rows"), None),
        P(("groups", "rows"), None),
        P(("groups", "rows"), None),
        P(("groups", "rows"), None, None),
        P(("groups", "rows"), None, None),
        P(("groups", "rows")),
        P("rows", None),
        P(("groups", "rows"), None),
        P(("groups", "rows")),
        P(),
        P(),
        P(),
    )
    out_specs = (P(("groups", "rows"), None), P(("groups", "rows"), None, None))
    return jax.shard_map(
        on_device, mesh=mesh, in_specs=in_specs, out_specs=out_specs, check_vma=False
    )
```

```python
import functools
import math

import jax
import jax.numpy as jnp
from jax import lax
from jax.experimental import pallas as pl
from jax.experimental.pallas import tpu as pltpu
from jax.sharding import PartitionSpec as P

HEAD_DIM = 128
FSQ_DIMS = 5
IMG_SPLIT = 4
TILE_H = 8
IMG_W = 48
LANES = 128
HALO = 2
ROW_WORDS = IMG_W // 2
TILE_ROWS = TILE_H + 2 * HALO
WINDOW = 3
PIECES = 2
CODE_ROWS = WINDOW * PIECES
TAP_ROWS = 24
FOLD_ROWS = 256
TAPS = [(dr, dc) for dc in (1, 0, 2) for dr in range(3)]
EARLY = 3
VMEM_LIMIT = 24 * 1024 * 1024


def window_start(section):
    return (TILE_H * ROW_WORDS * section - HALO * ROW_WORDS) // LANES


def member(at, tiles):
    return (at + tiles // 4 * 2 + 2) % tiles


def message_rows(features):
    return -(-(features + CODE_ROWS) // 16) * 16


def encode(code):
    fraction = (code & 127).astype(jnp.float32) * (1.0 / 128.0) + 1.0
    for bit in range(7):
        up = ((code >> (7 + bit)) & 1) == 1
        fraction = jnp.where(up, fraction * 2.0 ** (1 << bit), fraction)
        if bit == 5:
            fraction = fraction * 2.0**-64
    return jnp.where(((code >> 14) & 1) == 1, -fraction, fraction)


def decode_number(value):
    size = jnp.abs(value)
    code = jnp.where(value < 0.0, 1 << 14, 0)
    for bit in range(6, -1, -1):
        step = 1 << bit
        up = size >= 2.0 ** (step - 64)
        code = code + jnp.where(up, step << 7, 0)
        size = jnp.where(up, size * 2.0**-step, size)
    return code + ((size * 2.0**64 - 1.0) * 128.0).astype(jnp.int32)


def attend_kernel(
    lengths_any,
    slots_any,
    q_any,
    nk_any,
    nv_any,
    k_any,
    v_any,
    codes_any,
    out_ref,
    q_ref,
    nk_ref,
    nv_ref,
    k_ref,
    v_ref,
    codes_ref,
    msg,
    by_head,
    spread,
    lengths,
    slots,
    sems,
    *,
    tiles,
    per,
    feature_rows,
):
    rows, width = q_ref.shape
    small = [
        pltpu.make_async_copy(source, target, sems.at[at])
        for at, (source, target) in enumerate(
            (
                (q_any, q_ref),
                (nk_any, nk_ref),
                (nv_any, nv_ref),
                (codes_any, codes_ref),
                (lengths_any, lengths),
                (slots_any, slots),
            )
        )
    ]
    cached = k_any.shape[1]
    keys, values = (
        [
            pltpu.make_async_copy(
                source.at[r], target.at[pl.ds(r * cached, cached)], sems.at[base + r]
            )
            for r in range(rows)
        ]
        for source, target, base in ((k_any, k_ref, 6), (v_any, v_ref, 6 + rows))
    )
    for copy in small + keys + values:
        copy.start()

    heads = width // HEAD_DIM
    factor = 1.0 / math.sqrt(HEAD_DIM)
    msg[...] = jnp.zeros_like(msg)
    for copy in small:
        copy.wait()

    queries = q_ref[...].astype(jnp.float32)
    by_head[...] = jnp.zeros_like(by_head)
    for r in range(rows):
        for head in range(heads):
            by_head[r * heads + head : r * heads + head + 1, :] = queries[
                r : r + 1, head * LANES : (head + 1) * LANES
            ]
    turned = by_head[...].T
    column = lax.broadcasted_iota(jnp.int32, (1, LANES), 1)
    for head in range(heads):
        spread[head * LANES : (head + 1) * LANES, :] = jnp.where(
            column % heads == head, turned, 0.0
        ).astype(jnp.bfloat16)
    padding = jnp.zeros((16 - rows, width), jnp.float32)
    known = rows * cached
    k_ref[known:, :] = jnp.concatenate([nk_ref[...].astype(jnp.float32), padding], 0).astype(
        jnp.bfloat16
    )
    v_ref[known:, :] = jnp.concatenate([nv_ref[...].astype(jnp.float32), padding], 0).astype(
        jnp.bfloat16
    )
    for copy in keys:
        copy.wait()
    products = jnp.dot(k_ref[...], spread[...], preferred_element_type=jnp.float32) * factor
    words = codes_ref[...]
    blocks = words.shape[1] // LANES
    pieces = [encode(words & 32767), encode(words >> 15)]
    for slot in range(tiles // IMG_SPLIT):
        gains = [
            jnp.where(slots[r] == slot, 1.0, 0.0).astype(jnp.float32) for r in range(rows)
        ]
        for at, piece in enumerate(pieces):
            total = piece[0:1] * gains[0]
            for r in range(1, rows):
                total = total + piece[r : r + 1] * gains[r]
            for tile in range(tiles):
                number = (member(tile, tiles) + IMG_SPLIT // 2) % tiles
                if number // IMG_SPLIT != slot:
                    continue
                for step in range(WINDOW):
                    block = window_start(number % IMG_SPLIT) + step
                    if block < 0 or block >= blocks:
                        continue
                    place = feature_rows + at * WINDOW + step
                    msg[tile, place : place + 1, :] = total[:, block * LANES : (block + 1) * LANES]

    own_scores = products[known:]
    scores = products[:known]
    owner = column // heads
    own_at = lax.broadcasted_iota(jnp.int32, own_scores.shape, 0) == owner
    own_score = jnp.sum(jnp.where(own_at, own_scores, 0.0), 0, keepdims=True)
    limit = jnp.zeros(column.shape, jnp.int32)
    for r in range(rows):
        limit = jnp.where(owner == r, lengths[r], limit)
    position = lax.broadcasted_iota(jnp.int32, scores.shape, 0) - owner * cached
    live = (position >= 0) & (position < limit)
    scores = jnp.where(live, scores, jnp.float32(-1e30))
    highest = jnp.maximum(jnp.max(scores, 0, keepdims=True), own_score)
    cache_exp = jnp.where(live, jnp.exp(scores - highest), 0.0)
    own_exp = jnp.exp(own_score - highest)
    denom = jnp.sum(cache_exp, 0, keepdims=True) + own_exp
    cache_weight = (cache_exp / denom).T[: rows * heads]
    own_weight = jnp.where(own_at, own_exp / denom, 0.0)
    own_weight = jnp.concatenate(
        [own_weight, jnp.zeros((LANES - own_weight.shape[0], LANES), jnp.float32)], 0
    ).T[: rows * heads, :16]
    weight = jnp.concatenate([cache_weight, own_weight], 1).astype(jnp.bfloat16)
    for copy in values:
        copy.wait()
    attended = jnp.dot(weight, v_ref[...], preferred_element_type=jnp.float32)
    for tile in range(tiles):
        for r in range(rows):
            for step in range(per):
                head = member(tile, tiles) // 2 * per + step
                place = r * per + step
                msg[tile, place : place + 1, :] = attended[
                    r * heads + head : r * heads + head + 1, head * LANES : (head + 1) * LANES
                ]
    out_ref[...] = msg[...].astype(jnp.bfloat16)


def project_kernel(in_ref, own_ref, other_ref, out_any, held, total, out_ref, sems, *, rows, per):
    tiles, depth = in_ref.shape[:2]
    held[...] = in_ref[...].astype(jnp.float32).reshape(held.shape)
    groups = total.shape[0]
    lines = out_any.shape[2] // rows
    share = own_ref.shape[0]
    lhs = []
    for row in range(rows):
        parts = [held[pl.ds(row * per + j, tiles, stride=depth), :] for j in range(per)]
        lhs.append(jnp.concatenate(parts, 1))
    lhs = jnp.concatenate(lhs, 0)
    even = lax.axis_index("rows") % 2 == 0
    first, second = lhs[:, :share], lhs[:, share:]
    own = jnp.where(even, first, second).astype(jnp.bfloat16)
    other = jnp.where(even, second, first).astype(jnp.bfloat16)
    reach = lines * LANES
    copies = []
    for group in range(groups):
        columns = slice(group * reach, (group + 1) * reach)
        product = jnp.dot(own, own_ref[:, columns], preferred_element_type=jnp.float32) + jnp.dot(
            other, other_ref[:, columns], preferred_element_type=jnp.float32
        )
        for row in range(rows):
            for line in range(lines):
                total[group, pl.ds(row * lines + line, tiles, stride=rows * lines), :] = product[
                    row * tiles : (row + 1) * tiles, line * LANES : (line + 1) * LANES
                ]
        out_ref[group] = total[group].astype(jnp.bfloat16).reshape(tiles, rows * lines, LANES)
        copies.append(pltpu.make_async_copy(out_ref.at[group], out_any.at[:, group], sems.at[group]))
        copies[-1].start()
    for copy in copies:
        copy.wait()


def total_kernel(in_ref, out_ref, held, *, rows):
    tiles, groups, depth, _ = in_ref.shape
    lines = depth // rows
    parts = in_ref[...].astype(jnp.float32).reshape(tiles // 2, 2 * groups, depth, LANES)
    held[...] = jnp.sum(parts, 0)
    for group in range(2 * groups):
        for line in range(lines):
            begin = (group * lines + line) * LANES
            out_ref[:, begin : begin + LANES] = held[
                group, pl.ds(line, rows, stride=lines), :
            ].astype(jnp.bfloat16)


def split_three(whole):
    high = whole.astype(jnp.bfloat16).astype(jnp.float32)
    middle = (whole - high).astype(jnp.bfloat16).astype(jnp.float32)
    return jnp.concatenate([high, middle, whole - high - middle], 0)


def fold_kernel(
    cw_ref,
    conv_ref,
    weight_ref,
    other_ref,
    after_ref,
    out_ref,
    near_ref,
    near_other_ref,
    levels_w,
    folded,
    held,
    sems,
    near_sems,
):
    del after_ref
    taps = [(dr, dc) for dr in range(3) for dc in range(3)]
    copies = [
        pltpu.make_async_copy(conv_ref.at[dr, dc], held.at[at], sems.at[at])
        for at, (dr, dc) in enumerate(taps)
    ]
    for copy in copies:
        copy.start()
    begin = pl.multiple_of(lax.axis_index("rows") % 2 * near_ref.shape[1], LANES)
    columns = pl.ds(begin, near_ref.shape[1])
    brings = [
        pltpu.make_async_copy(source.at[:, columns], target, near_sems.at[at])
        for at, (source, target) in enumerate(((weight_ref, near_ref), (other_ref, near_other_ref)))
    ]
    for bring in brings:
        bring.start()
    levels_w[...] = jnp.zeros_like(levels_w)
    levels_w[0:FSQ_DIMS, :] = cw_ref[...]
    left = split_three(levels_w[...]).astype(jnp.bfloat16)
    folded[...] = jnp.zeros_like(folded)
    for at, copy in enumerate(copies):
        copy.wait()
        parts = jnp.dot(left, held[at], preferred_element_type=jnp.float32)
        total = parts[0:8] + parts[8:16] + parts[16:24]
        folded[at * TAP_ROWS : (at + 1) * TAP_ROWS, :] = split_three(total)
    out_ref[...] = folded[...].astype(jnp.bfloat16)
    for bring in brings:
        bring.wait()


def decode_kernel(
    in_ref, fold_ref, two_any, after_ref, out_ref, two_ref, sems, *, feature_rows
):
    del after_ref
    copies = [
        pltpu.make_async_copy(two_any.at[dr, dc], two_ref.at[at], sems.at[at])
        for at, (dr, dc) in enumerate(TAPS)
    ]
    for copy in copies[:EARLY]:
        copy.start()
    tiles = lax.axis_size("rows")
    section = (lax.axis_index("rows") + IMG_SPLIT // 2) % tiles % IMG_SPLIT
    got = jnp.sum(in_ref[...].astype(jnp.float32), 0)
    pieces = []
    for at in range(PIECES):
        lines = [
            got[feature_rows + at * WINDOW + step : feature_rows + at * WINDOW + step + 1]
            for step in range(WINDOW)
        ]
        pieces.append(jnp.concatenate(lines, 1))
    codes = decode_number(jnp.concatenate(pieces, 1))
    span = codes.shape[1]
    depth = fold_ref.shape[0]
    level = lax.broadcasted_iota(jnp.int32, (8, span), 0)
    taken = level < FSQ_DIMS
    shift = jnp.where(taken, level * 3, 0)
    value = (2 * ((jnp.broadcast_to(codes, (8, span)) >> shift) & 7) - 7).astype(
        jnp.float32
    ) * 0.125
    value = jnp.where(taken, value, 0.0)
    value = jnp.concatenate([value] * (depth // 8), 0).astype(jnp.bfloat16)

    count = TILE_ROWS * IMG_W
    begin = TILE_H * ROW_WORDS * section - HALO * ROW_WORDS
    offset = begin & (LANES - 1)
    spot = lax.broadcasted_iota(jnp.int32, (count, 1), 0)
    line = spot // IMG_W + TILE_H * section - HALO
    inside = (line >= 0) & (line < IMG_SPLIT * TILE_H)
    target = jnp.where(inside, (spot >> 1) + offset + (span // 2) * (spot & 1), -1)
    chooser = jnp.where(
        lax.broadcasted_iota(jnp.int32, (count, span), 1) == target, 1.0, 0.0
    ).astype(jnp.bfloat16)
    placed = lax.dot_general(
        chooser, value, (((1,), (1,)), ((), ())), preferred_element_type=jnp.float32
    )
    for copy in copies[EARLY:]:
        copy.start()
    column = spot % IMG_W
    moved = [
        jnp.where(column == 0, 0.0, pltpu.roll(placed, 1, 0)),
        placed,
        jnp.where(column == IMG_W - 1, 0.0, pltpu.roll(placed, count - 1, 0)),
    ]
    count = count - 2 * IMG_W
    tap_of = lax.broadcasted_iota(jnp.int32, (1, depth), 1) // TAP_ROWS
    taps = jnp.zeros((count, depth), jnp.float32)
    for dr in range(3):
        for dc in range(3):
            taps = jnp.where(
                tap_of == 3 * dr + dc, moved[dc][dr * IMG_W : dr * IMG_W + count], taps
            )
    hidden = jnp.dot(taps.astype(jnp.bfloat16), fold_ref[...], preferred_element_type=jnp.float32)

    line = lax.broadcasted_iota(jnp.int32, (count, 1), 0) // IMG_W + TILE_H * section - 1
    inside = (line >= 0) & (line < IMG_SPLIT * TILE_H)
    activated = jnp.where(inside, hidden * jax.nn.sigmoid(hidden), 0.0).astype(jnp.bfloat16)

    count = count - 2 * IMG_W
    column = lax.broadcasted_iota(jnp.int32, (count, 1), 0) % IMG_W
    summed = part = None
    for at, (dr, dc) in enumerate(TAPS):
        if at == 0:
            for copy in copies[:EARLY]:
                copy.wait()
        if at == EARLY:
            for copy in copies[EARLY:]:
                copy.wait()
        term = jnp.dot(
            activated[dr * IMG_W : dr * IMG_W + count],
            two_ref[at],
            preferred_element_type=jnp.float32,
        )
        part = term if part is None else part + term
        if dr < 2:
            continue
        if dc == 0:
            part = jnp.where(column == 0, 0.0, pltpu.roll(part, 1, 0))
        if dc == 2:
            part = jnp.where(column == IMG_W - 1, 0.0, pltpu.roll(part, count - 1, 0))
        summed = part if summed is None else summed + part
        part = None
    out_ref[...] = summed.astype(jnp.bfloat16)


def near(array):
    return pltpu.with_memory_space_constraint(array, pltpu.VMEM)


def far(array):
    return pltpu.with_memory_space_constraint(array, pltpu.HBM)


def on_device(
    queries,
    new_keys,
    new_values,
    cache_keys,
    cache_values,
    cache_lengths,
    out_weight,
    codes,
    tile_slot,
    code_weight,
    conv_one,
    conv_two,
):
    tiles = lax.axis_size("rows")
    rows, width = queries.shape
    channels = code_weight.shape[1]
    share = width // tiles
    per = 2 * share // LANES
    feature_rows = rows * per
    depth = message_rows(feature_rows)
    half = width // 2
    lines = 8
    groups = half // (lines * LANES)
    params = pltpu.CompilerParams(vmem_limit_bytes=VMEM_LIMIT)
    vmem = pl.BlockSpec(memory_space=pltpu.VMEM)
    anywhere = pl.BlockSpec(memory_space=pl.ANY)

    outgoing = pl.pallas_call(
        functools.partial(attend_kernel, tiles=tiles, per=per, feature_rows=feature_rows),
        in_specs=[anywhere] * 8,
        out_specs=vmem,
        out_shape=jax.ShapeDtypeStruct((tiles, depth, LANES), jnp.bfloat16),
        scratch_shapes=[
            pltpu.VMEM(queries.shape, queries.dtype),
            pltpu.VMEM(new_keys.shape, new_keys.dtype),
            pltpu.VMEM(new_values.shape, new_values.dtype),
            pltpu.VMEM((rows * cache_keys.shape[1] + 16, width), cache_keys.dtype),
            pltpu.VMEM((rows * cache_values.shape[1] + 16, width), cache_values.dtype),
            pltpu.VMEM(codes.shape, codes.dtype),
            pltpu.VMEM((tiles, depth, LANES), jnp.float32),
            pltpu.VMEM((LANES, LANES), jnp.float32),
            pltpu.VMEM((width, LANES), jnp.bfloat16),
            pltpu.SMEM(cache_lengths.shape, cache_lengths.dtype),
            pltpu.SMEM(tile_slot.shape, tile_slot.dtype),
            pltpu.SemaphoreType.DMA((6 + 2 * rows,)),
        ],
        compiler_params=pltpu.CompilerParams(vmem_limit_bytes=56 * 1024 * 1024),
    )(
        far(cache_lengths),
        far(tile_slot),
        far(queries),
        far(new_keys),
        far(new_values),
        far(cache_keys),
        far(cache_values),
        far(codes),
    )
    order = [[member(at, tiles) for at in range(tiles)]]
    incoming = lax.all_to_all(
        outgoing, "rows", split_axis=0, concat_axis=0, axis_index_groups=order, tiled=True
    )
    other = lax.ppermute(out_weight, "rows", [(i, i ^ 1) for i in range(tiles)])

    folded, own, other = pl.pallas_call(
        fold_kernel,
        in_specs=[vmem] + [anywhere] * 4,
        out_specs=[vmem] * 3,
        out_shape=[
            jax.ShapeDtypeStruct((FOLD_ROWS, channels), jnp.bfloat16),
            pltpu.VMEM((share, half), out_weight.dtype),
            pltpu.VMEM((share, half), out_weight.dtype),
        ],
        scratch_shapes=[
            pltpu.VMEM((8, channels), jnp.float32),
            pltpu.VMEM((FOLD_ROWS, channels), jnp.float32),
            pltpu.VMEM((9,) + conv_one.shape[2:], conv_one.dtype),
            pltpu.SemaphoreType.DMA((9,)),
            pltpu.SemaphoreType.DMA((2,)),
        ],
        compiler_params=params,
    )(far(code_weight), far(conv_one), far(out_weight), far(other), far(outgoing))

    partials = pl.pallas_call(
        functools.partial(project_kernel, rows=rows, per=per),
        in_specs=[vmem, vmem, vmem],
        out_specs=anywhere,
        out_shape=jax.ShapeDtypeStruct((tiles, groups, rows * lines, LANES), jnp.bfloat16),
        scratch_shapes=[
            pltpu.VMEM((tiles * depth, LANES), jnp.float32),
            pltpu.VMEM((groups, tiles * rows * lines, LANES), jnp.float32),
            pltpu.VMEM((groups, tiles, rows * lines, LANES), jnp.bfloat16),
            pltpu.SemaphoreType.DMA((groups,)),
        ],
        compiler_params=params,
    )(near(incoming), near(own), near(other))
    gathered = lax.all_to_all(
        partials, "rows", split_axis=0, concat_axis=0, axis_index_groups=order, tiled=True
    )

    decoded = pl.pallas_call(
        functools.partial(decode_kernel, feature_rows=feature_rows),
        in_specs=[vmem, vmem, anywhere, anywhere],
        out_specs=vmem,
        out_shape=jax.ShapeDtypeStruct((TILE_H * IMG_W, channels), jnp.bfloat16),
        scratch_shapes=[
            pltpu.VMEM((len(TAPS),) + conv_two.shape[2:], conv_two.dtype),
            pltpu.SemaphoreType.DMA((len(TAPS),)),
        ],
        compiler_params=params,
    )(near(incoming), near(folded), far(conv_two), far(partials))

    mixed = pl.pallas_call(
        functools.partial(total_kernel, rows=rows),
        in_specs=[vmem],
        out_shape=jax.ShapeDtypeStruct((rows, width), jnp.bfloat16),
        scratch_shapes=[pltpu.VMEM((2 * groups, rows * lines, LANES), jnp.float32)],
        compiler_params=params,
    )(near(gathered))
    return (mixed, decoded.reshape(TILE_H, IMG_W, channels))


def solution(mesh):
    in_specs = (
        P(("groups", "rows"), None),
        P(("groups", "rows"), None),
        P(("groups", "rows"), None),
        P(("groups", "rows"), None, None),
        P(("groups", "rows"), None, None),
        P(("groups", "rows")),
        P("rows", None),
        P(("groups", "rows"), None),
        P(("groups", "rows")),
        P(),
        P(),
        P(),
    )
    out_specs = (P(("groups", "rows"), None), P(("groups", "rows"), None, None))
    return jax.shard_map(
        on_device, mesh=mesh, in_specs=in_specs, out_specs=out_specs, check_vma=False
    )
```
